256 devices in a mesh: col: 16 (over x, y_lo, core), row: 16 (over z, y_hi).
Axes of the slice: x: 4, y: 4 (y_hi: 2, y_lo: 2; y = y_hi * 2 + y_lo), z: 8, core: 2. Of those that a mesh axis runs over, the one named last changes fastest.
Arguments:
- features: bfloat16 [4096, 512], P('col'), may hold values from -6 to 6
- block_values: bfloat16 [16, 16, 10, 128, 128], P('col', 'row'), may hold values from -0.25 to 0.25
- entry_cols: int32 [16, 16, 10], P('col', 'row'), may hold values from 0 to 31
- row_lengths: int32 [16, 48], P('col'), may hold values from 1 to 16, 160 in all within a row
- row_owner: int32 [16, 48], P('col'), may hold values from 0 to 47, each once within a row
- weight: bfloat16 [512, 512], replicated, may hold values from -0.25 to 0.25
- cotangent: bfloat16 [98304, 512], P(('col', 'row')), may hold values from -6 to 6
Outputs:
- output: bfloat16 [98304, 512], P(('col', 'row'))
- grad_weight: float32 [512, 512], replicated
- grad_features: float32 [4096, 512], P('col')
The draws below stay inside these ranges and needn't reach their ends.
Inputs may be any that keep to these rules, and one draw needn't show every extreme that they name: Each row of row_lengths sums to 160, and some block row has exactly 16 blocks. Each row of row_owner is a permutation of the group's slots.
All inputs are finite; a program needn't handle non-finite values.
Results may differ from the reference program's by a relative error of at most 0.0061.
Values may be sent and summed in bfloat16 or wider, within the bound.
A program may use at most 128 MiB of HBM per device.

```python
import math
import jax
import jax.numpy as jnp
import numpy as np
from jax import lax

F = 512
BLOCK = 128
MAX_LEN = 16
E_DEV = 10
CB_DEV = 2
GROUP_ROWS = 48
COL_BLOCKS = 32
FEAT_NODES = 4096
SLAB = 98304
N_COL = 16
N_ROW = 16


def place_ends(result, own_key, least, largest):
    longest = result.shape.index(max(result.shape))
    spots = []
    for shift in (0, 1):
        where = [jax.random.randint(jax.random.fold_in(own_key, axis), (), 0, length) for axis, length in enumerate(result.shape)]
        where[longest] = (where[longest] + shift) % result.shape[longest]
        spots.append(tuple(where))
    return result.at[spots[0]].set(least).at[spots[1]].set(largest)


def block_levels(rng, extent, split, low, top_value):
    factor_of = 1.0
    for dim, blocks in split:
        heights = jax.random.uniform(jax.random.fold_in(jax.random.fold_in(rng, 6), dim), (blocks,), jnp.float32, low / len(split), top_value / len(split))
        factor_of = factor_of * jnp.repeat(jnp.exp(heights), extent[dim] // blocks).reshape((-1,) + (1,) * (len(extent) - 1 - dim))
    return factor_of


def profile(number_of, total, most, skew):
    weights = [(1 << 20) // math.isqrt(grade ** skew) + 1 for grade in range(2, number_of + 1)]
    spare, holding = total - most - (number_of - 1), [1] * (number_of - 1)
    while spare > 0:
        movable = [i for i in range(number_of - 1) if holding[i] < most]
        pool, left = sum([weights[i] for i in movable]), spare
        for i in movable:
            extra = min(most - holding[i], max(1, left * weights[i] // pool), spare)
            holding[i] = holding[i] + extra
            spare = spare - extra
    return np.array([most] + holding)


def uneven_parts(rng, count, total, bound, skew):
    if count == 2:
        one = jax.random.randint(rng, (), max(1, total - bound), min(bound, total - 1) + 1)
        return jnp.stack([one, total - one])
    sizes = jnp.asarray(profile(count, total, bound, skew), jnp.int32)
    pairs = (count - 1) // 2
    giver, sink = sizes[1:1 + 2 * pairs:2], sizes[2:2 + 2 * pairs:2]
    slack = jnp.minimum(giver - 1, bound - sink)
    moved = jax.random.randint(jax.random.fold_in(rng, 1), (pairs,), 0, 1 << 20) % (slack + 1)
    sizes = sizes.at[1:1 + 2 * pairs:2].set(giver - moved).at[2:2 + 2 * pairs:2].set(sink + moved)
    return sizes[jax.random.permutation(jax.random.fold_in(rng, 2), count)]


def normal_values(own_key, extent, spread, most, shards=(), kind=jnp.bfloat16):
    array = spread * jax.random.normal(own_key, extent, jnp.float32)
    if shards:
        array = array * block_levels(own_key, extent, shards, -0.22, 0.18)
    return jnp.clip(array, -most, most).astype(kind)


def setup_inputs(seed: int = 0) -> dict:
    arg_keys = jax.random.split(jax.random.key(seed), 8)
    features = normal_values(arg_keys[0], (FEAT_NODES, F), 1.0, 6.0, ((0, 16),))
    block_values = normal_values(arg_keys[1], (N_COL, N_ROW, E_DEV, BLOCK, BLOCK), (4 * BLOCK) ** -0.5, 0.25, ((0, 16), (1, 16)))
    entry_cols = place_ends(jax.random.randint(arg_keys[2], (N_COL, N_ROW, E_DEV), 0, COL_BLOCKS), jax.random.fold_in(arg_keys[2], 1), 0, COL_BLOCKS - 1).astype(jnp.int32)
    row_lengths = jax.vmap(lambda own: uneven_parts(own, GROUP_ROWS, E_DEV * N_ROW, MAX_LEN, 2))(jax.random.split(arg_keys[3], N_COL)).reshape((N_COL, GROUP_ROWS)).astype(jnp.int32)
    row_owner = jax.vmap(lambda own: jax.random.permutation(own, GROUP_ROWS))(jax.random.split(arg_keys[4], N_COL)).reshape((N_COL, GROUP_ROWS)).astype(jnp.int32)
    weight = normal_values(arg_keys[5], (F, F), F ** -0.5, 0.25)
    cotangent = normal_values(arg_keys[6], (SLAB, F), 1.0, 6.0, ((0, 256),))
    return dict(features=features, block_values=block_values, entry_cols=entry_cols, row_lengths=row_lengths, row_owner=row_owner, weight=weight, cotangent=cotangent)


def activate(value):
    return jax.nn.gelu(value, approximate=True)

def reference(features, block_values, entry_cols, row_lengths, row_owner, weight, cotangent):
    col_blocks = features.reshape(CB_DEV * N_COL, BLOCK, F)
    cot_groups = cotangent.reshape(N_COL, GROUP_ROWS * BLOCK, F)

    def group(carry, inputs):
        grad_feat, grad_w = carry
        values, columns, lengths, owners, cot_group = inputs
        values = values.reshape(N_ROW * E_DEV, BLOCK, BLOCK).astype(jnp.float32)
        columns = columns.reshape(N_ROW * E_DEV).astype(jnp.int32)
        ends = jnp.cumsum(lengths).astype(jnp.int32)
        position = jnp.arange(N_ROW * E_DEV, dtype=jnp.int32)
        rowid = lax.optimization_barrier(jnp.sum((ends[None, :] <= position[:, None]).astype(jnp.int32), axis=1))
        slots = owners[rowid].astype(jnp.int32)
        picked = col_blocks[columns].astype(jnp.float32)
        tiles = jnp.einsum('ebk,ekf->ebf', values, picked, precision=lax.Precision.HIGHEST)
        summed = jax.ops.segment_sum(tiles, slots, num_segments=GROUP_ROWS)
        hidden = summed.reshape(GROUP_ROWS * BLOCK, F).astype(jnp.bfloat16)
        pre = jnp.dot(hidden, weight, preferred_element_type=jnp.float32)
        act, back = jax.vjp(activate, pre)
        grad_pre = back(cot_group.astype(jnp.float32))[0].astype(jnp.bfloat16)
        grad_w = grad_w + jnp.dot(hidden.T, grad_pre, preferred_element_type=jnp.float32)
        grad_hidden = jnp.dot(grad_pre, weight.T, preferred_element_type=jnp.float32).astype(jnp.bfloat16)
        picked_grad = grad_hidden.reshape(GROUP_ROWS, BLOCK, F)[slots].astype(jnp.float32)
        back_tiles = jnp.einsum('ebk,ebf->ekf', values, picked_grad, precision=lax.Precision.HIGHEST)
        grad_feat = grad_feat + jax.ops.segment_sum(back_tiles, columns, num_segments=CB_DEV * N_COL)
        return ((grad_feat, grad_w), act.astype(jnp.bfloat16))
    start = (jnp.zeros((CB_DEV * N_COL, BLOCK, F), jnp.float32), jnp.zeros((F, F), jnp.float32))
    (grad_feat, grad_w), outputs = lax.scan(group, start, (block_values, entry_cols, row_lengths, row_owner, cot_groups))
    output = outputs.reshape(SLAB, F)
    grad_weight = grad_w * (1.0 / math.sqrt(SLAB))
    return (output, grad_weight, grad_feat.reshape(FEAT_NODES, F))
```

```python
import functools
import math

import jax
import jax.numpy as jnp
from jax import lax
from jax.experimental import pallas as pl
from jax.experimental.pallas import tpu as pltpu
from jax.sharding import PartitionSpec as P

F = 512
BLOCK = 128
NX, NYL, NC = 4, 2, 2
NZ, NYH = 8, 2
N_COL = NX * NYL * NC
N_ROW = NZ * NYH
E_DEV = 10
ROWS = 48
SLOTS = ROWS // N_ROW
MAX_LEN = 16
CHUNK = 256
PIECE = CHUNK // N_ROW
MESH = pl.DeviceIdType.MESH
HALF = E_DEV * BLOCK // 2
MIB = 1 << 20


def place():
    col, row = lax.axis_index("col"), lax.axis_index("row")
    core = lax.rem(col, NC)
    yl = lax.rem(col // NC, NYL)
    x = col // (NC * NYL)
    z = row // NYH
    yh = lax.rem(row, NYH)
    return col, row, x, yl, core, z, yh


def col_of(x, yl, core):
    return (lax.rem(x + NX, NX) * NYL + yl) * NC + core


def row_of(z, yh):
    return lax.rem(z + NZ, NZ) * NYH + yh


def greet(peers):
    barrier = pltpu.get_barrier_semaphore()
    for peer in peers:
        pl.semaphore_signal(barrier, inc=1, device_id=peer, device_id_type=MESH)
    pl.semaphore_wait(barrier, len(peers))


class Copies:
    def __init__(self, send, recv):
        self.send, self.recv, self.count, self.all = send, recv, 0, []

    def start(self, src, dst, peer):
        copy = pltpu.make_async_remote_copy(
            src_ref=src,
            dst_ref=dst,
            send_sem=self.send.at[self.count],
            recv_sem=self.recv.at[self.count],
            device_id=peer,
            device_id_type=MESH,
        )
        copy.start()
        self.count += 1
        self.all.append(copy)
        return copy

    def finish(self):
        for copy in self.all:
            copy.wait_send()


GATHER_COPIES = 64


def gather_kernel(a_in, f_in, c_in, g_out, f_out, c_out, c_pad, send, recv, local):
    col, row, x, yl, core, z, yh = place()
    up, down = (col, row_of(z + 1, yh)), (col, row_of(z - 1, yh))
    across = (col, row_of(z, 1 - yh))
    right, left = (col_of(x + 1, yl, core), row), (col_of(x - 1, yl, core), row)
    beside = (col_of(x, 1 - yl, core), row)
    twin = (col_of(x, yl, 1 - core), row)
    others = [(col, lax.rem(row + d, N_ROW)) for d in range(1, N_ROW)]
    greet(others + [right, left, beside, twin])
    go = Copies(send, recv)

    own = [
        pltpu.make_async_copy(a_in, g_out.at[row], local.at[0]),
        pltpu.make_async_copy(f_in, f_out.at[col], local.at[1]),
    ]
    got = {}
    cross = go.start(a_in, g_out.at[row], across)
    got[0, 0, 1] = go.start(a_in, g_out.at[row], up)
    got[0, 0, -1] = go.start(a_in, g_out.at[row], down)
    f_beside = go.start(f_in, f_out.at[col], beside)
    f_right = go.start(f_in, f_out.at[col], right)
    f_left = go.start(f_in, f_out.at[col], left)
    twins = [go.start(f_in, f_out.at[col], twin)]
    for copy in own:
        copy.start()
    c_pad[...] = jnp.zeros_like(c_pad)
    c_pad[0:1, 0:E_DEV] = c_in[...]
    own.append(pltpu.make_async_copy(c_pad, c_out.at[row], local.at[2]))
    own[-1].start()
    cols = [go.start(c_pad, c_out.at[row], peer) for peer in others]

    def pass_on(stream, t):
        y = yh if stream == 0 else 1 - yh
        for way, peer in ((1, up), (-1, down)):
            if t:
                got[stream, t - 1, way].wait_recv()
            whose = row_of(z - way * t, y)
            if t < 3:
                part = g_out.at[whose]
            else:
                part = g_out.at[whose, pl.ds(0 if way == 1 else HALF, HALF)]
            got[stream, t, way] = go.start(part, part, peer)

    def chunk(dx, y):
        return f_out.at[col_of(x + dx, y, core)]

    f_beside.wait_recv()
    part = chunk(0, 1 - yl)
    f_right2 = go.start(part, part, right)
    f_left2 = go.start(part, part, left)
    twins.append(go.start(part, part, twin))
    cross.wait_recv()
    pass_on(1, 0)
    pass_on(0, 1)
    f_right.wait_recv()
    part = chunk(-1, yl)
    far_right = go.start(part, part, right)
    twins.append(go.start(part, part, twin))
    f_left.wait_recv()
    part = chunk(1, yl)
    twins.append(go.start(part, part, twin))
    pass_on(1, 1)
    f_left2.wait_recv()
    part = chunk(1, 1 - yl)
    far_left = go.start(part, part, left)
    twins.append(go.start(part, part, twin))
    f_right2.wait_recv()
    part = chunk(-1, 1 - yl)
    twins.append(go.start(part, part, twin))
    pass_on(0, 2)
    far_right.wait_recv()
    part = chunk(2, yl)
    twins.append(go.start(part, part, twin))
    far_left.wait_recv()
    part = chunk(2, 1 - yl)
    twins.append(go.start(part, part, twin))
    pass_on(1, 2)
    pass_on(0, 3)
    pass_on(1, 3)
    for copy in cols + twins:
        copy.wait_recv()
    for stream in (0, 1):
        for way in (1, -1):
            got[stream, 3, way].wait_recv()
    for copy in own:
        copy.wait()
    go.finish()


def gather(values, features, columns):
    any_space = pl.BlockSpec(memory_space=pl.ANY)
    return pl.pallas_call(
        gather_kernel,
        name="gather",
        out_shape=(
            jax.ShapeDtypeStruct((N_ROW, E_DEV * BLOCK, BLOCK), jnp.bfloat16),
            jax.ShapeDtypeStruct((N_COL, CHUNK, F), jnp.bfloat16),
            jax.ShapeDtypeStruct((N_ROW, 8, 128), jnp.int32),
        ),
        in_specs=[any_space, any_space, pl.BlockSpec(memory_space=pltpu.VMEM)],
        out_specs=(any_space, any_space, any_space),
        scratch_shapes=[
            pltpu.VMEM((8, 128), jnp.int32),
            pltpu.SemaphoreType.DMA((GATHER_COPIES,)),
            pltpu.SemaphoreType.DMA((GATHER_COPIES,)),
            pltpu.SemaphoreType.DMA((3,)),
        ],
        compiler_params=pltpu.CompilerParams(
            collective_id=0, has_side_effects=True, vmem_limit_bytes=4 * MIB
        ),
    )(values, features, columns)


A_SCALE = math.sqrt(2.0 / math.pi)
CUBE = 0.044715


def layer_kernel(
    cols, lengths, owners, g_in, f_in, w_in, cot_in, out, gw_out, gf_out,
    dense, feats, stage, acc, hid, gpre, ghid, sems, f_sems,
):
    row = lax.axis_index("row")
    steps = f_sems.shape[0]
    per = N_COL // steps

    def f_copy(i):
        part = pl.ds(i * per, per)
        return pltpu.make_async_copy(f_in.at[part], feats.at[part], f_sems.at[i])

    def find(q, state):
        begin, starts, sizes = state
        length = lengths[0, q]
        which = owners[0, q] - row * SLOTS
        starts = tuple(jnp.where(which == s, begin, v) for s, v in enumerate(starts))
        sizes = tuple(jnp.where(which == s, length, v) for s, v in enumerate(sizes))
        return begin + length, starts, sizes

    nought = jnp.int32(0)
    _, starts, sizes = lax.fori_loop(0, ROWS, find, (nought, (nought,) * SLOTS, (nought,) * SLOTS))

    def a_copy(s, k):
        i = s * MAX_LEN + k
        return pltpu.make_async_copy(g_in.at[starts[s] + k], stage.at[i], sems.at[i])

    for s in range(SLOTS):

        @pl.loop(0, sizes[s])
        def _(k):
            a_copy(s, k).start()

    for i in range(steps):
        f_copy(i).start()
    dense[...] = jnp.zeros_like(dense)
    for s in range(SLOTS):

        @pl.loop(0, sizes[s])
        def _(k):
            a_copy(s, k).wait()
            g = starts[s] + k
            j = cols[g // E_DEV, 0, lax.rem(g, E_DEV)]
            spot = (pl.ds(s * BLOCK, BLOCK), pl.ds(pl.multiple_of(j * BLOCK, BLOCK), BLOCK))
            dense[spot] = dense[spot] + stage[s * MAX_LEN + k]

    acc[...] = jnp.zeros_like(acc)

    @pl.loop(0, steps)
    def _(i):
        f_copy(i).wait()
        wide = per * CHUNK
        part = feats[pl.ds(i * per, per)].reshape(wide, F)
        left = dense[:, pl.ds(pl.multiple_of(i * wide, wide), wide)]
        acc[...] += jnp.dot(left, part, preferred_element_type=jnp.float32)

    hid[...] = acc[...].astype(jnp.bfloat16)
    acc[...] = jnp.dot(hid[...], w_in[...], preferred_element_type=jnp.float32)

    @pl.loop(0, SLOTS * BLOCK // 32)
    def _(i):
        part = pl.ds(pl.multiple_of(i * 32, 32), 32)
        v = acc[part]
        square = v * v
        t = jnp.tanh(A_SCALE * (v + CUBE * (v * square)))
        cdf = 0.5 * (1.0 + t)
        out[part] = (v * cdf).astype(jnp.bfloat16)
        slope = cdf + 0.5 * v * (1.0 - t * t) * (A_SCALE * (1.0 + 3.0 * CUBE * square))
        gpre[part] = (cot_in[part].astype(jnp.float32) * slope).astype(jnp.bfloat16)

    over_rows = (((0,), (0,)), ((), ()))
    for half in range(2):
        gw_out[half] = lax.dot_general(
            hid[:, half * CHUNK : (half + 1) * CHUNK], gpre[...], over_rows,
            preferred_element_type=jnp.float32,
        ).astype(jnp.bfloat16)
    ghid[...] = lax.dot_general(
        gpre[...], w_in[...], (((1,), (1,)), ((), ())), preferred_element_type=jnp.float32
    ).astype(jnp.bfloat16)

    @pl.loop(0, N_COL)
    def _(c):
        left = dense[:, pl.ds(pl.multiple_of(c * CHUNK, CHUNK), CHUNK)]
        gf_out[lax.rem(c, NC), c // NC] = lax.dot_general(
            left, ghid[...], over_rows, preferred_element_type=jnp.float32
        ).astype(jnp.bfloat16)


def layer(cols, lengths, owners, blocks, feats, weight, cotangent):
    smem = pl.BlockSpec(memory_space=pltpu.SMEM)
    vmem = pl.BlockSpec(memory_space=pltpu.VMEM)
    any_space = pl.BlockSpec(memory_space=pl.ANY)
    rows = SLOTS * BLOCK
    return pl.pallas_call(
        layer_kernel,
        name="layer",
        out_shape=(
            jax.ShapeDtypeStruct((rows, F), jnp.bfloat16),
            jax.ShapeDtypeStruct((NC, CHUNK, F), jnp.bfloat16),
            jax.ShapeDtypeStruct((NC, N_COL // NC, CHUNK, F), jnp.bfloat16),
        ),
        in_specs=[smem, smem, smem, any_space, any_space, vmem, vmem],
        out_specs=(vmem, vmem, vmem),
        scratch_shapes=[
            pltpu.VMEM((rows, N_COL * CHUNK), jnp.bfloat16),
            pltpu.VMEM((N_COL, CHUNK, F), jnp.bfloat16),
            pltpu.VMEM((SLOTS * MAX_LEN, BLOCK, BLOCK), jnp.bfloat16),
            pltpu.VMEM((rows, F), jnp.float32),
            pltpu.VMEM((rows, F), jnp.bfloat16),
            pltpu.VMEM((rows, F), jnp.bfloat16),
            pltpu.VMEM((rows, F), jnp.bfloat16),
            pltpu.SemaphoreType.DMA((SLOTS * MAX_LEN,)),
            pltpu.SemaphoreType.DMA((4,)),
        ],
        compiler_params=pltpu.CompilerParams(vmem_limit_bytes=32 * MIB),
    )(cols, lengths, owners, blocks, feats, weight, cotangent)


REDUCE_COPIES = 96


def f32(value):
    return value.astype(jnp.float32)


def reduce_kernel(
    gw_in, gf_in, gw_out, gf_out,
    r0, s0, relay, from_left, from_right, mine, theirs, whole, pieces, final,
    w_r0, w_s0, w_pieces, w_cols, w_final, w_other, send, recv,
):
    col, row, x, yl, core, z, yh = place()
    right, left = (col_of(x + 1, yl, core), row), (col_of(x - 1, yl, core), row)
    beside = (col_of(x, 1 - yl, core), row)
    twin = (col_of(x, yl, 1 - core), row)
    others = [(col, lax.rem(row + d, N_ROW)) for d in range(1, N_ROW)]
    plane = N_COL // NC
    here = col // NC
    plane_peers = [(lax.rem(here + d, plane) * NC + core, row) for d in range(1, plane)]
    greet(others + plane_peers + [twin])
    go = Copies(send, recv)
    half = NC * CHUNK // 2

    w_twin = go.start(gw_in.at[1 - core], w_r0, twin)
    order = [(dx, y) for dx in (2, 1, -1, 0) for y in (1 - yl, yl)]
    spots = [lax.rem(x + dx + NX, NX) * NYL + y for dx, y in order]
    twins = [go.start(gf_in.at[1 - core, spot], r0.at[o], twin) for o, spot in enumerate(spots)]

    def my_piece(r):
        return pl.ds(pl.multiple_of(r * PIECE, PIECE), PIECE)

    w_twin.wait_recv()
    w_s0[...] = (f32(gw_in[core]) + f32(w_r0[...])).astype(jnp.bfloat16)
    w_rows = [
        go.start(w_s0.at[my_piece(peer[1])], w_pieces.at[d], peer) for d, peer in enumerate(others)
    ]

    def add_twin(o):
        twins[o].wait_recv()
        s0[o] = (f32(gf_in[core, spots[o]]) + f32(r0[o])).astype(jnp.bfloat16)

    add_twin(0)
    far_right = go.start(s0.at[0], relay.at[0], right)
    add_twin(1)
    far_left = go.start(s0.at[1], relay.at[1], left)
    add_twin(3)
    near_right = [None, go.start(s0.at[3], from_left.at[1], right)]
    add_twin(4)
    near_left = [go.start(s0.at[4], from_right.at[0], left), None]
    add_twin(2)
    add_twin(5)
    far_right.wait_recv()
    s0[2] = (f32(s0[2]) + f32(relay[0])).astype(jnp.bfloat16)
    near_right[0] = go.start(s0.at[2], from_left.at[0], right)
    far_left.wait_recv()
    s0[5] = (f32(s0[5]) + f32(relay[1])).astype(jnp.bfloat16)
    near_left[1] = go.start(s0.at[5], from_right.at[1], left)
    add_twin(6)
    add_twin(7)

    for copy in w_rows:
        copy.wait_recv()
    total = f32(w_s0[my_piece(row)])
    for d in range(N_ROW - 1):
        total = total + f32(w_pieces[d])
    w_cols[here] = total.astype(jnp.bfloat16)
    w_plane = [go.start(w_cols.at[here], w_cols.at[here], peer) for peer in plane_peers]

    near_right[0].wait_recv()
    near_left[0].wait_recv()
    mine[0] = (f32(s0[6]) + f32(from_left[0]) + f32(from_right[0])).astype(jnp.bfloat16)
    to_beside = go.start(mine.at[0], theirs, beside)

    for copy in w_plane:
        copy.wait_recv()
    total = f32(w_cols[0])
    for p in range(1, plane):
        total = total + f32(w_cols[p])
    scale = 1.0 / math.sqrt(N_COL * N_ROW * SLOTS * BLOCK)
    w_final[my_piece(row)] = (total * scale).astype(jnp.bfloat16)
    part = w_final.at[my_piece(row)]
    w_all = [go.start(part, part, peer) for peer in others]

    near_right[1].wait_recv()
    near_left[1].wait_recv()
    to_beside.wait_recv()
    whole[...] = (
        f32(s0[7]) + f32(from_left[1]) + f32(from_right[1]) + f32(theirs[...])
    ).astype(jnp.bfloat16)
    rows = [go.start(whole.at[my_piece(peer[1])], pieces.at[d], peer) for d, peer in enumerate(others)]

    for copy in w_all:
        copy.wait_recv()
    w_back = go.start(w_final, w_other, twin)

    for copy in rows:
        copy.wait_recv()
    total = f32(whole[my_piece(row)])
    for d in range(N_ROW - 1):
        total = total + f32(pieces[d])
    final[my_piece(row)] = total.astype(jnp.bfloat16)
    part = final.at[my_piece(row)]
    everyone = [go.start(part, part, peer) for peer in others]

    gw_out[pl.ds(pl.multiple_of(core * half, half), half)] = f32(w_final[...])
    w_back.wait_recv()
    gw_out[pl.ds(pl.multiple_of((1 - core) * half, half), half)] = f32(w_other[...])
    for copy in everyone:
        copy.wait_recv()
    gf_out[...] = f32(final[...])
    go.finish()


def reduce(gw_part, gf_part):
    vmem = pl.BlockSpec(memory_space=pltpu.VMEM)
    block = (CHUNK, F)

    def buffer(*lead):
        return pltpu.VMEM(lead + block, jnp.bfloat16)

    def small(n):
        return pltpu.VMEM((n, PIECE, F), jnp.bfloat16)

    return pl.pallas_call(
        reduce_kernel,
        name="reduce",
        out_shape=(
            jax.ShapeDtypeStruct((F, F), jnp.float32),
            jax.ShapeDtypeStruct(block, jnp.float32),
        ),
        in_specs=[vmem, vmem],
        out_specs=(vmem, vmem),
        scratch_shapes=[
            buffer(8), buffer(8), buffer(2), buffer(2), buffer(2), buffer(1), buffer(), buffer(),
            small(N_ROW), buffer(),
            buffer(), buffer(), small(N_ROW), small(N_COL // NC), buffer(), buffer(),
            pltpu.SemaphoreType.DMA((REDUCE_COPIES,)),
            pltpu.SemaphoreType.DMA((REDUCE_COPIES,)),
        ],
        compiler_params=pltpu.CompilerParams(
            collective_id=1, has_side_effects=True, vmem_limit_bytes=32 * MIB
        ),
    )(gw_part, gf_part)


def body(features, block_values, entry_cols, row_lengths, row_owner, weight, cotangent):
    values = block_values.reshape(E_DEV * BLOCK, BLOCK)
    blocks, feats, cols = gather(values, features, entry_cols.reshape(1, E_DEV))
    blocks = blocks.reshape(N_ROW * E_DEV, BLOCK, BLOCK)
    output, gw_part, gf_part = layer(
        cols, row_lengths, row_owner, blocks, feats, weight, cotangent
    )
    grad_weight, grad_features = reduce(gw_part, gf_part)
    return (output, grad_weight, grad_features)


def solution(mesh):
    placed = (
        P("col", None),
        P("col", "row", None, None, None),
        P("col", "row", None),
        P("col", None),
        P("col", None),
        P(),
        P(("col", "row"), None),
    )
    return jax.shard_map(
        body,
        mesh=mesh,
        in_specs=placed,
        out_specs=(P(("col", "row"), None), P(), P("col", None)),
        check_vma=False,
    )
```

```python
import functools
import math

import jax
import jax.numpy as jnp
from jax import lax
from jax.experimental import pallas as pl
from jax.experimental.pallas import tpu as pltpu
from jax.sharding import PartitionSpec as P

F = 512
BLOCK = 128
NX, NYL, NC = 4, 2, 2
NZ, NYH = 8, 2
N_COL = NX * NYL * NC
N_ROW = NZ * NYH
E_DEV = 10
ROWS = 48
SLOTS = ROWS // N_ROW
MAX_LEN = 16
CHUNK = 256
PIECE = CHUNK // N_ROW
MESH = pl.DeviceIdType.MESH
HALF = E_DEV * BLOCK // 2
OVER = 6 * BLOCK
PARTS = 2
WIDE = F // PARTS
MIB = 1 << 20


def place():
    col, row = lax.axis_index("col"), lax.axis_index("row")
    core = lax.rem(col, NC)
    yl = lax.rem(col // NC, NYL)
    x = col // (NC * NYL)
    z = row // NYH
    yh = lax.rem(row, NYH)
    return col, row, x, yl, core, z, yh


def col_of(x, yl, core):
    return (lax.rem(x + NX, NX) * NYL + yl) * NC + core


def row_of(z, yh):
    return lax.rem(z + NZ, NZ) * NYH + yh


def greet(peers, meanwhile=None):
    barrier = pltpu.get_barrier_semaphore()
    for peer in peers:
        pl.semaphore_signal(barrier, inc=1, device_id=peer, device_id_type=MESH)
    if meanwhile is not None:
        meanwhile()
    pl.semaphore_wait(barrier, len(peers))


def in_hbm(*arrays):
    return [pltpu.with_memory_space_constraint(array, pltpu.HBM) for array in arrays]


class Copies:
    def __init__(self, send, recv):
        self.send, self.recv, self.count, self.all = send, recv, 0, []

    def start(self, src, dst, peer):
        copy = pltpu.make_async_remote_copy(
            src_ref=src,
            dst_ref=dst,
            send_sem=self.send.at[self.count],
            recv_sem=self.recv.at[self.count],
            device_id=peer,
            device_id_type=MESH,
        )
        copy.start()
        self.count += 1
        self.all.append(copy)
        return copy

    def finish(self):
        for copy in self.all:
            copy.wait_send()


GATHER_COPIES = 64


def gather_kernel(
    a_in, f_in, c_in, g_out, f_out, c_out, c_raw, c_pad, send, recv, local
):
    col, row, x, yl, core, z, yh = place()
    up, down = (col, row_of(z + 1, yh)), (col, row_of(z - 1, yh))
    across = (col, row_of(z, 1 - yh))
    right, left = (col_of(x + 1, yl, core), row), (col_of(x - 1, yl, core), row)
    beside = (col_of(x, 1 - yl, core), row)
    twin = (col_of(x, yl, 1 - core), row)
    others = [(col, lax.rem(row + d, N_ROW)) for d in range(1, N_ROW)]

    own = [
        pltpu.make_async_copy(a_in, g_out.at[row], local.at[0]),
        pltpu.make_async_copy(f_in, f_out.at[col], local.at[1]),
    ]

    def columns():
        load = pltpu.make_async_copy(c_in, c_raw, local.at[2])
        load.start()
        for copy in own:
            copy.start()
        load.wait()
        c_pad[...] = jnp.zeros_like(c_pad)
        c_pad[:, 0:E_DEV] = c_raw[...]

    greet(others + [right, left, beside, twin], columns)
    go = Copies(send, recv)

    low, high = pl.ds(0, OVER), pl.ds(OVER, E_DEV * BLOCK - OVER)
    got = {}
    got[0, 0, 1] = go.start(a_in, g_out.at[row], up)
    got[0, 0, -1] = go.start(a_in, g_out.at[row], down)
    cross = go.start(a_in.at[high], g_out.at[row, high], across)
    over = [go.start(a_in.at[low], g_out.at[row, low], across)]
    f_beside = go.start(f_in, f_out.at[col], beside)
    f_right = go.start(f_in, f_out.at[col], right)
    f_left = go.start(f_in, f_out.at[col], left)
    twins = [go.start(f_in, f_out.at[col], twin)]
    own.append(pltpu.make_async_copy(c_pad, c_out.at[row], local.at[3]))
    own[-1].start()
    cols = [go.start(c_pad, c_out.at[row], peer) for peer in others]

    def rows_of(stream, t, way):
        if t < 3:
            return pl.ds(0, E_DEV * BLOCK) if stream == 0 else high
        if stream == 0:
            return pl.ds(0 if way == 1 else HALF, HALF)
        size = (E_DEV * BLOCK - OVER) // 2
        return pl.ds(OVER if way == 1 else OVER + size, size)

    def arrived(t, way):
        got[0, t, way].wait_recv()
        whose = row_of(z - way * (t + 1), yh)
        if t < 3:
            rows = low
        else:
            rows = pl.ds(0, HALF) if way == 1 else pl.ds(HALF, OVER - HALF)
        part = g_out.at[whose, rows]
        over.append(go.start(part, part, across))

    def pass_on(stream, t):
        y = yh if stream == 0 else 1 - yh
        for way, peer in ((1, up), (-1, down)):
            if t and stream == 1:
                got[stream, t - 1, way].wait_recv()
            elif t:
                arrived(t - 1, way)
            part = g_out.at[row_of(z - way * t, y), rows_of(stream, t, way)]
            got[stream, t, way] = go.start(part, part, peer)

    def chunk(dx, y):
        return f_out.at[col_of(x + dx, y, core)]

    f_beside.wait_recv()
    part = chunk(0, 1 - yl)
    f_right2 = go.start(part, part, right)
    f_left2 = go.start(part, part, left)
    twins.append(go.start(part, part, twin))
    cross.wait_recv()
    pass_on(1, 0)
    pass_on(0, 1)
    f_right.wait_recv()
    part = chunk(-1, yl)
    far_right = go.start(part, part, right)
    twins.append(go.start(part, part, twin))
    f_left.wait_recv()
    part = chunk(1, yl)
    twins.append(go.start(part, part, twin))
    pass_on(1, 1)
    f_left2.wait_recv()
    part = chunk(1, 1 - yl)
    far_left = go.start(part, part, left)
    twins.append(go.start(part, part, twin))
    f_right2.wait_recv()
    part = chunk(-1, 1 - yl)
    twins.append(go.start(part, part, twin))
    pass_on(0, 2)
    pass_on(1, 2)
    far_right.wait_recv()
    part = chunk(2, yl)
    twins.append(go.start(part, part, twin))
    far_left.wait_recv()
    part = chunk(2, 1 - yl)
    twins.append(go.start(part, part, twin))
    pass_on(0, 3)
    pass_on(1, 3)
    for copy in cols + twins:
        copy.wait_recv()
    for way in (1, -1):
        arrived(3, way)
    for way in (1, -1):
        got[1, 3, way].wait_recv()
    for copy in over:
        copy.wait_recv()
    for copy in own:
        copy.wait()
    go.finish()


def gather(values, features, columns):
    any_space = pl.BlockSpec(memory_space=pl.ANY)
    hbm = pl.BlockSpec(memory_space=pltpu.HBM)
    return pl.pallas_call(
        gather_kernel,
        name="gather",
        out_shape=(
            jax.ShapeDtypeStruct((N_ROW, E_DEV * BLOCK, BLOCK), jnp.bfloat16),
            jax.ShapeDtypeStruct((N_COL, CHUNK, F), jnp.bfloat16),
            jax.ShapeDtypeStruct((N_ROW, 1, 128), jnp.int32),
        ),
        in_specs=[hbm, hbm, hbm],
        out_specs=(any_space, any_space, any_space),
        scratch_shapes=[
            pltpu.VMEM((1, E_DEV), jnp.int32),
            pltpu.VMEM((1, 128), jnp.int32),
            pltpu.SemaphoreType.DMA((GATHER_COPIES,)),
            pltpu.SemaphoreType.DMA((GATHER_COPIES,)),
            pltpu.SemaphoreType.DMA((4,)),
        ],
        compiler_params=pltpu.CompilerParams(
            collective_id=0, has_side_effects=True, vmem_limit_bytes=4 * MIB
        ),
    )(*in_hbm(values, features, columns))


A_SCALE = math.sqrt(2.0 / math.pi)
CUBE = 0.044715


def layer_kernel(
    cols, len_in, own_in, blocks, feats, w_in, cot_in, out, dense, hid, gpre, ghid,
    lengths, owners, weight, cot, acc, sems,
):
    row = lax.axis_index("row")
    small = [
        pltpu.make_async_copy(len_in, lengths, sems.at[0]),
        pltpu.make_async_copy(own_in, owners, sems.at[1]),
    ]
    get_weight = pltpu.make_async_copy(w_in, weight, sems.at[2])
    get_cot = pltpu.make_async_copy(cot_in, cot, sems.at[3])
    for copy in small + [get_weight, get_cot]:
        copy.start()
    dense[...] = jnp.zeros_like(dense)
    for copy in small:
        copy.wait()

    def find(q, state):
        begin, starts, sizes = state
        length = lengths[0, q]
        which = owners[0, q] - row * SLOTS
        starts = tuple(jnp.where(which == s, begin, v) for s, v in enumerate(starts))
        sizes = tuple(jnp.where(which == s, length, v) for s, v in enumerate(sizes))
        return begin + length, starts, sizes

    nought = jnp.int32(0)
    _, starts, sizes = lax.fori_loop(0, ROWS, find, (nought, (nought,) * SLOTS, (nought,) * SLOTS))
    for s in range(SLOTS):

        @pl.loop(0, sizes[s])
        def _(k):
            g = starts[s] + k
            j = cols[g // E_DEV, 0, lax.rem(g, E_DEV)]
            spot = (pl.ds(s * BLOCK, BLOCK), pl.ds(pl.multiple_of(j * BLOCK, BLOCK), BLOCK))
            dense[spot] = dense[spot] + blocks[g]

    wide = N_COL * CHUNK // 4
    acc[...] = jnp.zeros_like(acc)

    @pl.loop(0, 4)
    def _(i):
        part = pl.ds(pl.multiple_of(i * wide, wide), wide)
        acc[...] += jnp.dot(dense[:, part], feats[part], preferred_element_type=jnp.float32)

    hid[...] = acc[...].astype(jnp.bfloat16)
    get_weight.wait()
    acc[...] = jnp.dot(hid[...], weight[...], preferred_element_type=jnp.float32)
    get_cot.wait()

    @pl.loop(0, SLOTS * BLOCK // 32)
    def _(i):
        part = pl.ds(pl.multiple_of(i * 32, 32), 32)
        v = acc[part]
        square = v * v
        t = jnp.tanh(A_SCALE * (v + CUBE * (v * square)))
        cdf = 0.5 * (1.0 + t)
        out[part] = (v * cdf).astype(jnp.bfloat16)
        slope = cdf + 0.5 * v * (1.0 - t * t) * (A_SCALE * (1.0 + 3.0 * CUBE * square))
        gpre[part] = (cot[part].astype(jnp.float32) * slope).astype(jnp.bfloat16)

    ghid[...] = lax.dot_general(
        gpre[...], weight[...], (((1,), (1,)), ((), ())), preferred_element_type=jnp.float32
    ).astype(jnp.bfloat16)


def layer(cols, lengths, owners, blocks, feats, weight, cotangent):
    smem = pl.BlockSpec(memory_space=pltpu.SMEM)
    vmem = pl.BlockSpec(memory_space=pltpu.VMEM)
    hbm = pl.BlockSpec(memory_space=pltpu.HBM)
    rows = SLOTS * BLOCK
    part = jax.ShapeDtypeStruct((rows, F), jnp.bfloat16)
    return pl.pallas_call(
        layer_kernel,
        name="layer",
        out_shape=(
            part,
            jax.ShapeDtypeStruct((rows, N_COL * CHUNK), jnp.bfloat16),
            part,
            part,
            part,
        ),
        in_specs=[smem, hbm, hbm, vmem, vmem, hbm, hbm],
        out_specs=(vmem,) * 5,
        scratch_shapes=[
            pltpu.SMEM((1, ROWS), jnp.int32),
            pltpu.SMEM((1, ROWS), jnp.int32),
            pltpu.VMEM((F, F), jnp.bfloat16),
            pltpu.VMEM((rows, F), jnp.bfloat16),
            pltpu.VMEM((rows, F), jnp.float32),
            pltpu.SemaphoreType.DMA((4,)),
        ],
        compiler_params=pltpu.CompilerParams(vmem_limit_bytes=32 * MIB),
    )(cols, *in_hbm(lengths, owners), blocks, feats, *in_hbm(weight, cotangent))


REDUCE_COPIES = 256


def f32(value):
    return value.astype(jnp.float32)


def bf16(value):
    return value.astype(jnp.bfloat16)


OVER_ROWS = (((0,), (0,)), ((), ()))


def reduce_kernel(
    dense, hid, gpre, ghid, gw_out, gf_out,
    p0, r0, s0, relay, from_left, from_right, mine, theirs, whole, pieces, final,
    w_p0, w_r0, w_s0, w_pieces, w_cols, w_final, w_other, send, recv,
):
    col, row, x, yl, core, z, yh = place()
    right, left = (col_of(x + 1, yl, core), row), (col_of(x - 1, yl, core), row)
    beside = (col_of(x, 1 - yl, core), row)
    twin = (col_of(x, yl, 1 - core), row)
    others = [(col, lax.rem(row + d, N_ROW)) for d in range(1, N_ROW)]
    plane = N_COL // NC
    here = col // NC
    plane_peers = [(lax.rem(here + d, plane) * NC + core, row) for d in range(1, plane)]
    go = Copies(send, recv)
    parts = range(PARTS)
    order = [(dx, y) for dx in (2, 1, -1, 0) for y in (1 - yl, yl)]

    def lanes(i):
        return pl.ds(pl.multiple_of(i * CHUNK, CHUNK), CHUNK)

    def weight_term(c):
        return lax.dot_general(
            hid[:, lanes(c)], gpre[...], OVER_ROWS, preferred_element_type=jnp.float32
        )

    def feature_term(o, c):
        dx, y = order[o]
        return lax.dot_general(
            dense[:, lanes(col_of(x + dx, y, c))], ghid[...], OVER_ROWS,
            preferred_element_type=jnp.float32,
        )

    def for_twin(o):
        term = bf16(feature_term(o, 1 - core))
        for h in parts:
            p0[o, h] = term[:, h * WIDE : (h + 1) * WIDE]

    def first():
        w_p0[...] = bf16(weight_term(1 - core))
        for_twin(0)
        for_twin(1)

    greet(others + plane_peers + [twin], first)
    twins = {}
    for o in (0, 1):
        twins[o] = go.start(p0.at[o], r0.at[o], twin)
    w_twin = go.start(w_p0, w_r0, twin)
    for o in (3, 4, 2, 5, 6, 7):
        for_twin(o)
        twins[o] = go.start(p0.at[o], r0.at[o], twin)

    def my_piece(r):
        return pl.ds(pl.multiple_of(r * PIECE, PIECE), PIECE)

    def add_twin(o):
        term = feature_term(o, core)
        twins[o].wait_recv()
        for h in parts:
            s0[o, h] = bf16(term[:, h * WIDE : (h + 1) * WIDE] + f32(r0[o, h]))

    add_twin(0)
    far_right = [go.start(s0.at[0, h], relay.at[0, h], right) for h in parts]
    add_twin(1)
    far_left = [go.start(s0.at[1, h], relay.at[1, h], left) for h in parts]

    term = weight_term(core)
    w_twin.wait_recv()
    w_s0[...] = bf16(term + f32(w_r0[...]))
    w_rows = [
        go.start(w_s0.at[my_piece(peer[1])], w_pieces.at[d], peer) for d, peer in enumerate(others)
    ]

    add_twin(3)
    add_twin(4)
    near_right, near_left = {}, {}

    def send_near(h):
        near_right[1, h] = go.start(s0.at[3, h], from_left.at[1, h], right)
        near_left[0, h] = go.start(s0.at[4, h], from_right.at[0, h], left)

    def send_relayed(h):
        far_right[h].wait_recv()
        s0[2, h] = bf16(f32(s0[2, h]) + f32(relay[0, h]))
        near_right[0, h] = go.start(s0.at[2, h], from_left.at[0, h], right)
        far_left[h].wait_recv()
        s0[5, h] = bf16(f32(s0[5, h]) + f32(relay[1, h]))
        near_left[1, h] = go.start(s0.at[5, h], from_right.at[1, h], left)

    to_beside, rows, everyone = {}, {}, {}

    def send_beside(h):
        near_right[0, h].wait_recv()
        near_left[0, h].wait_recv()
        mine[h] = bf16(f32(s0[6, h]) + f32(from_left[0, h]) + f32(from_right[0, h]))
        to_beside[h] = go.start(mine.at[h], theirs.at[h], beside)

    def send_rows(h):
        near_right[1, h].wait_recv()
        near_left[1, h].wait_recv()
        near = f32(s0[7, h]) + f32(from_left[1, h]) + f32(from_right[1, h])
        to_beside[h].wait_recv()
        whole[h] = bf16(near + f32(theirs[h]))
        rows[h] = [
            go.start(whole.at[h, my_piece(peer[1])], pieces.at[h, d], peer)
            for d, peer in enumerate(others)
        ]

    def send_everyone(h):
        for copy in rows[h]:
            copy.wait_recv()
        total = f32(whole[h, my_piece(row)])
        for d in range(N_ROW - 1):
            total = total + f32(pieces[h, d])
        final[h, my_piece(row)] = bf16(total)
        part = final.at[h, my_piece(row)]
        everyone[h] = [go.start(part, part, peer) for peer in others]

    send_near(0)
    add_twin(2)
    add_twin(5)
    send_relayed(0)
    for h in range(1, PARTS):
        send_near(h)
        send_relayed(h)
    add_twin(6)
    add_twin(7)

    for copy in w_rows:
        copy.wait_recv()
    total = f32(w_s0[my_piece(row)])
    for d in range(N_ROW - 1):
        total = total + f32(w_pieces[d])
    w_cols[here] = bf16(total)
    w_plane = [go.start(w_cols.at[here], w_cols.at[here], peer) for peer in plane_peers]

    send_beside(0)
    for copy in w_plane:
        copy.wait_recv()
    total = f32(w_cols[0])
    for p in range(1, plane):
        total = total + f32(w_cols[p])
    scale = 1.0 / math.sqrt(N_COL * N_ROW * SLOTS * BLOCK)
    w_final[my_piece(row)] = bf16(total * scale)
    part = w_final.at[my_piece(row)]
    w_all = [go.start(part, part, peer) for peer in others]
    send_rows(0)
    for h in range(1, PARTS):
        send_beside(h)
        send_everyone(h - 1)
        send_rows(h)

    for copy in w_all:
        copy.wait_recv()
    w_back = go.start(w_final, w_other, twin)
    gw_out[lanes(core)] = f32(w_final[...])
    send_everyone(PARTS - 1)
    w_back.wait_recv()
    gw_out[lanes(1 - core)] = f32(w_other[...])
    for h in parts:
        for copy in everyone[h]:
            copy.wait_recv()
        gf_out[:, h * WIDE : (h + 1) * WIDE] = f32(final[h])
    go.finish()


def reduce(dense, hid, gpre, ghid):
    vmem = pl.BlockSpec(memory_space=pltpu.VMEM)

    def buffer(*lead):
        return pltpu.VMEM(lead + (PARTS, CHUNK, WIDE), jnp.bfloat16)

    def small(*lead):
        return pltpu.VMEM(lead + (PIECE, F), jnp.bfloat16)

    chunk = pltpu.VMEM((CHUNK, F), jnp.bfloat16)
    return pl.pallas_call(
        reduce_kernel,
        name="reduce",
        out_shape=(
            jax.ShapeDtypeStruct((F, F), jnp.float32),
            jax.ShapeDtypeStruct((CHUNK, F), jnp.float32),
        ),
        in_specs=[vmem] * 4,
        out_specs=(vmem, vmem),
        scratch_shapes=[
            buffer(8), buffer(8), buffer(8), buffer(2), buffer(2), buffer(2),
            buffer(), buffer(), buffer(),
            pltpu.VMEM((PARTS, N_ROW, PIECE, WIDE), jnp.bfloat16), buffer(),
            chunk, chunk, chunk, small(N_ROW), small(N_COL // NC), chunk, chunk,
            pltpu.SemaphoreType.DMA((REDUCE_COPIES,)),
            pltpu.SemaphoreType.DMA((REDUCE_COPIES,)),
        ],
        compiler_params=pltpu.CompilerParams(
            collective_id=1, has_side_effects=True, vmem_limit_bytes=32 * MIB
        ),
    )(dense, hid, gpre, ghid)


def body(features, block_values, entry_cols, row_lengths, row_owner, weight, cotangent):
    values = block_values.reshape(E_DEV * BLOCK, BLOCK)
    blocks, feats, cols = gather(values, features, entry_cols.reshape(1, E_DEV))
    blocks = blocks.reshape(N_ROW * E_DEV, BLOCK, BLOCK)
    feats = feats.reshape(N_COL * CHUNK, F)
    output, dense, hid, gpre, ghid = layer(
        cols, row_lengths, row_owner, blocks, feats, weight, cotangent
    )
    grad_weight, grad_features = reduce(dense, hid, gpre, ghid)
    return (output, grad_weight, grad_features)


def solution(mesh):
    placed = (
        P("col", None),
        P("col", "row", None, None, None),
        P("col", "row", None),
        P("col", None),
        P("col", None),
        P(),
        P(("col", "row"), None),
    )
    return jax.shard_map(
        body,
        mesh=mesh,
        in_specs=placed,
        out_specs=(P(("col", "row"), None), P(), P("col", None)),
        check_vma=False,
    )
```

```python
import functools
import math

import jax
import jax.numpy as jnp
from jax import lax
from jax.experimental import pallas as pl
from jax.experimental.pallas import tpu as pltpu
from jax.sharding import PartitionSpec as P

F = 512
BLOCK = 128
NX, NYL, NC = 4, 2, 2
NZ, NYH = 8, 2
N_COL = NX * NYL * NC
N_ROW = NZ * NYH
E_DEV = 10
ROWS = 48
SLOTS = ROWS // N_ROW
MAX_LEN = 16
CHUNK = 256
PIECE = CHUNK // N_ROW
MESH = pl.DeviceIdType.MESH
HALF = E_DEV * BLOCK // 2
OVER = 6 * BLOCK
WIDE = F // 2
NY = NYL * NYH
MIB = 1 << 20


def place():
    col, row = lax.axis_index("col"), lax.axis_index("row")
    core = lax.rem(col, NC)
    yl = lax.rem(col // NC, NYL)
    x = col // (NC * NYL)
    z = row // NYH
    yh = lax.rem(row, NYH)
    return col, row, x, yl, core, z, yh


def col_of(x, yl, core):
    return (lax.rem(x + NX, NX) * NYL + yl) * NC + core


def row_of(z, yh):
    return lax.rem(z + NZ, NZ) * NYH + yh


def greet(peers, meanwhile=None):
    barrier = pltpu.get_barrier_semaphore()
    for peer in peers:
        pl.semaphore_signal(barrier, inc=1, device_id=peer, device_id_type=MESH)
    if meanwhile is not None:
        meanwhile()
    pl.semaphore_wait(barrier, len(peers))


def in_hbm(*arrays):
    return [pltpu.with_memory_space_constraint(array, pltpu.HBM) for array in arrays]


class Copies:
    def __init__(self, send, recv):
        self.send, self.recv, self.count, self.all = send, recv, 0, []

    def start(self, src, dst, peer):
        copy = pltpu.make_async_remote_copy(
            src_ref=src,
            dst_ref=dst,
            send_sem=self.send.at[self.count],
            recv_sem=self.recv.at[self.count],
            device_id=peer,
            device_id_type=MESH,
        )
        copy.start()
        self.count += 1
        self.all.append(copy)
        return copy

    def start_all(self, copies, received):
        for src, dst, peer in copies:
            copy = pltpu.make_async_remote_copy(
                src_ref=src,
                dst_ref=dst,
                send_sem=self.send.at[self.count],
                recv_sem=self.recv.at[self.count],
                device_id=peer,
                device_id_type=MESH,
            )
            copy.start()
        total = pltpu.make_async_remote_copy(
            src_ref=received,
            dst_ref=received,
            send_sem=self.send.at[self.count],
            recv_sem=self.recv.at[self.count],
            device_id=copies[0][2],
            device_id_type=MESH,
        )
        self.count += 1
        self.all.append(total)
        return total

    def finish(self):
        for copy in self.all:
            copy.wait_send()


GATHER_COPIES = 64


def gather_kernel(
    a_in, f_in, c_in, g_out, f_out, c_out, c_raw, c_pad, c_all, send, recv, local
):
    col, row, x, yl, core, z, yh = place()
    up, down = (col, row_of(z + 1, yh)), (col, row_of(z - 1, yh))
    across = (col, row_of(z, 1 - yh))
    right, left = (col_of(x + 1, yl, core), row), (col_of(x - 1, yl, core), row)
    beside = (col_of(x, 1 - yl, core), row)
    twin = (col_of(x, yl, 1 - core), row)
    others = [(col, lax.rem(row + d, N_ROW)) for d in range(1, N_ROW)]

    own = [
        pltpu.make_async_copy(a_in, g_out.at[row], local.at[0]),
        pltpu.make_async_copy(f_in, f_out.at[col], local.at[1]),
    ]

    def columns():
        load = pltpu.make_async_copy(c_in, c_raw, local.at[2])
        load.start()
        for copy in own:
            copy.start()
        load.wait()
        c_pad[...] = jnp.zeros_like(c_pad)
        c_pad[:, 0:E_DEV] = c_raw[...]

    greet(others + [right, left, beside, twin], columns)
    go = Copies(send, recv)

    low, high = pl.ds(0, OVER), pl.ds(OVER, E_DEV * BLOCK - OVER)
    own_low = (a_in.at[low], g_out.at[row, low])
    own_high = (a_in.at[high], g_out.at[row, high])
    ways = ((1, up), (-1, down))
    got = {("a", 0, way): go.start(*own_low, peer) for way, peer in ways}
    cross = go.start(*own_high, across)
    f_beside = go.start(f_in, f_out.at[col], beside)
    f_right = go.start(f_in, f_out.at[col], right)
    f_left = go.start(f_in, f_out.at[col], left)
    got.update({("b", 0, way): go.start(*own_high, peer) for way, peer in ways})
    over = [go.start(*own_low, across)]
    twins = [go.start(f_in, f_out.at[col], twin)]
    own.append(pltpu.make_async_copy(c_pad, c_out.at[row], local.at[3]))
    own[-1].start()
    cols = go.start_all([(c_pad, c_out.at[row], peer) for peer in others], c_all)

    def rows_of(stream, t, way):
        if t < 3:
            return low if stream == "a" else high
        if stream == "a":
            return pl.ds(0, HALF) if way == 1 else pl.ds(HALF, OVER - HALF)
        if stream == "b":
            return None if way == 1 else high
        size = (E_DEV * BLOCK - OVER) // 2
        return pl.ds(OVER if way == 1 else OVER + size, size)

    def arrived(stream, t, way):
        if (stream, t, way) in got:
            got[stream, t, way].wait_recv()
        if stream == "a":
            part = g_out.at[row_of(z - way * (t + 1), yh), rows_of(stream, t, way)]
            over.append(go.start(part, part, across))

    def pass_on(stream, t):
        y = 1 - yh if stream == "c" else yh
        for way, peer in ways:
            rows = rows_of(stream, t, way)
            part = g_out.at[row_of(z - way * t, y), rows] if rows is not None else None
            if t and stream == "a":
                got[stream, t - 1, way].wait_recv()
            elif t:
                arrived(stream, t - 1, way)
            if rows is not None:
                got[stream, t, way] = go.start(part, part, peer)
            if t and stream == "a":
                arrived_low = g_out.at[row_of(z - way * t, y), low]
                over.append(go.start(arrived_low, arrived_low, across))

    def chunk(dx, y):
        return f_out.at[col_of(x + dx, y, core)]

    f_beside.wait_recv()
    part = chunk(0, 1 - yl)
    f_right2 = go.start(part, part, right)
    f_left2 = go.start(part, part, left)
    twins.append(go.start(part, part, twin))
    cross.wait_recv()
    pass_on("c", 0)
    pass_on("a", 1)
    f_right.wait_recv()
    part = chunk(-1, yl)
    far_right = go.start(part, part, right)
    twins.append(go.start(part, part, twin))
    f_left.wait_recv()
    part = chunk(1, yl)
    twins.append(go.start(part, part, twin))
    pass_on("b", 1)
    pass_on("c", 1)
    f_left2.wait_recv()
    part = chunk(1, 1 - yl)
    far_left = go.start(part, part, left)
    twins.append(go.start(part, part, twin))
    f_right2.wait_recv()
    part = chunk(-1, 1 - yl)
    twins.append(go.start(part, part, twin))
    pass_on("a", 2)
    pass_on("b", 2)
    pass_on("c", 2)
    far_right.wait_recv()
    part = chunk(2, yl)
    twins.append(go.start(part, part, twin))
    far_left.wait_recv()
    part = chunk(2, 1 - yl)
    twins.append(go.start(part, part, twin))
    pass_on("a", 3)
    pass_on("b", 3)
    pass_on("c", 3)
    cols.wait_recv()
    for copy in twins:
        copy.wait_recv()
    for stream in ("a", "b", "c"):
        for way in (1, -1):
            arrived(stream, 3, way)
    for copy in over:
        copy.wait_recv()
    for copy in own:
        copy.wait()
    go.finish()


def gather(values, features, columns):
    any_space = pl.BlockSpec(memory_space=pl.ANY)
    hbm = pl.BlockSpec(memory_space=pltpu.HBM)
    return pl.pallas_call(
        gather_kernel,
        name="gather",
        out_shape=(
            jax.ShapeDtypeStruct((N_ROW, E_DEV * BLOCK, BLOCK), jnp.bfloat16),
            jax.ShapeDtypeStruct((N_COL, CHUNK, F), jnp.bfloat16),
            jax.ShapeDtypeStruct((N_ROW, 1, 128), jnp.int32),
        ),
        in_specs=[hbm, hbm, hbm],
        out_specs=(any_space, any_space, any_space),
        scratch_shapes=[
            pltpu.VMEM((1, E_DEV), jnp.int32),
            pltpu.VMEM((1, 128), jnp.int32),
            pltpu.VMEM((N_ROW - 1, 1, 128), jnp.int32),
            pltpu.SemaphoreType.DMA((GATHER_COPIES,)),
            pltpu.SemaphoreType.DMA((GATHER_COPIES,)),
            pltpu.SemaphoreType.DMA((4,)),
        ],
        compiler_params=pltpu.CompilerParams(
            collective_id=0, has_side_effects=True, vmem_limit_bytes=4 * MIB
        ),
    )(*in_hbm(values, features, columns))


A_SCALE = math.sqrt(2.0 / math.pi)
CUBE = 0.044715


def layer_kernel(
    cols, len_in, own_in, blocks, feats, w_in, cot_in, out, dense, hid, gpre, ghid,
    lengths, owners, weight, cot, acc, sems,
):
    row = lax.axis_index("row")
    small = [
        pltpu.make_async_copy(len_in, lengths, sems.at[0]),
        pltpu.make_async_copy(own_in, owners, sems.at[1]),
    ]
    get_weight = pltpu.make_async_copy(w_in, weight, sems.at[2])
    get_cot = pltpu.make_async_copy(cot_in, cot, sems.at[3])
    for copy in small + [get_weight, get_cot]:
        copy.start()
    dense[...] = jnp.zeros_like(dense)
    for copy in small:
        copy.wait()

    def find(q, state):
        begin, starts, sizes = state
        length = lengths[0, q]
        which = owners[0, q] - row * SLOTS
        starts = tuple(jnp.where(which == s, begin, v) for s, v in enumerate(starts))
        sizes = tuple(jnp.where(which == s, length, v) for s, v in enumerate(sizes))
        return begin + length, starts, sizes

    nought = jnp.int32(0)
    _, starts, sizes = lax.fori_loop(0, ROWS, find, (nought, (nought,) * SLOTS, (nought,) * SLOTS))
    for s in range(SLOTS):

        @pl.loop(0, sizes[s])
        def _(k):
            g = starts[s] + k
            j = cols[g // E_DEV, 0, lax.rem(g, E_DEV)]
            spot = (pl.ds(s * BLOCK, BLOCK), pl.ds(pl.multiple_of(j * BLOCK, BLOCK), BLOCK))
            dense[spot] = dense[spot] + blocks[g]

    wide = N_COL * CHUNK // 4
    acc[...] = jnp.zeros_like(acc)

    @pl.loop(0, 4)
    def _(i):
        part = pl.ds(pl.multiple_of(i * wide, wide), wide)
        acc[...] += jnp.dot(dense[:, part], feats[part], preferred_element_type=jnp.float32)

    hid[...] = acc[...].astype(jnp.bfloat16)
    get_weight.wait()
    acc[...] = jnp.dot(hid[...], weight[...], preferred_element_type=jnp.float32)
    get_cot.wait()

    @pl.loop(0, SLOTS * BLOCK // 32)
    def _(i):
        part = pl.ds(pl.multiple_of(i * 32, 32), 32)
        v = acc[part]
        square = v * v
        t = jnp.tanh(A_SCALE * (v + CUBE * (v * square)))
        cdf = 0.5 * (1.0 + t)
        out[part] = (v * cdf).astype(jnp.bfloat16)
        slope = cdf + 0.5 * v * (1.0 - t * t) * (A_SCALE * (1.0 + 3.0 * CUBE * square))
        gpre[part] = (cot[part].astype(jnp.float32) * slope).astype(jnp.bfloat16)

    ghid[...] = lax.dot_general(
        gpre[...], weight[...], (((1,), (1,)), ((), ())), preferred_element_type=jnp.float32
    ).astype(jnp.bfloat16)


def layer(cols, lengths, owners, blocks, feats, weight, cotangent):
    smem = pl.BlockSpec(memory_space=pltpu.SMEM)
    vmem = pl.BlockSpec(memory_space=pltpu.VMEM)
    hbm = pl.BlockSpec(memory_space=pltpu.HBM)
    rows = SLOTS * BLOCK
    part = jax.ShapeDtypeStruct((rows, F), jnp.bfloat16)
    return pl.pallas_call(
        layer_kernel,
        name="layer",
        out_shape=(
            part,
            jax.ShapeDtypeStruct((rows, N_COL * CHUNK), jnp.bfloat16),
            part,
            part,
            part,
        ),
        in_specs=[smem, hbm, hbm, vmem, vmem, hbm, hbm],
        out_specs=(vmem,) * 5,
        scratch_shapes=[
            pltpu.SMEM((1, ROWS), jnp.int32),
            pltpu.SMEM((1, ROWS), jnp.int32),
            pltpu.VMEM((F, F), jnp.bfloat16),
            pltpu.VMEM((rows, F), jnp.bfloat16),
            pltpu.VMEM((rows, F), jnp.float32),
            pltpu.SemaphoreType.DMA((4,)),
        ],
        compiler_params=pltpu.CompilerParams(vmem_limit_bytes=32 * MIB),
    )(cols, *in_hbm(lengths, owners), blocks, feats, *in_hbm(weight, cotangent))


REDUCE_COPIES = 40


def f32(value):
    return value.astype(jnp.float32)


def bf16(value):
    return value.astype(jnp.bfloat16)


def added(terms):
    total = f32(terms[0])
    for term in terms[1:]:
        total = total + f32(term)
    return total


OVER_ROWS = (((0,), (0,)), ((), ()))
HALF_CHUNK = CHUNK // 2
ORDER = ((2, 0), (2, 1), (1, 0), (3, 0), (0, 0), (1, 1), (3, 1), (0, 1))


def reduce_kernel(
    dense, hid, gpre, ghid, gw_out, gf_out,
    p0, r0, sx, rx, px, qx, sy, ry, py, qy, whole, pieces, final,
    w_p0, w_r0, w_s, w_rx, w_t, w_ry, w_z, w_all, w_other, send, recv,
):
    col, row, x, yl, core, z, yh = place()
    y = yh * NYL + yl
    twin = (col_of(x, yl, 1 - core), row)

    def at_y(dx, dy):
        there = lax.rem(y + dy, NY)
        return (col_of(x + dx, lax.rem(there, NYL), core), row_of(z, there // NYL))

    x_peers = [at_y(dx, 0) for dx in range(1, NX)]
    y_peers = [at_y(0, dy) for dy in range(1, NY)]
    z_peers = [(col, row_of(z + dz, yh)) for dz in range(1, NZ)]
    plane_peers = [at_y(dx, dy) for dx in range(NX) for dy in range(NY) if dx or dy]
    row_peers = [(col, lax.rem(row + d, N_ROW)) for d in range(1, N_ROW)]
    far_rows = [(col, row_of(z + dz, 1 - yh)) for dz in range(1, NZ)]
    go = Copies(send, recv)

    def lanes(i):
        return pl.ds(pl.multiple_of(i * CHUNK, CHUNK), CHUNK)

    def weight_term(c):
        return lax.dot_general(
            hid[:, lanes(c)], gpre[...], OVER_ROWS, preferred_element_type=jnp.float32
        )

    def side(own):
        return yl if own else 1 - yl

    def feature_term(o, c):
        dx, own = ORDER[o]
        return lax.dot_general(
            dense[:, lanes(col_of(x + dx, side(own), c))], ghid[...], OVER_ROWS,
            preferred_element_type=jnp.float32,
        )

    def first():
        w_p0[...] = bf16(weight_term(1 - core))
        for o in range(8):
            p0[o] = bf16(feature_term(o, 1 - core))

    greet(plane_peers + z_peers + far_rows + [twin], first)

    twins = [go.start(p0.at[o], r0.at[o], twin) for o in range(2)]
    w_twin = go.start(w_p0, w_r0, twin)
    twins += [go.start(p0.at[o], r0.at[o], twin) for o in range(2, 8)]

    def add_twin(o):
        dx, own = ORDER[o]
        term = feature_term(o, core)
        twins[o].wait_recv()
        term = term + f32(r0[o])
        sx[dx, side(own)] = bf16(term[:, :WIDE])
        for h in range(NYH):
            dy = lax.rem(h * NYL + side(own) - y + NY, NY)
            part = term[h * HALF_CHUNK : (h + 1) * HALF_CHUNK, WIDE:]
            sy[dy, lax.rem(x + dx, NX)] = bf16(part)

    def x_send(dx):
        return go.start(sx.at[dx], rx.at[dx - 1], x_peers[dx - 1])

    def y_send(dy):
        return go.start(sy.at[dy], ry.at[dy - 1], y_peers[dy - 1])

    by_x, by_y = {}, {}
    add_twin(0)
    add_twin(1)
    by_x[2] = x_send(2)
    term = weight_term(core)
    w_twin.wait_recv()
    w_s[...] = bf16(term + f32(w_r0[...]))

    def quarter(i):
        return pl.ds(pl.multiple_of(i * (CHUNK // NX), CHUNK // NX), CHUNK // NX)

    def piece(i):
        return pl.ds(pl.multiple_of(i * PIECE, PIECE), PIECE)

    w_x = go.start_all(
        [
            (w_s.at[quarter(lax.rem(x + dx, NX))], w_rx.at[dx - 1], x_peers[dx - 1])
            for dx in range(1, NX)
        ],
        w_rx,
    )
    add_twin(2)
    add_twin(3)
    add_twin(4)
    by_y[1] = y_send(1)
    by_y[3] = y_send(3)
    add_twin(5)
    by_x[1] = x_send(1)
    add_twin(6)
    by_x[3] = x_send(3)
    add_twin(7)
    by_y[2] = y_send(2)

    w_x.wait_recv()
    w_t[...] = added([w_s[quarter(x)]] + [w_rx[i] for i in range(NX - 1)])
    w_y = go.start_all(
        [
            (w_t.at[piece(lax.rem(y + dy, NY))], w_ry.at[dy - 1], y_peers[dy - 1])
            for dy in range(1, NY)
        ],
        w_ry,
    )
    for copy in by_x.values():
        copy.wait_recv()
    for i in range(NYL):
        for h in range(NYH):
            dy = lax.rem(h * NYL + i - y + NY, NY)
            part = pl.ds(h * HALF_CHUNK, HALF_CHUNK)
            px[dy] = bf16(added([sx[0, i, part]] + [rx[j, i, part] for j in range(NX - 1)]))
    x_then_y = go.start_all(
        [(px.at[dy], qx.at[dy - 1], y_peers[dy - 1]) for dy in range(1, NY)], qx
    )
    for copy in by_y.values():
        copy.wait_recv()
    for i in range(NX):
        dx = lax.rem(i - x + NX, NX)
        py[dx] = bf16(added([sy[0, i]] + [ry[j, i] for j in range(NY - 1)]))
    y_then_x = go.start_all(
        [(py.at[dx], qy.at[dx - 1], x_peers[dx - 1]) for dx in range(1, NX)], qy
    )
    w_y.wait_recv()
    w_z[z] = bf16(added([w_t[piece(y)]] + [w_ry[i] for i in range(NY - 1)]))
    w_rows = go.start_all([(w_z.at[z], w_z.at[z], peer) for peer in z_peers], w_z.at[pl.ds(0, NZ - 1)])

    x_then_y.wait_recv()
    whole[:, :WIDE] = bf16(added([px[0]] + [qx[i] for i in range(NY - 1)]))
    y_then_x.wait_recv()
    whole[:, WIDE:] = bf16(added([py[0]] + [qy[i] for i in range(NX - 1)]))
    rows = go.start_all(
        [
            (whole.at[piece(lax.rem(z + dz, NZ))], pieces.at[dz - 1], z_peers[dz - 1])
            for dz in range(1, NZ)
        ],
        pieces,
    )
    w_rows.wait_recv()
    scale = 1.0 / math.sqrt(N_COL * N_ROW * SLOTS * BLOCK)
    w_all[x * NY + y] = bf16(added([w_z[i] for i in range(NZ)]) * scale)
    part = w_all.at[x * NY + y]
    w_plane = go.start_all([(part, part, peer) for peer in plane_peers], w_all.at[pl.ds(0, NX * NY - 1)])
    rows.wait_recv()
    final[yh * NZ + z] = bf16(added([whole[piece(z)]] + [pieces[i] for i in range(NZ - 1)]))
    part = final.at[yh * NZ + z]
    everyone = go.start_all([(part, part, peer) for peer in row_peers], final.at[pl.ds(0, N_ROW - 1)])
    w_plane.wait_recv()
    w_back = go.start(w_all, w_other, twin)
    gw_out[lanes(core)] = f32(w_all[...]).reshape(CHUNK, F)
    w_back.wait_recv()
    gw_out[lanes(1 - core)] = f32(w_other[...]).reshape(CHUNK, F)
    everyone.wait_recv()
    gf_out[...] = f32(final[...]).reshape(CHUNK, F)
    go.finish()


def reduce(dense, hid, gpre, ghid):
    vmem = pl.BlockSpec(memory_space=pltpu.VMEM)

    def buffer(*shape):
        return pltpu.VMEM(shape, jnp.bfloat16)

    def lane(*lead):
        return buffer(*lead, HALF_CHUNK, WIDE)

    quarter = CHUNK // NX
    return pl.pallas_call(
        reduce_kernel,
        name="reduce",
        out_shape=(
            jax.ShapeDtypeStruct((F, F), jnp.float32),
            jax.ShapeDtypeStruct((CHUNK, F), jnp.float32),
        ),
        in_specs=[vmem] * 4,
        out_specs=(vmem, vmem),
        scratch_shapes=[
            buffer(8, CHUNK, F), buffer(8, CHUNK, F),
            buffer(NX, NYL, CHUNK, WIDE), buffer(NX - 1, NYL, CHUNK, WIDE),
            lane(NY), lane(NY - 1),
            lane(NY, NX), lane(NY - 1, NX),
            lane(NX), lane(NX - 1),
            buffer(HALF_CHUNK, F), buffer(NZ - 1, PIECE, F), buffer(N_ROW, PIECE, F),
            buffer(CHUNK, F), buffer(CHUNK, F), buffer(CHUNK, F), buffer(NX - 1, quarter, F),
            pltpu.VMEM((quarter, F), jnp.float32), pltpu.VMEM((NY - 1, PIECE, F), jnp.float32),
            buffer(NZ, PIECE, F), buffer(NX * NY, PIECE, F), buffer(NX * NY, PIECE, F),
            pltpu.SemaphoreType.DMA((REDUCE_COPIES,)),
            pltpu.SemaphoreType.DMA((REDUCE_COPIES,)),
        ],
        compiler_params=pltpu.CompilerParams(
            collective_id=1, has_side_effects=True, vmem_limit_bytes=32 * MIB
        ),
    )(dense, hid, gpre, ghid)


def body(features, block_values, entry_cols, row_lengths, row_owner, weight, cotangent):
    values = block_values.reshape(E_DEV * BLOCK, BLOCK)
    blocks, feats, cols = gather(values, features, entry_cols.reshape(1, E_DEV))
    blocks = blocks.reshape(N_ROW * E_DEV, BLOCK, BLOCK)
    feats = feats.reshape(N_COL * CHUNK, F)
    output, dense, hid, gpre, ghid = layer(
        cols, row_lengths, row_owner, blocks, feats, weight, cotangent
    )
    grad_weight, grad_features = reduce(dense, hid, gpre, ghid)
    return (output, grad_weight, grad_features)


def solution(mesh):
    placed = (
        P("col", None),
        P("col", "row", None, None, None),
        P("col", "row", None),
        P("col", None),
        P("col", None),
        P(),
        P(("col", "row"), None),
    )
    return jax.shard_map(
        body,
        mesh=mesh,
        in_specs=placed,
        out_specs=(P(("col", "row"), None), P(), P("col", None)),
        check_vma=False,
    )
```

```python
import functools
import math

import jax
import jax.numpy as jnp
from jax import lax
from jax.experimental import pallas as pl
from jax.experimental.pallas import tpu as pltpu
from jax.sharding import PartitionSpec as P

F = 512
BLOCK = 128
NX, NYL, NC = 4, 2, 2
NZ, NYH = 8, 2
N_COL = NX * NYL * NC
N_ROW = NZ * NYH
E_DEV = 10
ROWS = 48
SLOTS = ROWS // N_ROW
MAX_LEN = 16
CHUNK = 256
PIECE = CHUNK // N_ROW
SLAB_DEV = SLOTS * BLOCK
FEAT_NODES = N_COL * CHUNK
MESH = pl.DeviceIdType.MESH
HALF = E_DEV * BLOCK // 2
OVER = 5 * BLOCK + 32
WIDE = 208
NY = NYL * NYH
MIB = 1 << 20


def place():
    col, row = lax.axis_index("col"), lax.axis_index("row")
    core = lax.rem(col, NC)
    yl = lax.rem(col // NC, NYL)
    x = col // (NC * NYL)
    z = row // NYH
    yh = lax.rem(row, NYH)
    return col, row, x, yl, core, z, yh


def col_of(x, yl, core):
    return (lax.rem(x + NX, NX) * NYL + yl) * NC + core


def row_of(z, yh):
    return lax.rem(z + NZ, NZ) * NYH + yh


def greet(peers, meanwhile=None):
    barrier = pltpu.get_barrier_semaphore()
    for peer in peers:
        pl.semaphore_signal(barrier, inc=1, device_id=peer, device_id_type=MESH)
    if meanwhile is not None:
        meanwhile()
    pl.semaphore_wait(barrier, len(peers))


def in_hbm(*arrays):
    return [pltpu.with_memory_space_constraint(array, pltpu.HBM) for array in arrays]


class Copies:
    def __init__(self, send, recv):
        self.send, self.recv, self.count, self.all = send, recv, 0, []

    def start(self, src, dst, peer):
        copy = pltpu.make_async_remote_copy(
            src_ref=src,
            dst_ref=dst,
            send_sem=self.send.at[self.count],
            recv_sem=self.recv.at[self.count],
            device_id=peer,
            device_id_type=MESH,
        )
        copy.start()
        self.count += 1
        self.all.append(copy)
        return copy

    def group(self, received):
        group = Group(self.send.at[self.count], self.recv.at[self.count], received)
        self.count += 1
        self.all.append(group)
        return group

    def start_all(self, copies, received):
        group = self.group(received)
        for copy in copies:
            group.start(*copy)
        return group

    def finish(self):
        for copy in self.all:
            copy.wait_send()


class Group:
    def __init__(self, send, recv, received):
        self.send, self.recv, self.received, self.peer = send, recv, received, None

    def copy(self, src, dst, peer):
        return pltpu.make_async_remote_copy(
            src_ref=src,
            dst_ref=dst,
            send_sem=self.send,
            recv_sem=self.recv,
            device_id=peer,
            device_id_type=MESH,
        )

    def start(self, src, dst, peer):
        self.peer = peer
        self.copy(src, dst, peer).start()

    def wait_recv(self):
        self.copy(self.received, self.received, self.peer).wait_recv()

    def wait_send(self):
        self.copy(self.received, self.received, self.peer).wait_send()


GATHER_COPIES = 64


def gather_kernel(
    a_in, f_in, c_in, g_out, f_out, c_out, c_raw, c_pad, c_all, send, recv, local
):
    col, row, x, yl, core, z, yh = place()
    up, down = (col, row_of(z + 1, yh)), (col, row_of(z - 1, yh))
    across = (col, row_of(z, 1 - yh))
    right, left = (col_of(x + 1, yl, core), row), (col_of(x - 1, yl, core), row)
    beside = [(col_of(x, 1 - yl, core), row_of(z, h)) for h in (yh, 1 - yh)]
    twin = (col_of(x, yl, 1 - core), row)
    others = [(col, lax.rem(row + d, N_ROW)) for d in range(1, N_ROW)]

    own = [
        pltpu.make_async_copy(a_in, g_out.at[row], local.at[0]),
        pltpu.make_async_copy(f_in, f_out.at[col], local.at[1]),
    ]

    def columns():
        load = pltpu.make_async_copy(c_in, c_raw, local.at[2])
        load.start()
        for copy in own:
            copy.start()
        load.wait()
        c_pad[...] = jnp.zeros_like(c_pad)
        c_pad[:, 0:E_DEV] = c_raw[...]

    greet(others + beside + [right, left, twin], columns)
    go = Copies(send, recv)

    low, high = pl.ds(0, OVER), pl.ds(OVER, E_DEV * BLOCK - OVER)
    own_low = (a_in.at[low], g_out.at[row, low])
    own_high = (a_in.at[high], g_out.at[row, high])
    ways = ((1, up), (-1, down))
    got = {("a", 0, way): go.start(*own_low, peer) for way, peer in ways}
    cross = go.start(*own_high, across)
    f_beside = []
    for i, peer in enumerate(beside):
        half = pl.ds(i * (CHUNK // 2), CHUNK // 2)
        f_beside.append(go.start(f_in.at[half], f_out.at[col, half], peer))
    f_right = go.start(f_in, f_out.at[col], right)
    f_left = go.start(f_in, f_out.at[col], left)
    got.update({("b", 0, way): go.start(*own_high, peer) for way, peer in ways})
    over = [go.start(*own_low, across)]
    twins = [go.start(f_in, f_out.at[col], twin)]
    own.append(pltpu.make_async_copy(c_pad, c_out.at[row], local.at[3]))
    own[-1].start()
    cols = go.start_all([(c_pad, c_out.at[row], peer) for peer in others], c_all)

    def rows_of(stream, t, way):
        if t < 3:
            return low if stream == "a" else high
        if stream == "a":
            return pl.ds(0, HALF) if way == 1 else pl.ds(HALF, OVER - HALF)
        if stream == "b":
            return None if way == 1 else high
        size = (E_DEV * BLOCK - OVER) // 2
        return pl.ds(OVER if way == 1 else OVER + size, size)

    def arrived(stream, t, way):
        if (stream, t, way) in got:
            got[stream, t, way].wait_recv()
        if stream == "a":
            part = g_out.at[row_of(z - way * (t + 1), yh), rows_of(stream, t, way)]
            over.append(go.start(part, part, across))

    def pass_on(stream, t):
        y = 1 - yh if stream == "c" else yh
        for way, peer in ways:
            rows = rows_of(stream, t, way)
            part = g_out.at[row_of(z - way * t, y), rows] if rows is not None else None
            if t and stream == "a":
                got[stream, t - 1, way].wait_recv()
            elif t:
                arrived(stream, t - 1, way)
            if rows is not None:
                got[stream, t, way] = go.start(part, part, peer)
            if t and stream == "a":
                arrived_low = g_out.at[row_of(z - way * t, y), low]
                over.append(go.start(arrived_low, arrived_low, across))

    def chunk(dx, y):
        return f_out.at[col_of(x + dx, y, core)]

    for copy in f_beside:
        copy.wait_recv()
    part = chunk(0, 1 - yl)
    f_right2 = go.start(part, part, right)
    f_left2 = go.start(part, part, left)
    twins.append(go.start(part, part, twin))
    cross.wait_recv()
    pass_on("c", 0)
    pass_on("a", 1)
    f_right.wait_recv()
    part = chunk(-1, yl)
    far_right = go.start(part, part, right)
    twins.append(go.start(part, part, twin))
    f_left.wait_recv()
    part = chunk(1, yl)
    twins.append(go.start(part, part, twin))
    pass_on("b", 1)
    pass_on("c", 1)
    f_left2.wait_recv()
    part = chunk(1, 1 - yl)
    far_left = go.start(part, part, left)
    twins.append(go.start(part, part, twin))
    f_right2.wait_recv()
    part = chunk(-1, 1 - yl)
    twins.append(go.start(part, part, twin))
    pass_on("a", 2)
    pass_on("b", 2)
    pass_on("c", 2)
    far_right.wait_recv()
    part = chunk(2, yl)
    twins.append(go.start(part, part, twin))
    far_left.wait_recv()
    part = chunk(2, 1 - yl)
    twins.append(go.start(part, part, twin))
    pass_on("a", 3)
    pass_on("b", 3)
    pass_on("c", 3)
    cols.wait_recv()
    for copy in twins:
        copy.wait_recv()
    for stream in ("a", "b", "c"):
        for way in (1, -1):
            arrived(stream, 3, way)
    for copy in over:
        copy.wait_recv()
    for copy in own:
        copy.wait()
    go.finish()


def gather(values, features, columns):
    any_space = pl.BlockSpec(memory_space=pl.ANY)
    hbm = pl.BlockSpec(memory_space=pltpu.HBM)
    return pl.pallas_call(
        gather_kernel,
        name="gather",
        out_shape=(
            jax.ShapeDtypeStruct((N_ROW, E_DEV * BLOCK, BLOCK), jnp.bfloat16),
            jax.ShapeDtypeStruct((N_COL, CHUNK, F), jnp.bfloat16),
            jax.ShapeDtypeStruct((N_ROW, 1, 128), jnp.int32),
        ),
        in_specs=[hbm, hbm, hbm],
        out_specs=(any_space, any_space, any_space),
        scratch_shapes=[
            pltpu.VMEM((1, E_DEV), jnp.int32),
            pltpu.VMEM((1, 128), jnp.int32),
            pltpu.VMEM((N_ROW - 1, 1, 128), jnp.int32),
            pltpu.SemaphoreType.DMA((GATHER_COPIES,)),
            pltpu.SemaphoreType.DMA((GATHER_COPIES,)),
            pltpu.SemaphoreType.DMA((4,)),
        ],
        compiler_params=pltpu.CompilerParams(
            collective_id=0, has_side_effects=True, vmem_limit_bytes=4 * MIB
        ),
    )(*in_hbm(values, features, columns))


def place_kernel(cols, len_in, own_in, blocks, dense, lengths, owners, sems):
    row = lax.axis_index("row")
    small = [
        pltpu.make_async_copy(len_in, lengths, sems.at[0]),
        pltpu.make_async_copy(own_in, owners, sems.at[1]),
    ]
    for copy in small:
        copy.start()
    dense[...] = jnp.zeros_like(dense)
    for copy in small:
        copy.wait()

    def find(q, state):
        begin, starts, sizes = state
        length = lengths[0, q]
        which = owners[0, q] - row * SLOTS
        starts = tuple(jnp.where(which == s, begin, v) for s, v in enumerate(starts))
        sizes = tuple(jnp.where(which == s, length, v) for s, v in enumerate(sizes))
        return begin + length, starts, sizes

    nought = jnp.int32(0)
    _, starts, sizes = lax.fori_loop(0, ROWS, find, (nought, (nought,) * SLOTS, (nought,) * SLOTS))
    for s in range(SLOTS):

        @pl.loop(0, sizes[s])
        def _(k):
            g = starts[s] + k
            j = cols[g // E_DEV, 0, lax.rem(g, E_DEV)]
            spot = (pl.ds(s * BLOCK, BLOCK), pl.ds(pl.multiple_of(j * BLOCK, BLOCK), BLOCK))
            dense[spot] = dense[spot] + blocks[g]


def place_blocks(cols, lengths, owners, blocks):
    smem = pl.BlockSpec(memory_space=pltpu.SMEM)
    vmem = pl.BlockSpec(memory_space=pltpu.VMEM)
    hbm = pl.BlockSpec(memory_space=pltpu.HBM)
    return pl.pallas_call(
        place_kernel,
        name="place",
        out_shape=jax.ShapeDtypeStruct((SLAB_DEV, FEAT_NODES), jnp.bfloat16),
        in_specs=[smem, hbm, hbm, vmem],
        out_specs=vmem,
        scratch_shapes=[
            pltpu.SMEM((1, ROWS), jnp.int32),
            pltpu.SMEM((1, ROWS), jnp.int32),
            pltpu.SemaphoreType.DMA((2,)),
        ],
        compiler_params=pltpu.CompilerParams(vmem_limit_bytes=24 * MIB),
    )(cols, *in_hbm(lengths, owners), blocks)


REDUCE_COPIES = 40
A_SCALE = math.sqrt(2.0 / math.pi)
CUBE = 0.044715


def f32(value):
    return value.astype(jnp.float32)


def bf16(value):
    return value.astype(jnp.bfloat16)


def added(terms):
    total = f32(terms[0])
    for term in terms[1:]:
        total = total + f32(term)
    return total


OVER_ROWS = (((0,), (0,)), ((), ()))
HALF_CHUNK = CHUNK // 2
ORDER = ((2, 1), (2, 0), (1, 1), (3, 1), (0, 1), (1, 0), (3, 0), (0, 0))


def layer(dense, feats, weight, cot, out, acc, hid, gpre, ghid, get_weight, get_cot):
    wide = FEAT_NODES // 4
    acc[...] = jnp.zeros_like(acc)

    @pl.loop(0, 4)
    def _(i):
        part = pl.ds(pl.multiple_of(i * wide, wide), wide)
        acc[...] += jnp.dot(dense[:, part], feats[part], preferred_element_type=jnp.float32)

    hid[...] = acc[...].astype(jnp.bfloat16)
    get_weight.wait()
    acc[...] = jnp.dot(hid[...], weight[...], preferred_element_type=jnp.float32)
    get_cot.wait()

    @pl.loop(0, SLAB_DEV // 32)
    def _(i):
        part = pl.ds(pl.multiple_of(i * 32, 32), 32)
        v = acc[part]
        square = v * v
        t = jnp.tanh(A_SCALE * (v + CUBE * (v * square)))
        cdf = 0.5 * (1.0 + t)
        out[part] = (v * cdf).astype(jnp.bfloat16)
        slope = cdf + 0.5 * v * (1.0 - t * t) * (A_SCALE * (1.0 + 3.0 * CUBE * square))
        gpre[part] = (cot[part].astype(jnp.float32) * slope).astype(jnp.bfloat16)

    ghid[...] = lax.dot_general(
        weight[...], gpre[...], (((1,), (1,)), ((), ())), preferred_element_type=jnp.float32
    ).astype(jnp.bfloat16)


def reduce_kernel(
    dense, feats, w_in, cot_in, out, gw_out, gf_out,
    weight, cot, acc, hid, gpre, ghid, local,
    p0, r0, sx, rx, x_relay, px, qx, sy, ry, y_relay, py, qy, whole, pieces, final,
    w_p0, w_r0, w_s, w_rx, w_t, w_ry, w_z, w_all, w_other, send, recv,
):
    col, row, x, yl, core, z, yh = place()
    y = yh * NYL + yl
    twin = (col_of(x, yl, 1 - core), row)

    def at_y(dx, dy):
        there = lax.rem(y + dy, NY)
        return (col_of(x + dx, lax.rem(there, NYL), core), row_of(z, there // NYL))

    x_peers = [at_y(dx, 0) for dx in range(1, NX)]
    y_peers = [at_y(0, dy) for dy in range(1, NY)]
    z_peers = [(col, row_of(z + dz, yh)) for dz in range(1, NZ)]
    plane_peers = [at_y(dx, dy) for dx in range(NX) for dy in range(NY) if dx or dy]
    row_peers = [(col, lax.rem(row + d, N_ROW)) for d in range(1, N_ROW)]
    far_rows = [(col, row_of(z + dz, 1 - yh)) for dz in range(1, NZ)]
    go = Copies(send, recv)

    def lanes(i):
        return pl.ds(pl.multiple_of(i * CHUNK, CHUNK), CHUNK)

    def weight_term(c):
        return lax.dot_general(
            hid[:, lanes(c)], gpre[...], OVER_ROWS, preferred_element_type=jnp.float32
        )

    def side(own):
        return yl if own else 1 - yl

    def feature_term(o, c):
        dx, own = ORDER[o]
        nodes = lanes(col_of(x + dx, side(own), c))
        return jnp.dot(ghid[...], dense[:, nodes], preferred_element_type=jnp.float32)

    get_weight = pltpu.make_async_copy(w_in, weight, local.at[0])
    get_cot = pltpu.make_async_copy(cot_in, cot, local.at[1])
    get_weight.start()
    get_cot.start()

    def first():
        layer(dense, feats, weight, cot, out, acc, hid, gpre, ghid, get_weight, get_cot)
        for o in range(2):
            p0[o] = bf16(feature_term(o, 1 - core))
        w_p0[...] = bf16(weight_term(1 - core))

    greet(plane_peers + z_peers + far_rows + [twin], first)

    twins = [go.start(p0.at[o], r0.at[o], twin) for o in range(2)]
    w_twin = go.start(w_p0, w_r0, twin)

    def to_twin(o):
        p0[o] = bf16(feature_term(o, 1 - core))
        twins.append(go.start(p0.at[o], r0.at[o], twin))

    def add_twin(o):
        dx, own = ORDER[o]
        term = feature_term(o, core)
        twins[o].wait_recv()
        term = term + f32(r0[o])
        sx[dx, side(own)] = bf16(term[:WIDE])
        if dx == 2:
            far_x[own] = go.start(sx.at[2, side(own)], x_relay.at[own], x_peers[0 if own else 2])
        elif (dx, own) in ((3, 1), (1, 0)):
            near_x(dx, own)
        there = lax.rem(x + dx, NX)
        part = bf16(term[WIDE:])
        for h in range(NYH):
            half = lax.rem(yh + h, NYH)
            dy = lax.rem(half * NYL + side(own) - y + NY, NY)
            sy[dy, there] = jnp.where(half == 0, part[:, :HALF_CHUNK], part[:, HALF_CHUNK:])
        way = 1 if dx in (1, 2) else 3
        if own:
            far_y[dx] = go.start(sy.at[2, there], y_relay.at[dx], y_peers[way - 1])
        else:
            near_y(4 - way, dx)

    def near_x(dx, own):
        part = rx.at[dx // 2, side(own)]
        by_x.append(go.start(sx.at[dx, side(own)], part, x_peers[dx - 1]))

    def near_y(dy, dx):
        there = lax.rem(x + dx, NX)
        by_y[dy].start(sy.at[dy, there], ry.at[dy // 2, there], y_peers[dy - 1])

    def relay_x(dx, own):
        far_x[own].wait_recv()
        sx[dx, side(own)] = bf16(added([sx[dx, side(own)], x_relay[own]]))
        near_x(dx, own)

    def relay_y(dx):
        dy = 1 if dx in (1, 2) else 3
        there = lax.rem(x + dx, NX)
        far_y[dx].wait_recv()
        sy[dy, there] = bf16(added([sy[dy, there], y_relay[dx]]))
        near_y(dy, dx)

    by_x, far_x, far_y = [], {}, {}
    by_y = {dy: go.group(ry.at[0]) for dy in (1, 3)}
    to_twin(2)
    to_twin(3)
    for o in range(4):
        add_twin(o)
        to_twin(o + 4)
    term = weight_term(core)
    w_twin.wait_recv()
    w_s[...] = bf16(term + f32(w_r0[...]))

    def quarter(i):
        return pl.ds(pl.multiple_of(i * (CHUNK // NX), CHUNK // NX), CHUNK // NX)

    def piece(i):
        return pl.ds(pl.multiple_of(i * PIECE, PIECE), PIECE)

    w_x = go.start_all(
        [
            (w_s.at[quarter(lax.rem(x + dx, NX))], w_rx.at[dx - 1], x_peers[dx - 1])
            for dx in range(1, NX)
        ],
        w_rx,
    )
    add_twin(4)
    add_twin(5)
    add_twin(6)
    add_twin(7)
    relay_x(1, 1)
    relay_x(3, 0)
    for dx in (2, 1, 3, 0):
        relay_y(dx)

    def units(i):
        return pl.ds(pl.multiple_of(i * (F // NZ), F // NZ), F // NZ)

    w_x.wait_recv()
    w_t[...] = added([w_s[quarter(x)]] + [w_rx[i] for i in range(NX - 1)])
    w_y = go.start_all(
        [
            (w_t.at[piece(lax.rem(y + dy, NY))], w_ry.at[dy - 1], y_peers[dy - 1])
            for dy in range(1, NY)
        ],
        w_ry,
    )
    for copy in by_x:
        copy.wait_recv()
    for i in range(NYL):
        for h in range(NYH):
            dy = lax.rem(h * NYL + i - y + NY, NY)
            part = (slice(None), slice(h * HALF_CHUNK, (h + 1) * HALF_CHUNK))
            px[dy] = bf16(added([sx[(0, i) + part]] + [rx[(j, i) + part] for j in range(2)]))
    x_then_y = go.start_all(
        [(px.at[dy], qx.at[dy - 1], y_peers[dy - 1]) for dy in range(1, NY)], qx
    )
    for copy in by_y.values():
        copy.wait_recv()
    for i in range(NX):
        dx = lax.rem(i - x + NX, NX)
        py[dx] = bf16(added([sy[0, i]] + [ry[j, i] for j in range(2)]))
    y_then_x = go.start_all(
        [(py.at[dx], qy.at[dx - 1], x_peers[dx - 1]) for dx in range(1, NX)], qy
    )
    w_y.wait_recv()
    w_z[z] = bf16(added([w_t[piece(y)]] + [w_ry[i] for i in range(NY - 1)]))
    w_rows = go.start_all([(w_z.at[z], w_z.at[z], peer) for peer in z_peers], w_z.at[pl.ds(0, NZ - 1)])

    x_then_y.wait_recv()
    whole[:WIDE] = bf16(added([px[0]] + [qx[i] for i in range(NY - 1)]))
    y_then_x.wait_recv()
    whole[WIDE:] = bf16(added([py[0]] + [qy[i] for i in range(NX - 1)]))
    rows = go.start_all(
        [
            (whole.at[units(lax.rem(z + dz, NZ))], pieces.at[dz - 1], z_peers[dz - 1])
            for dz in range(1, NZ)
        ],
        pieces,
    )
    w_rows.wait_recv()
    scale = 1.0 / math.sqrt(N_COL * N_ROW * SLOTS * BLOCK)
    w_all[x * NY + y] = bf16(added([w_z[i] for i in range(NZ)]) * scale)
    part = w_all.at[x * NY + y]
    w_plane = go.start_all([(part, part, peer) for peer in plane_peers], w_all.at[pl.ds(0, NX * NY - 1)])
    rows.wait_recv()
    final[yh * NZ + z] = bf16(added([whole[units(z)]] + [pieces[i] for i in range(NZ - 1)]))
    part = final.at[yh * NZ + z]
    everyone = go.start_all([(part, part, peer) for peer in row_peers], final.at[pl.ds(0, N_ROW - 1)])
    w_plane.wait_recv()
    w_back = go.start(w_all, w_other, twin)
    gw_out[lanes(core)] = w_all[...].reshape(CHUNK, F)
    w_back.wait_recv()
    gw_out[lanes(1 - core)] = w_other[...].reshape(CHUNK, F)
    everyone.wait_recv()
    gf_out[...] = final[...].reshape(NYH, F, HALF_CHUNK)
    go.finish()


def reduce(dense, feats, weight, cotangent):
    vmem = pl.BlockSpec(memory_space=pltpu.VMEM)
    hbm = pl.BlockSpec(memory_space=pltpu.HBM)
    rows = (SLAB_DEV, F)

    def buffer(*shape):
        return pltpu.VMEM(shape, jnp.bfloat16)

    def lane(rows, *lead):
        return buffer(*lead, rows, HALF_CHUNK)

    quarter = CHUNK // NX
    return pl.pallas_call(
        reduce_kernel,
        name="reduce",
        out_shape=(
            jax.ShapeDtypeStruct(rows, jnp.bfloat16),
            jax.ShapeDtypeStruct((F, F), jnp.bfloat16),
            jax.ShapeDtypeStruct((NYH, F, HALF_CHUNK), jnp.bfloat16),
        ),
        in_specs=[vmem, vmem, hbm, hbm],
        out_specs=(vmem, vmem, vmem),
        scratch_shapes=[
            buffer(F, F), buffer(*rows), pltpu.VMEM(rows, jnp.float32),
            buffer(*rows), buffer(*rows), buffer(F, SLAB_DEV), pltpu.SemaphoreType.DMA((2,)),
            buffer(8, F, CHUNK), buffer(8, F, CHUNK),
            buffer(NX, NYL, WIDE, CHUNK), buffer(2, NYL, WIDE, CHUNK), buffer(2, WIDE, CHUNK),
            lane(WIDE, NY), lane(WIDE, NY - 1),
            lane(F - WIDE, NY, NX), lane(F - WIDE, 2, NX), lane(F - WIDE, NX),
            lane(F - WIDE, NX), lane(F - WIDE, NX - 1),
            buffer(F, HALF_CHUNK), buffer(NZ - 1, F // NZ, HALF_CHUNK), buffer(N_ROW, F // NZ, HALF_CHUNK),
            buffer(CHUNK, F), buffer(CHUNK, F), buffer(CHUNK, F), buffer(NX - 1, quarter, F),
            pltpu.VMEM((quarter, F), jnp.float32), pltpu.VMEM((NY - 1, PIECE, F), jnp.float32),
            buffer(NZ, PIECE, F), buffer(NX * NY, PIECE, F), buffer(NX * NY, PIECE, F),
            pltpu.SemaphoreType.DMA((REDUCE_COPIES,)),
            pltpu.SemaphoreType.DMA((REDUCE_COPIES,)),
        ],
        compiler_params=pltpu.CompilerParams(
            collective_id=1, has_side_effects=True, vmem_limit_bytes=32 * MIB
        ),
    )(dense, feats, *in_hbm(weight, cotangent))


def finish_kernel(out_in, gw_in, gf_in, out, gw_out, gf_out, gw, gf, sems):
    copies = [pltpu.make_async_copy(out_in, out, sems.at[0])]
    copies[0].start()
    for i in range(2):
        part = pl.ds(i * CHUNK, CHUNK)
        gw[part] = f32(gw_in[part])
        copies.append(pltpu.make_async_copy(gw.at[part], gw_out.at[part], sems.at[1 + i]))
        copies[-1].start()
    for h in range(NYH):
        gf[h * HALF_CHUNK : (h + 1) * HALF_CHUNK] = f32(gf_in[h]).T
    copies.append(pltpu.make_async_copy(gf, gf_out, sems.at[3]))
    copies[-1].start()
    for copy in copies:
        copy.wait()


def finish(output, gw, gf):
    vmem = pl.BlockSpec(memory_space=pltpu.VMEM)
    hbm = pl.BlockSpec(memory_space=pltpu.HBM)
    return pl.pallas_call(
        finish_kernel,
        name="finish",
        out_shape=(
            jax.ShapeDtypeStruct(output.shape, jnp.bfloat16),
            jax.ShapeDtypeStruct(gw.shape, jnp.float32),
            jax.ShapeDtypeStruct((CHUNK, F), jnp.float32),
        ),
        in_specs=[vmem] * 3,
        out_specs=(hbm,) * 3,
        scratch_shapes=[
            pltpu.VMEM(gw.shape, jnp.float32),
            pltpu.VMEM((CHUNK, F), jnp.float32),
            pltpu.SemaphoreType.DMA((4,)),
        ],
        compiler_params=pltpu.CompilerParams(vmem_limit_bytes=8 * MIB),
    )(output, gw, gf)


def body(features, block_values, entry_cols, row_lengths, row_owner, weight, cotangent):
    values = block_values.reshape(E_DEV * BLOCK, BLOCK)
    blocks, feats, cols = gather(values, features, entry_cols.reshape(1, E_DEV))
    blocks = blocks.reshape(N_ROW * E_DEV, BLOCK, BLOCK)
    dense = place_blocks(cols, row_lengths, row_owner, blocks)
    return finish(*reduce(dense, feats.reshape(FEAT_NODES, F), weight, cotangent))


def solution(mesh):
    placed = (
        P("col", None),
        P("col", "row", None, None, None),
        P("col", "row", None),
        P("col", None),
        P("col", None),
        P(),
        P(("col", "row"), None),
    )
    return jax.shard_map(
        body,
        mesh=mesh,
        in_specs=placed,
        out_specs=(P(("col", "row"), None), P(), P("col", None)),
        check_vma=False,
    )
```

```python
import functools
import math

import jax
import jax.numpy as jnp
from jax import lax
from jax.experimental import pallas as pl
from jax.experimental.pallas import tpu as pltpu
from jax.sharding import PartitionSpec as P

F = 512
BLOCK = 128
NX, NYL, NC = 4, 2, 2
NZ, NYH = 8, 2
N_COL = NX * NYL * NC
N_ROW = NZ * NYH
E_DEV = 10
ROWS = 48
SLOTS = ROWS // N_ROW
MAX_LEN = 16
CHUNK = 256
PIECE = CHUNK // N_ROW
SLAB_DEV = SLOTS * BLOCK
FEAT_NODES = N_COL * CHUNK
MESH = pl.DeviceIdType.MESH
HALF = E_DEV * BLOCK // 2
OVER = 768
WIDE = 208
NY = NYL * NYH
MIB = 1 << 20


def place():
    col, row = lax.axis_index("col"), lax.axis_index("row")
    core = lax.rem(col, NC)
    yl = lax.rem(col // NC, NYL)
    x = col // (NC * NYL)
    z = row // NYH
    yh = lax.rem(row, NYH)
    return col, row, x, yl, core, z, yh


def col_of(x, yl, core):
    return (lax.rem(x + NX, NX) * NYL + yl) * NC + core


def row_of(z, yh):
    return lax.rem(z + NZ, NZ) * NYH + yh


def greet(peers, meanwhile=None):
    barrier = pltpu.get_barrier_semaphore()
    for peer in peers:
        pl.semaphore_signal(barrier, inc=1, device_id=peer, device_id_type=MESH)
    if meanwhile is not None:
        meanwhile()
    pl.semaphore_wait(barrier, len(peers))


def in_hbm(*arrays):
    return [pltpu.with_memory_space_constraint(array, pltpu.HBM) for array in arrays]


class Copies:
    def __init__(self, send, recv):
        self.send, self.recv, self.count, self.all = send, recv, 0, []

    def start(self, src, dst, peer):
        copy = pltpu.make_async_remote_copy(
            src_ref=src,
            dst_ref=dst,
            send_sem=self.send.at[self.count],
            recv_sem=self.recv.at[self.count],
            device_id=peer,
            device_id_type=MESH,
        )
        copy.start()
        self.count += 1
        self.all.append(copy)
        return copy

    def group(self, received):
        group = Group(self.send.at[self.count], self.recv.at[self.count], received)
        self.count += 1
        self.all.append(group)
        return group

    def start_all(self, copies, received):
        group = self.group(received)
        for copy in copies:
            group.start(*copy)
        return group

    def finish(self):
        for copy in self.all:
            copy.wait_send()


class Group:
    def __init__(self, send, recv, received):
        self.send, self.recv, self.received, self.peer = send, recv, received, None

    def copy(self, src, dst, peer):
        return pltpu.make_async_remote_copy(
            src_ref=src,
            dst_ref=dst,
            send_sem=self.send,
            recv_sem=self.recv,
            device_id=peer,
            device_id_type=MESH,
        )

    def start(self, src, dst, peer):
        self.peer = peer
        self.copy(src, dst, peer).start()

    def wait_recv(self):
        self.copy(self.received, self.received, self.peer).wait_recv()

    def wait_send(self):
        self.copy(self.received, self.received, self.peer).wait_send()


GATHER_COPIES = 64


def gather_kernel(
    a_in, f_in, c_in, g_out, f_out, c_out, c_raw, c_pad, c_all, send, recv, local
):
    col, row, x, yl, core, z, yh = place()
    up, down = (col, row_of(z + 1, yh)), (col, row_of(z - 1, yh))
    across = (col, row_of(z, 1 - yh))
    right, left = (col_of(x + 1, yl, core), row), (col_of(x - 1, yl, core), row)
    beside = [(col_of(x, 1 - yl, core), row_of(z, h)) for h in (yh, 1 - yh)]
    twin = (col_of(x, yl, 1 - core), row)
    others = [(col, lax.rem(row + d, N_ROW)) for d in range(1, N_ROW)]

    own = [
        pltpu.make_async_copy(a_in, g_out.at[row], local.at[0]),
        pltpu.make_async_copy(f_in, f_out.at[col], local.at[1]),
    ]

    def columns():
        load = pltpu.make_async_copy(c_in, c_raw, local.at[2])
        load.start()
        for copy in own:
            copy.start()
        load.wait()
        c_pad[...] = jnp.zeros_like(c_pad)
        c_pad[:, 0:E_DEV] = c_raw[...]

    greet(others + beside + [right, left, twin], columns)
    go = Copies(send, recv)

    low, high = pl.ds(0, OVER), pl.ds(OVER, E_DEV * BLOCK - OVER)
    own_low = (a_in.at[low], g_out.at[row, low])
    own_high = (a_in.at[high], g_out.at[row, high])
    ways = ((1, up), (-1, down))
    got = {("a", 0, way): go.start(*own_low, peer) for way, peer in ways}
    cross = go.start(*own_high, across)
    f_beside = []
    for i, peer in enumerate(beside):
        half = pl.ds(i * (CHUNK // 2), CHUNK // 2)
        f_beside.append(go.start(f_in.at[half], f_out.at[col, half], peer))
    f_right = go.start(f_in, f_out.at[col], right)
    f_left = go.start(f_in, f_out.at[col], left)
    got.update({("b", 0, way): go.start(*own_high, peer) for way, peer in ways})
    over = [go.start(*own_low, across)]
    twins = [go.start(f_in, f_out.at[col], twin)]
    own.append(pltpu.make_async_copy(c_pad, c_out.at[row], local.at[3]))
    own[-1].start()
    cols = go.start_all([(c_pad, c_out.at[row], peer) for peer in others], c_all)

    def rows_of(stream, t, way):
        if t < 3:
            return low if stream == "a" else high
        if stream != "c":
            first, last = (0, OVER) if stream == "a" else (OVER, E_DEV * BLOCK)
            first, last = (first, min(last, HALF)) if way == 1 else (max(first, HALF), last)
            return pl.ds(first, last - first) if first < last else None
        size = (E_DEV * BLOCK - OVER) // 2
        return pl.ds(OVER if way == 1 else OVER + size, size)

    def arrived(stream, t, way):
        if (stream, t, way) in got:
            got[stream, t, way].wait_recv()
        rows = rows_of(stream, t, way)
        if stream == "a" and rows is not None:
            part = g_out.at[row_of(z - way * (t + 1), yh), rows]
            over.append(go.start(part, part, across))

    def pass_on(stream, t):
        y = 1 - yh if stream == "c" else yh
        for way, peer in ways:
            rows = rows_of(stream, t, way)
            part = g_out.at[row_of(z - way * t, y), rows] if rows is not None else None
            if t and stream == "a":
                got[stream, t - 1, way].wait_recv()
            elif t:
                arrived(stream, t - 1, way)
            if rows is not None:
                got[stream, t, way] = go.start(part, part, peer)
            if t and stream == "a":
                arrived_low = g_out.at[row_of(z - way * t, y), low]
                over.append(go.start(arrived_low, arrived_low, across))

    def chunk(dx, y):
        return f_out.at[col_of(x + dx, y, core)]

    for copy in f_beside:
        copy.wait_recv()
    part = chunk(0, 1 - yl)
    f_right2 = go.start(part, part, right)
    f_left2 = go.start(part, part, left)
    twins.append(go.start(part, part, twin))
    cross.wait_recv()
    pass_on("c", 0)
    pass_on("a", 1)
    f_right.wait_recv()
    part = chunk(-1, yl)
    far_right = go.start(part, part, right)
    twins.append(go.start(part, part, twin))
    f_left.wait_recv()
    part = chunk(1, yl)
    twins.append(go.start(part, part, twin))
    pass_on("c", 1)
    pass_on("b", 1)
    f_left2.wait_recv()
    part = chunk(1, 1 - yl)
    far_left = go.start(part, part, left)
    twins.append(go.start(part, part, twin))
    f_right2.wait_recv()
    part = chunk(-1, 1 - yl)
    twins.append(go.start(part, part, twin))
    pass_on("a", 2)
    pass_on("c", 2)
    pass_on("b", 2)
    far_right.wait_recv()
    part = chunk(2, yl)
    twins.append(go.start(part, part, twin))
    far_left.wait_recv()
    part = chunk(2, 1 - yl)
    twins.append(go.start(part, part, twin))
    pass_on("a", 3)
    pass_on("b", 3)
    pass_on("c", 3)
    cols.wait_recv()
    for copy in twins:
        copy.wait_recv()
    for stream in ("a", "b", "c"):
        for way in (1, -1):
            arrived(stream, 3, way)
    for copy in over:
        copy.wait_recv()
    for copy in own:
        copy.wait()
    go.finish()


def gather(values, features, columns):
    any_space = pl.BlockSpec(memory_space=pl.ANY)
    hbm = pl.BlockSpec(memory_space=pltpu.HBM)
    return pl.pallas_call(
        gather_kernel,
        name="gather",
        out_shape=(
            jax.ShapeDtypeStruct((N_ROW, E_DEV * BLOCK, BLOCK), jnp.bfloat16),
            jax.ShapeDtypeStruct((N_COL, CHUNK, F), jnp.bfloat16),
            jax.ShapeDtypeStruct((N_ROW, 1, 128), jnp.int32),
        ),
        in_specs=[hbm, hbm, hbm],
        out_specs=(any_space, any_space, any_space),
        scratch_shapes=[
            pltpu.VMEM((1, E_DEV), jnp.int32),
            pltpu.VMEM((1, 128), jnp.int32),
            pltpu.VMEM((N_ROW - 1, 1, 128), jnp.int32),
            pltpu.SemaphoreType.DMA((GATHER_COPIES,)),
            pltpu.SemaphoreType.DMA((GATHER_COPIES,)),
            pltpu.SemaphoreType.DMA((4,)),
        ],
        compiler_params=pltpu.CompilerParams(
            collective_id=0, has_side_effects=True, vmem_limit_bytes=4 * MIB
        ),
    )(*in_hbm(values, features, columns))


def place_kernel(cols_in, len_in, own_in, blocks, dense, cols, lengths, owners, sems):
    row = lax.axis_index("row")
    small = [
        pltpu.make_async_copy(len_in, lengths, sems.at[0]),
        pltpu.make_async_copy(own_in, owners, sems.at[1]),
        pltpu.make_async_copy(cols_in, cols, sems.at[2]),
    ]
    for copy in small:
        copy.start()
    dense[...] = jnp.zeros_like(dense)
    for copy in small:
        copy.wait()

    def find(q, state):
        begin, starts, sizes = state
        length = lengths[0, q]
        which = owners[0, q] - row * SLOTS
        starts = tuple(jnp.where(which == s, begin, v) for s, v in enumerate(starts))
        sizes = tuple(jnp.where(which == s, length, v) for s, v in enumerate(sizes))
        return begin + length, starts, sizes

    nought = jnp.int32(0)
    _, starts, sizes = lax.fori_loop(0, ROWS, find, (nought, (nought,) * SLOTS, (nought,) * SLOTS))
    for s in range(SLOTS):

        @pl.loop(0, sizes[s])
        def _(k):
            g = starts[s] + k
            j = cols[g // E_DEV, 0, lax.rem(g, E_DEV)]
            spot = (pl.ds(s * BLOCK, BLOCK), pl.ds(pl.multiple_of(j * BLOCK, BLOCK), BLOCK))
            dense[spot] = dense[spot] + blocks[g]


def place_blocks(cols, lengths, owners, blocks):
    any_space = pl.BlockSpec(memory_space=pl.ANY)
    vmem = pl.BlockSpec(memory_space=pltpu.VMEM)
    hbm = pl.BlockSpec(memory_space=pltpu.HBM)
    return pl.pallas_call(
        place_kernel,
        name="place",
        out_shape=jax.ShapeDtypeStruct((SLAB_DEV, FEAT_NODES), jnp.bfloat16),
        in_specs=[any_space, hbm, hbm, vmem],
        out_specs=vmem,
        scratch_shapes=[
            pltpu.SMEM((N_ROW, 1, 128), jnp.int32),
            pltpu.SMEM((1, ROWS), jnp.int32),
            pltpu.SMEM((1, ROWS), jnp.int32),
            pltpu.SemaphoreType.DMA((3,)),
        ],
        compiler_params=pltpu.CompilerParams(vmem_limit_bytes=24 * MIB),
    )(cols, *in_hbm(lengths, owners), blocks)


REDUCE_COPIES = 40
A_SCALE = math.sqrt(2.0 / math.pi)
CUBE = 0.044715


def f32(value):
    return value.astype(jnp.float32)


def bf16(value):
    return value.astype(jnp.bfloat16)


def added(terms):
    total = f32(terms[0])
    for term in terms[1:]:
        total = total + f32(term)
    return total


OVER_ROWS = (((0,), (0,)), ((), ()))
HALF_CHUNK = CHUNK // 2
ORDER = ((2, 1), (2, 0), (1, 1), (3, 1), (0, 1), (1, 0), (3, 0), (0, 0))


def layer(dense, feats, weight, cot, out, acc, hid, gpre, ghid, get_weight, get_cot):
    wide = FEAT_NODES // 4
    acc[...] = jnp.zeros_like(acc)

    @pl.loop(0, 4)
    def _(i):
        part = pl.ds(pl.multiple_of(i * wide, wide), wide)
        acc[...] += jnp.dot(dense[:, part], feats[part], preferred_element_type=jnp.float32)

    hid[...] = acc[...].astype(jnp.bfloat16)
    get_weight.wait()
    acc[...] = jnp.dot(hid[...], weight[...], preferred_element_type=jnp.float32)
    get_cot.wait()

    @pl.loop(0, SLAB_DEV // 32)
    def _(i):
        part = pl.ds(pl.multiple_of(i * 32, 32), 32)
        v = acc[part]
        square = v * v
        t = jnp.tanh(A_SCALE * (v + CUBE * (v * square)))
        cdf = 0.5 * (1.0 + t)
        out[part] = (v * cdf).astype(jnp.bfloat16)
        slope = cdf + 0.5 * v * (1.0 - t * t) * (A_SCALE * (1.0 + 3.0 * CUBE * square))
        gpre[part] = (cot[part].astype(jnp.float32) * slope).astype(jnp.bfloat16)

    ghid[...] = lax.dot_general(
        weight[...], gpre[...], (((1,), (1,)), ((), ())), preferred_element_type=jnp.float32
    ).astype(jnp.bfloat16)


def reduce_kernel(
    dense, feats, w_in, cot_in, out, gw_out, gf_out,
    weight, cot, acc, hid, gpre, ghid, local,
    p0, r0, sx, rx, x_relay, px, qx, sy, ry, y_relay, py, qy, whole, pieces, final,
    w_p0, w_r0, w_s, w_rx, w_t, w_ry, w_z, w_all, w_other, send, recv,
):
    col, row, x, yl, core, z, yh = place()
    y = yh * NYL + yl
    twin = (col_of(x, yl, 1 - core), row)

    def at_y(dx, dy):
        there = lax.rem(y + dy, NY)
        return (col_of(x + dx, lax.rem(there, NYL), core), row_of(z, there // NYL))

    x_peers = [at_y(dx, 0) for dx in range(1, NX)]
    y_peers = [at_y(0, dy) for dy in range(1, NY)]
    z_peers = [(col, row_of(z + dz, yh)) for dz in range(1, NZ)]
    plane_peers = [at_y(dx, dy) for dx in range(NX) for dy in range(NY) if dx or dy]
    row_peers = [(col, lax.rem(row + d, N_ROW)) for d in range(1, N_ROW)]
    far_rows = [(col, row_of(z + dz, 1 - yh)) for dz in range(1, NZ)]
    go = Copies(send, recv)

    def lanes(i):
        return pl.ds(pl.multiple_of(i * CHUNK, CHUNK), CHUNK)

    def weight_term(c):
        return lax.dot_general(
            hid[:, lanes(c)], gpre[...], OVER_ROWS, preferred_element_type=jnp.float32
        )

    def side(own):
        return yl if own else 1 - yl

    def feature_term(o, c):
        dx, own = ORDER[o]
        nodes = lanes(col_of(x + dx, side(own), c))
        return jnp.dot(ghid[...], dense[:, nodes], preferred_element_type=jnp.float32)

    get_weight = pltpu.make_async_copy(w_in, weight, local.at[0])
    get_cot = pltpu.make_async_copy(cot_in, cot, local.at[1])
    get_weight.start()
    get_cot.start()

    def first():
        layer(dense, feats, weight, cot, out, acc, hid, gpre, ghid, get_weight, get_cot)
        for o in range(8):
            p0[o] = bf16(feature_term(o, 1 - core))
        w_p0[...] = bf16(weight_term(1 - core))

    greet(plane_peers + z_peers + far_rows + [twin], first)

    twins = [go.start(p0.at[o], r0.at[o], twin) for o in range(2)]
    w_twin = go.start(w_p0, w_r0, twin)
    twins += [go.start(p0.at[o], r0.at[o], twin) for o in range(2, 8)]

    def to_twin(o):
        p0[o] = bf16(feature_term(o, 1 - core))
        twins.append(go.start(p0.at[o], r0.at[o], twin))

    def add_twin(o):
        dx, own = ORDER[o]
        term = feature_term(o, core)
        twins[o].wait_recv()
        term = term + f32(r0[o])
        sx[dx, side(own)] = bf16(term[:WIDE])
        if dx == 2:
            far_x[own] = go.start(sx.at[2, side(own)], x_relay.at[own], x_peers[0 if own else 2])
        elif (dx, own) in ((3, 1), (1, 0)):
            near_x(dx, own)
        there = lax.rem(x + dx, NX)
        part = bf16(term[WIDE:])
        for h in range(NYH):
            half = lax.rem(yh + h, NYH)
            dy = lax.rem(half * NYL + side(own) - y + NY, NY)
            sy[dy, there] = jnp.where(half == 0, part[:, :HALF_CHUNK], part[:, HALF_CHUNK:])
        way = 1 if dx in (1, 2) else 3
        if own:
            far_y[dx] = go.start(sy.at[2, there], y_relay.at[dx], y_peers[way - 1])
        else:
            near_y(4 - way, dx)

    def near_x(dx, own):
        part = rx.at[dx // 2, side(own)]
        by_x.append(go.start(sx.at[dx, side(own)], part, x_peers[dx - 1]))

    def near_y(dy, dx):
        there = lax.rem(x + dx, NX)
        by_y[dy].start(sy.at[dy, there], ry.at[dy // 2, there], y_peers[dy - 1])

    def relay_x(dx, own):
        far_x[own].wait_recv()
        sx[dx, side(own)] = bf16(added([sx[dx, side(own)], x_relay[own]]))
        near_x(dx, own)

    def relay_y(dx):
        dy = 1 if dx in (1, 2) else 3
        there = lax.rem(x + dx, NX)
        far_y[dx].wait_recv()
        sy[dy, there] = bf16(added([sy[dy, there], y_relay[dx]]))
        near_y(dy, dx)

    by_x, far_x, far_y = [], {}, {}
    by_y = {dy: go.group(ry.at[0]) for dy in (1, 3)}
    for o in range(4):
        add_twin(o)
    term = weight_term(core)
    w_twin.wait_recv()
    w_s[...] = bf16(term + f32(w_r0[...]))

    def quarter(i):
        return pl.ds(pl.multiple_of(i * (CHUNK // NX), CHUNK // NX), CHUNK // NX)

    def piece(i):
        return pl.ds(pl.multiple_of(i * PIECE, PIECE), PIECE)

    w_x = go.start_all(
        [
            (w_s.at[quarter(lax.rem(x + dx, NX))], w_rx.at[dx - 1], x_peers[dx - 1])
            for dx in range(1, NX)
        ],
        w_rx,
    )
    add_twin(4)
    add_twin(5)
    add_twin(6)
    add_twin(7)
    relay_x(1, 1)
    relay_x(3, 0)
    for dx in (2, 1, 3, 0):
        relay_y(dx)

    def units(i):
        return pl.ds(pl.multiple_of(i * (F // NZ), F // NZ), F // NZ)

    w_x.wait_recv()
    w_t[...] = added([w_s[quarter(x)]] + [w_rx[i] for i in range(NX - 1)])
    w_y = go.start_all(
        [
            (w_t.at[piece(lax.rem(y + dy, NY))], w_ry.at[dy - 1], y_peers[dy - 1])
            for dy in range(1, NY)
        ],
        w_ry,
    )
    for copy in by_x:
        copy.wait_recv()
    for i in range(NYL):
        for h in range(NYH):
            dy = lax.rem(h * NYL + i - y + NY, NY)
            part = (slice(None), slice(h * HALF_CHUNK, (h + 1) * HALF_CHUNK))
            px[dy] = bf16(added([sx[(0, i) + part]] + [rx[(j, i) + part] for j in range(2)]))
    x_then_y = go.start_all(
        [(px.at[dy], qx.at[dy - 1], y_peers[dy - 1]) for dy in range(1, NY)], qx
    )
    for copy in by_y.values():
        copy.wait_recv()
    for i in range(NX):
        dx = lax.rem(i - x + NX, NX)
        py[dx] = bf16(added([sy[0, i]] + [ry[j, i] for j in range(2)]))
    y_then_x = go.start_all(
        [(py.at[dx], qy.at[dx - 1], x_peers[dx - 1]) for dx in range(1, NX)], qy
    )
    w_y.wait_recv()
    w_z[z] = bf16(added([w_t[piece(y)]] + [w_ry[i] for i in range(NY - 1)]))
    w_rows = go.start_all([(w_z.at[z], w_z.at[z], peer) for peer in z_peers], w_z.at[pl.ds(0, NZ - 1)])

    x_then_y.wait_recv()
    whole[:WIDE] = bf16(added([px[0]] + [qx[i] for i in range(NY - 1)]))
    y_then_x.wait_recv()
    whole[WIDE:] = bf16(added([py[0]] + [qy[i] for i in range(NX - 1)]))
    rows = go.start_all(
        [
            (whole.at[units(lax.rem(z + dz, NZ))], pieces.at[dz - 1], z_peers[dz - 1])
            for dz in range(1, NZ)
        ],
        pieces,
    )
    w_rows.wait_recv()
    scale = 1.0 / math.sqrt(N_COL * N_ROW * SLOTS * BLOCK)
    w_all[x * NY + y] = bf16(added([w_z[i] for i in range(NZ)]) * scale)
    part = w_all.at[x * NY + y]
    w_plane = go.start_all([(part, part, peer) for peer in plane_peers], w_all.at[pl.ds(0, NX * NY - 1)])
    rows.wait_recv()
    final[yh * NZ + z] = bf16(added([whole[units(z)]] + [pieces[i] for i in range(NZ - 1)]))
    part = final.at[yh * NZ + z]
    everyone = go.start_all([(part, part, peer) for peer in row_peers], final.at[pl.ds(0, N_ROW - 1)])
    w_plane.wait_recv()
    w_back = go.start(w_all, w_other, twin)
    gw_out[lanes(core)] = w_all[...].reshape(CHUNK, F)
    w_back.wait_recv()
    gw_out[lanes(1 - core)] = w_other[...].reshape(CHUNK, F)
    everyone.wait_recv()
    gf_out[...] = final[...].reshape(NYH, F, HALF_CHUNK)
    go.finish()


def reduce(dense, feats, weight, cotangent):
    vmem = pl.BlockSpec(memory_space=pltpu.VMEM)
    hbm = pl.BlockSpec(memory_space=pltpu.HBM)
    rows = (SLAB_DEV, F)

    def buffer(*shape):
        return pltpu.VMEM(shape, jnp.bfloat16)

    def lane(rows, *lead):
        return buffer(*lead, rows, HALF_CHUNK)

    quarter = CHUNK // NX
    return pl.pallas_call(
        reduce_kernel,
        name="reduce",
        out_shape=(
            jax.ShapeDtypeStruct(rows, jnp.bfloat16),
            jax.ShapeDtypeStruct((F, F), jnp.bfloat16),
            jax.ShapeDtypeStruct((NYH, F, HALF_CHUNK), jnp.bfloat16),
        ),
        in_specs=[vmem, vmem, hbm, hbm],
        out_specs=(vmem, vmem, vmem),
        scratch_shapes=[
            buffer(F, F), buffer(*rows), pltpu.VMEM(rows, jnp.float32),
            buffer(*rows), buffer(*rows), buffer(F, SLAB_DEV), pltpu.SemaphoreType.DMA((2,)),
            buffer(8, F, CHUNK), buffer(8, F, CHUNK),
            buffer(NX, NYL, WIDE, CHUNK), buffer(2, NYL, WIDE, CHUNK), buffer(2, WIDE, CHUNK),
            lane(WIDE, NY), lane(WIDE, NY - 1),
            lane(F - WIDE, NY, NX), lane(F - WIDE, 2, NX), lane(F - WIDE, NX),
            lane(F - WIDE, NX), lane(F - WIDE, NX - 1),
            buffer(F, HALF_CHUNK), buffer(NZ - 1, F // NZ, HALF_CHUNK), buffer(N_ROW, F // NZ, HALF_CHUNK),
            buffer(CHUNK, F), buffer(CHUNK, F), buffer(CHUNK, F), buffer(NX - 1, quarter, F),
            pltpu.VMEM((quarter, F), jnp.float32), pltpu.VMEM((NY - 1, PIECE, F), jnp.float32),
            buffer(NZ, PIECE, F), buffer(NX * NY, PIECE, F), buffer(NX * NY, PIECE, F),
            pltpu.SemaphoreType.DMA((REDUCE_COPIES,)),
            pltpu.SemaphoreType.DMA((REDUCE_COPIES,)),
        ],
        compiler_params=pltpu.CompilerParams(
            collective_id=1, has_side_effects=True, vmem_limit_bytes=32 * MIB
        ),
    )(dense, feats, *in_hbm(weight, cotangent))


def finish_kernel(out_in, gw_in, gf_in, out, gw_out, gf_out, gw, gf, sems):
    copies = [pltpu.make_async_copy(out_in, out, sems.at[0])]
    copies[0].start()
    for i in range(2):
        part = pl.ds(i * CHUNK, CHUNK)
        gw[part] = f32(gw_in[part])
        copies.append(pltpu.make_async_copy(gw.at[part], gw_out.at[part], sems.at[1 + i]))
        copies[-1].start()
    for h in range(NYH):
        gf[h * HALF_CHUNK : (h + 1) * HALF_CHUNK] = f32(gf_in[h]).T
    copies.append(pltpu.make_async_copy(gf, gf_out, sems.at[3]))
    copies[-1].start()
    for copy in copies:
        copy.wait()


def finish(output, gw, gf):
    vmem = pl.BlockSpec(memory_space=pltpu.VMEM)
    hbm = pl.BlockSpec(memory_space=pltpu.HBM)
    return pl.pallas_call(
        finish_kernel,
        name="finish",
        out_shape=(
            jax.ShapeDtypeStruct(output.shape, jnp.bfloat16),
            jax.ShapeDtypeStruct(gw.shape, jnp.float32),
            jax.ShapeDtypeStruct((CHUNK, F), jnp.float32),
        ),
        in_specs=[vmem] * 3,
        out_specs=(hbm,) * 3,
        scratch_shapes=[
            pltpu.VMEM(gw.shape, jnp.float32),
            pltpu.VMEM((CHUNK, F), jnp.float32),
            pltpu.SemaphoreType.DMA((4,)),
        ],
        compiler_params=pltpu.CompilerParams(vmem_limit_bytes=8 * MIB),
    )(output, gw, gf)


def body(features, block_values, entry_cols, row_lengths, row_owner, weight, cotangent):
    values = block_values.reshape(E_DEV * BLOCK, BLOCK)
    blocks, feats, cols = gather(values, features, entry_cols.reshape(1, E_DEV))
    blocks = blocks.reshape(N_ROW * E_DEV, BLOCK, BLOCK)
    dense = place_blocks(cols, row_lengths, row_owner, blocks)
    return finish(*reduce(dense, feats.reshape(FEAT_NODES, F), weight, cotangent))


def solution(mesh):
    placed = (
        P("col", None),
        P("col", "row", None, None, None),
        P("col", "row", None),
        P("col", None),
        P("col", None),
        P(),
        P(("col", "row"), None),
    )
    return jax.shard_map(
        body,
        mesh=mesh,
        in_specs=placed,
        out_specs=(P(("col", "row"), None), P(), P("col", None)),
        check_vma=False,
    )
```

```python
import functools
import math

import jax
import jax.numpy as jnp
from jax import lax
from jax.experimental import pallas as pl
from jax.experimental.pallas import tpu as pltpu
from jax.sharding import PartitionSpec as P

F = 512
BLOCK = 128
NX, NYL, NC = 4, 2, 2
NZ, NYH = 8, 2
N_COL = NX * NYL * NC
N_ROW = NZ * NYH
E_DEV = 10
ROWS = 48
SLOTS = ROWS // N_ROW
MAX_LEN = 16
CHUNK = 256
PIECE = CHUNK // N_ROW
SLAB_DEV = SLOTS * BLOCK
FEAT_NODES = N_COL * CHUNK
MESH = pl.DeviceIdType.MESH
HALF = E_DEV * BLOCK // 2
OVER = 768
WIDE = 208
NY = NYL * NYH
MIB = 1 << 20


def place():
    col, row = lax.axis_index("col"), lax.axis_index("row")
    core = lax.rem(col, NC)
    yl = lax.rem(col // NC, NYL)
    x = col // (NC * NYL)
    z = row // NYH
    yh = lax.rem(row, NYH)
    return col, row, x, yl, core, z, yh


def col_of(x, yl, core):
    return (lax.rem(x + NX, NX) * NYL + yl) * NC + core


def row_of(z, yh):
    return lax.rem(z + NZ, NZ) * NYH + yh


def greet(peers, meanwhile=None):
    barrier = pltpu.get_barrier_semaphore()
    for peer in peers:
        pl.semaphore_signal(barrier, inc=1, device_id=peer, device_id_type=MESH)
    if meanwhile is not None:
        meanwhile()
    pl.semaphore_wait(barrier, len(peers))


def in_hbm(*arrays):
    return [pltpu.with_memory_space_constraint(array, pltpu.HBM) for array in arrays]


class Copies:
    def __init__(self, send, recv):
        self.send, self.recv, self.count, self.all = send, recv, 0, []

    def start(self, src, dst, peer):
        copy = pltpu.make_async_remote_copy(
            src_ref=src,
            dst_ref=dst,
            send_sem=self.send.at[self.count],
            recv_sem=self.recv.at[self.count],
            device_id=peer,
            device_id_type=MESH,
        )
        copy.start()
        self.count += 1
        self.all.append(copy)
        return copy

    def group(self, received):
        group = Group(self.send.at[self.count], self.recv.at[self.count], received)
        self.count += 1
        self.all.append(group)
        return group

    def start_all(self, copies, received):
        group = self.group(received)
        for copy in copies:
            group.start(*copy)
        return group

    def finish(self):
        for copy in self.all:
            copy.wait_send()


class Group:
    def __init__(self, send, recv, received):
        self.send, self.recv, self.received, self.peer = send, recv, received, None

    def copy(self, src, dst, peer):
        return pltpu.make_async_remote_copy(
            src_ref=src,
            dst_ref=dst,
            send_sem=self.send,
            recv_sem=self.recv,
            device_id=peer,
            device_id_type=MESH,
        )

    def start(self, src, dst, peer):
        self.peer = peer
        self.copy(src, dst, peer).start()

    def wait_recv(self):
        self.copy(self.received, self.received, self.peer).wait_recv()

    def wait_send(self):
        self.copy(self.received, self.received, self.peer).wait_send()


GATHER_COPIES = 64


def gather_kernel(
    a_in, f_in, c_in, g_out, f_out, c_out, c_raw, c_pad, c_all, send, recv, local
):
    col, row, x, yl, core, z, yh = place()
    up, down = (col, row_of(z + 1, yh)), (col, row_of(z - 1, yh))
    across = (col, row_of(z, 1 - yh))
    right, left = (col_of(x + 1, yl, core), row), (col_of(x - 1, yl, core), row)
    beside = [(col_of(x, 1 - yl, core), row_of(z, h)) for h in (yh, 1 - yh)]
    twin = (col_of(x, yl, 1 - core), row)
    others = [(col, lax.rem(row + d, N_ROW)) for d in range(1, N_ROW)]

    own = [
        pltpu.make_async_copy(a_in, g_out.at[row], local.at[0]),
        pltpu.make_async_copy(f_in, f_out.at[col], local.at[1]),
    ]

    def columns():
        load = pltpu.make_async_copy(c_in, c_raw, local.at[2])
        load.start()
        for copy in own:
            copy.start()
        load.wait()
        c_pad[...] = jnp.zeros_like(c_pad)
        c_pad[:, 0:E_DEV] = c_raw[...]

    greet(others + beside + [right, left, twin], columns)
    go = Copies(send, recv)

    low, high = pl.ds(0, OVER), pl.ds(OVER, E_DEV * BLOCK - OVER)
    own_low = (a_in.at[low], g_out.at[row, low])
    own_high = (a_in.at[high], g_out.at[row, high])
    ways = ((1, up), (-1, down))
    got = {("a", 0, way): [go.start(*own_low, peer)] for way, peer in ways}
    cross = go.start(*own_high, across)
    f_beside = []
    for i, peer in enumerate(beside):
        half = pl.ds(i * (CHUNK // 2), CHUNK // 2)
        f_beside.append(go.start(f_in.at[half], f_out.at[col, half], peer))
    f_right = go.start(f_in, f_out.at[col], right)
    f_left = go.start(f_in, f_out.at[col], left)
    got.update({("b", 0, way): [go.start(*own_high, peer)] for way, peer in ways})
    over = [go.start(*own_low, across)]
    twins = [go.start(f_in, f_out.at[col], twin)]
    own.append(pltpu.make_async_copy(c_pad, c_out.at[row], local.at[3]))
    own[-1].start()
    cols = go.start_all([(c_pad, c_out.at[row], peer) for peer in others], c_all)

    def rows_of(stream, t, way):
        if t < 3:
            return [low if stream == "a" else high]
        if stream != "c":
            first, last = (0, OVER) if stream == "a" else (OVER, E_DEV * BLOCK)
            first, last = (first, min(last, HALF)) if way == 1 else (max(first, HALF), last)
            cuts = [first, (first + last) // 2, last] if stream == "a" and way == 1 else [first, last]
            return [pl.ds(i, j - i) for i, j in zip(cuts, cuts[1:]) if i < j]
        size = (E_DEV * BLOCK - OVER) // 2
        return [pl.ds(OVER if way == 1 else OVER + size, size)]

    def arrived(stream, t, way):
        for copy, rows in zip(got[stream, t, way], rows_of(stream, t, way)):
            copy.wait_recv()
            if stream == "a":
                part = g_out.at[row_of(z - way * (t + 1), yh), rows]
                over.append(go.start(part, part, across))

    def pass_on(stream, t):
        y = 1 - yh if stream == "c" else yh
        for way, peer in ways:
            if t and stream == "a":
                got[stream, t - 1, way][0].wait_recv()
            elif t:
                arrived(stream, t - 1, way)
            parts = [g_out.at[row_of(z - way * t, y), rows] for rows in rows_of(stream, t, way)]
            got[stream, t, way] = [go.start(part, part, peer) for part in parts]
            if t and stream == "a":
                arrived_low = g_out.at[row_of(z - way * t, y), low]
                over.append(go.start(arrived_low, arrived_low, across))

    def chunk(dx, y):
        return f_out.at[col_of(x + dx, y, core)]

    for copy in f_beside:
        copy.wait_recv()
    part = chunk(0, 1 - yl)
    f_right2 = go.start(part, part, right)
    f_left2 = go.start(part, part, left)
    twins.append(go.start(part, part, twin))
    cross.wait_recv()
    pass_on("c", 0)
    pass_on("a", 1)
    f_right.wait_recv()
    part = chunk(-1, yl)
    far_right = go.start(part, part, right)
    twins.append(go.start(part, part, twin))
    f_left.wait_recv()
    part = chunk(1, yl)
    twins.append(go.start(part, part, twin))
    pass_on("c", 1)
    pass_on("b", 1)
    f_left2.wait_recv()
    part = chunk(1, 1 - yl)
    far_left = go.start(part, part, left)
    twins.append(go.start(part, part, twin))
    f_right2.wait_recv()
    part = chunk(-1, 1 - yl)
    twins.append(go.start(part, part, twin))
    pass_on("a", 2)
    pass_on("c", 2)
    pass_on("b", 2)
    far_right.wait_recv()
    part = chunk(2, yl)
    twins.append(go.start(part, part, twin))
    far_left.wait_recv()
    part = chunk(2, 1 - yl)
    twins.append(go.start(part, part, twin))
    pass_on("a", 3)
    pass_on("b", 3)
    pass_on("c", 3)
    cols.wait_recv()
    for copy in twins:
        copy.wait_recv()
    for stream in ("a", "b", "c"):
        for way in (1, -1):
            arrived(stream, 3, way)
    for copy in over:
        copy.wait_recv()
    for copy in own:
        copy.wait()
    go.finish()


def gather(values, features, columns):
    any_space = pl.BlockSpec(memory_space=pl.ANY)
    hbm = pl.BlockSpec(memory_space=pltpu.HBM)
    return pl.pallas_call(
        gather_kernel,
        name="gather",
        out_shape=(
            jax.ShapeDtypeStruct((N_ROW, E_DEV * BLOCK, BLOCK), jnp.bfloat16),
            jax.ShapeDtypeStruct((N_COL, CHUNK, F), jnp.bfloat16),
            jax.ShapeDtypeStruct((N_ROW, 1, 128), jnp.int32),
        ),
        in_specs=[hbm, hbm, hbm],
        out_specs=(any_space, any_space, any_space),
        scratch_shapes=[
            pltpu.VMEM((1, E_DEV), jnp.int32),
            pltpu.VMEM((1, 128), jnp.int32),
            pltpu.VMEM((N_ROW - 1, 1, 128), jnp.int32),
            pltpu.SemaphoreType.DMA((GATHER_COPIES,)),
            pltpu.SemaphoreType.DMA((GATHER_COPIES,)),
            pltpu.SemaphoreType.DMA((4,)),
        ],
        compiler_params=pltpu.CompilerParams(
            collective_id=0, has_side_effects=True, vmem_limit_bytes=4 * MIB
        ),
    )(*in_hbm(values, features, columns))


def place_kernel(cols_in, len_in, own_in, blocks, dense, cols, lengths, owners, sems):
    row = lax.axis_index("row")
    small = [
        pltpu.make_async_copy(len_in, lengths, sems.at[0]),
        pltpu.make_async_copy(own_in, owners, sems.at[1]),
        pltpu.make_async_copy(cols_in, cols, sems.at[2]),
    ]
    for copy in small:
        copy.start()
    dense[...] = jnp.zeros_like(dense)
    for copy in small:
        copy.wait()

    def find(q, state):
        begin, starts, sizes = state
        length = lengths[0, q]
        which = owners[0, q] - row * SLOTS
        starts = tuple(jnp.where(which == s, begin, v) for s, v in enumerate(starts))
        sizes = tuple(jnp.where(which == s, length, v) for s, v in enumerate(sizes))
        return begin + length, starts, sizes

    nought = jnp.int32(0)
    _, starts, sizes = lax.fori_loop(0, ROWS, find, (nought, (nought,) * SLOTS, (nought,) * SLOTS))
    for s in range(SLOTS):

        @pl.loop(0, sizes[s])
        def _(k):
            g = starts[s] + k
            j = cols[g // E_DEV, 0, lax.rem(g, E_DEV)]
            spot = (pl.ds(s * BLOCK, BLOCK), pl.ds(pl.multiple_of(j * BLOCK, BLOCK), BLOCK))
            dense[spot] = dense[spot] + blocks[g]


def place_blocks(cols, lengths, owners, blocks):
    any_space = pl.BlockSpec(memory_space=pl.ANY)
    vmem = pl.BlockSpec(memory_space=pltpu.VMEM)
    hbm = pl.BlockSpec(memory_space=pltpu.HBM)
    return pl.pallas_call(
        place_kernel,
        name="place",
        out_shape=jax.ShapeDtypeStruct((SLAB_DEV, FEAT_NODES), jnp.bfloat16),
        in_specs=[any_space, hbm, hbm, vmem],
        out_specs=vmem,
        scratch_shapes=[
            pltpu.SMEM((N_ROW, 1, 128), jnp.int32),
            pltpu.SMEM((1, ROWS), jnp.int32),
            pltpu.SMEM((1, ROWS), jnp.int32),
            pltpu.SemaphoreType.DMA((3,)),
        ],
        compiler_params=pltpu.CompilerParams(vmem_limit_bytes=24 * MIB),
    )(cols, *in_hbm(lengths, owners), blocks)


REDUCE_COPIES = 40
A_SCALE = math.sqrt(2.0 / math.pi)
CUBE = 0.044715


def f32(value):
    return value.astype(jnp.float32)


def bf16(value):
    return value.astype(jnp.bfloat16)


def added(terms):
    total = f32(terms[0])
    for term in terms[1:]:
        total = total + f32(term)
    return total


OVER_ROWS = (((0,), (0,)), ((), ()))
HALF_CHUNK = CHUNK // 2
ORDER = ((2, 1), (2, 0), (1, 1), (3, 1), (0, 1), (1, 0), (3, 0), (0, 0))


def layer(dense, feats, weight, cot, out, acc, hid, gpre, ghid, get_weight, get_cot):
    wide = FEAT_NODES // 4
    acc[...] = jnp.zeros_like(acc)

    @pl.loop(0, 4)
    def _(i):
        part = pl.ds(pl.multiple_of(i * wide, wide), wide)
        acc[...] += jnp.dot(dense[:, part], feats[part], preferred_element_type=jnp.float32)

    hid[...] = acc[...].astype(jnp.bfloat16)
    get_weight.wait()
    acc[...] = jnp.dot(hid[...], weight[...], preferred_element_type=jnp.float32)
    get_cot.wait()

    @pl.loop(0, SLAB_DEV // 32)
    def _(i):
        part = pl.ds(pl.multiple_of(i * 32, 32), 32)
        v = acc[part]
        square = v * v
        t = jnp.tanh(A_SCALE * (v + CUBE * (v * square)))
        cdf = 0.5 * (1.0 + t)
        out[part] = (v * cdf).astype(jnp.bfloat16)
        slope = cdf + 0.5 * v * (1.0 - t * t) * (A_SCALE * (1.0 + 3.0 * CUBE * square))
        gpre[part] = (cot[part].astype(jnp.float32) * slope).astype(jnp.bfloat16)

    ghid[...] = lax.dot_general(
        weight[...], gpre[...], (((1,), (1,)), ((), ())), preferred_element_type=jnp.float32
    ).astype(jnp.bfloat16)


def reduce_kernel(
    dense, feats, w_in, cot_in, out, gw_out, gf_out,
    weight, cot, acc, hid, gpre, ghid, local,
    p0, r0, sx, rx, x_relay, px, qx, sy, ry, y_relay, py, qy, whole, pieces, final,
    w_p0, w_r0, w_s, w_rx, w_t, w_ry, w_z, w_all, w_other, send, recv,
):
    col, row, x, yl, core, z, yh = place()
    y = yh * NYL + yl
    twin = (col_of(x, yl, 1 - core), row)

    def at_y(dx, dy):
        there = lax.rem(y + dy, NY)
        return (col_of(x + dx, lax.rem(there, NYL), core), row_of(z, there // NYL))

    x_peers = [at_y(dx, 0) for dx in range(1, NX)]
    y_peers = [at_y(0, dy) for dy in range(1, NY)]
    z_peers = [(col, row_of(z + dz, yh)) for dz in range(1, NZ)]
    plane_peers = [at_y(dx, dy) for dx in (2, 1, 3, 0) for dy in (2, 1, 3, 0) if dx or dy]
    far_first = (4, 3, 5, 2, 6, 1, 7)
    row_peers = [(col, row_of(z + dz, h)) for dz in far_first for h in (1 - yh, yh)]
    row_peers.append((col, row_of(z, 1 - yh)))
    far_rows = [(col, row_of(z + dz, 1 - yh)) for dz in range(1, NZ)]
    go = Copies(send, recv)

    def lanes(i):
        return pl.ds(pl.multiple_of(i * CHUNK, CHUNK), CHUNK)

    def weight_term(c):
        return lax.dot_general(
            hid[:, lanes(c)], gpre[...], OVER_ROWS, preferred_element_type=jnp.float32
        )

    def side(own):
        return yl if own else 1 - yl

    def feature_term(o, c):
        dx, own = ORDER[o]
        nodes = lanes(col_of(x + dx, side(own), c))
        return jnp.dot(ghid[...], dense[:, nodes], preferred_element_type=jnp.float32)

    get_weight = pltpu.make_async_copy(w_in, weight, local.at[0])
    get_cot = pltpu.make_async_copy(cot_in, cot, local.at[1])
    get_weight.start()
    get_cot.start()

    def first():
        layer(dense, feats, weight, cot, out, acc, hid, gpre, ghid, get_weight, get_cot)
        for o in range(8):
            p0[o] = bf16(feature_term(o, 1 - core))
        w_p0[...] = bf16(weight_term(1 - core))

    greet(plane_peers + z_peers + far_rows + [twin], first)

    twins = [go.start(p0.at[o], r0.at[o], twin) for o in range(2)]
    w_twin = go.start(w_p0, w_r0, twin)
    twins += [go.start(p0.at[o], r0.at[o], twin) for o in range(2, 8)]

    def to_twin(o):
        p0[o] = bf16(feature_term(o, 1 - core))
        twins.append(go.start(p0.at[o], r0.at[o], twin))

    def add_twin(o):
        dx, own = ORDER[o]
        term = feature_term(o, core)
        twins[o].wait_recv()
        term = term + f32(r0[o])
        sx[dx, side(own)] = bf16(term[:WIDE])
        if dx == 2:
            far_x[own] = go.start(sx.at[2, side(own)], x_relay.at[own], x_peers[0 if own else 2])
        elif (dx, own) in ((3, 1), (1, 0)):
            near_x(dx, own)
        there = lax.rem(x + dx, NX)
        part = bf16(term[WIDE:])
        for h in range(NYH):
            half = lax.rem(yh + h, NYH)
            dy = lax.rem(half * NYL + side(own) - y + NY, NY)
            sy[dy, there] = jnp.where(half == 0, part[:, :HALF_CHUNK], part[:, HALF_CHUNK:])
        way = 1 if dx in (1, 2) else 3
        if own:
            far_y[dx] = go.start(sy.at[2, there], y_relay.at[dx], y_peers[way - 1])
        else:
            near_y(4 - way, dx)

    def near_x(dx, own):
        part = rx.at[dx // 2, side(own)]
        by_x.append(go.start(sx.at[dx, side(own)], part, x_peers[dx - 1]))

    def near_y(dy, dx):
        there = lax.rem(x + dx, NX)
        by_y[dy].start(sy.at[dy, there], ry.at[dy // 2, there], y_peers[dy - 1])

    def relay_x(dx, own):
        far_x[own].wait_recv()
        sx[dx, side(own)] = bf16(added([sx[dx, side(own)], x_relay[own]]))
        near_x(dx, own)

    def relay_y(dx):
        dy = 1 if dx in (1, 2) else 3
        there = lax.rem(x + dx, NX)
        far_y[dx].wait_recv()
        sy[dy, there] = bf16(added([sy[dy, there], y_relay[dx]]))
        near_y(dy, dx)

    by_x, far_x, far_y = [], {}, {}
    by_y = {dy: go.group(ry.at[0]) for dy in (1, 3)}
    for o in range(4):
        add_twin(o)
    term = weight_term(core)
    w_twin.wait_recv()
    w_s[...] = bf16(term + f32(w_r0[...]))

    def quarter(i):
        return pl.ds(pl.multiple_of(i * (CHUNK // NX), CHUNK // NX), CHUNK // NX)

    def piece(i):
        return pl.ds(pl.multiple_of(i * PIECE, PIECE), PIECE)

    w_x = go.start_all(
        [
            (w_s.at[quarter(lax.rem(x + dx, NX))], w_rx.at[dx - 1], x_peers[dx - 1])
            for dx in range(1, NX)
        ],
        w_rx,
    )
    add_twin(4)
    add_twin(5)
    add_twin(6)
    add_twin(7)
    relay_x(1, 1)
    relay_x(3, 0)
    for dx in (2, 1, 3, 0):
        relay_y(dx)

    def units(i):
        return pl.ds(pl.multiple_of(i * (F // NZ), F // NZ), F // NZ)

    w_x.wait_recv()
    w_t[...] = added([w_s[quarter(x)]] + [w_rx[i] for i in range(NX - 1)])
    w_y = go.start_all(
        [
            (w_t.at[piece(lax.rem(y + dy, NY))], w_ry.at[dy - 1], y_peers[dy - 1])
            for dy in range(1, NY)
        ],
        w_ry,
    )
    for copy in by_x:
        copy.wait_recv()
    for i in range(NYL):
        for h in range(NYH):
            dy = lax.rem(h * NYL + i - y + NY, NY)
            part = (slice(None), slice(h * HALF_CHUNK, (h + 1) * HALF_CHUNK))
            px[dy] = bf16(added([sx[(0, i) + part]] + [rx[(j, i) + part] for j in range(2)]))
    x_then_y = go.start_all(
        [(px.at[dy], qx.at[dy - 1], y_peers[dy - 1]) for dy in (2, 1, 3)], qx
    )
    for copy in by_y.values():
        copy.wait_recv()
    for i in range(NX):
        dx = lax.rem(i - x + NX, NX)
        py[dx] = bf16(added([sy[0, i]] + [ry[j, i] for j in range(2)]))
    y_then_x = go.start_all(
        [(py.at[dx], qy.at[dx - 1], x_peers[dx - 1]) for dx in (2, 1, 3)], qy
    )
    w_y.wait_recv()
    w_z[z] = bf16(added([w_t[piece(y)]] + [w_ry[i] for i in range(NY - 1)]))
    w_rows = go.start_all([(w_z.at[z], w_z.at[z], z_peers[dz - 1]) for dz in far_first], w_z.at[pl.ds(0, NZ - 1)])

    x_then_y.wait_recv()
    whole[:WIDE] = bf16(added([px[0]] + [qx[i] for i in range(NY - 1)]))
    y_then_x.wait_recv()
    whole[WIDE:] = bf16(added([py[0]] + [qy[i] for i in range(NX - 1)]))
    rows = go.start_all(
        [
            (whole.at[units(lax.rem(z + dz, NZ))], pieces.at[dz - 1], z_peers[dz - 1])
            for dz in far_first
        ],
        pieces,
    )
    w_rows.wait_recv()
    scale = 1.0 / math.sqrt(N_COL * N_ROW * SLOTS * BLOCK)
    w_all[x * NY + y] = bf16(added([w_z[i] for i in range(NZ)]) * scale)
    part = w_all.at[x * NY + y]
    w_plane = go.start_all([(part, part, peer) for peer in plane_peers], w_all.at[pl.ds(0, NX * NY - 1)])
    rows.wait_recv()
    final[yh * NZ + z] = bf16(added([whole[units(z)]] + [pieces[i] for i in range(NZ - 1)]))
    part = final.at[yh * NZ + z]
    everyone = go.start_all([(part, part, peer) for peer in row_peers], final.at[pl.ds(0, N_ROW - 1)])
    w_plane.wait_recv()
    w_back = go.start(w_all, w_other, twin)
    gw_out[lanes(core)] = w_all[...].reshape(CHUNK, F)
    w_back.wait_recv()
    gw_out[lanes(1 - core)] = w_other[...].reshape(CHUNK, F)
    everyone.wait_recv()
    gf_out[...] = final[...].reshape(NYH, F, HALF_CHUNK)
    go.finish()


def reduce(dense, feats, weight, cotangent):
    vmem = pl.BlockSpec(memory_space=pltpu.VMEM)
    hbm = pl.BlockSpec(memory_space=pltpu.HBM)
    rows = (SLAB_DEV, F)

    def buffer(*shape):
        return pltpu.VMEM(shape, jnp.bfloat16)

    def lane(rows, *lead):
        return buffer(*lead, rows, HALF_CHUNK)

    quarter = CHUNK // NX
    return pl.pallas_call(
        reduce_kernel,
        name="reduce",
        out_shape=(
            jax.ShapeDtypeStruct(rows, jnp.bfloat16),
            jax.ShapeDtypeStruct((F, F), jnp.bfloat16),
            jax.ShapeDtypeStruct((NYH, F, HALF_CHUNK), jnp.bfloat16),
        ),
        in_specs=[vmem, vmem, hbm, hbm],
        out_specs=(vmem, vmem, vmem),
        scratch_shapes=[
            buffer(F, F), buffer(*rows), pltpu.VMEM(rows, jnp.float32),
            buffer(*rows), buffer(*rows), buffer(F, SLAB_DEV), pltpu.SemaphoreType.DMA((2,)),
            buffer(8, F, CHUNK), buffer(8, F, CHUNK),
            buffer(NX, NYL, WIDE, CHUNK), buffer(2, NYL, WIDE, CHUNK), buffer(2, WIDE, CHUNK),
            lane(WIDE, NY), lane(WIDE, NY - 1),
            lane(F - WIDE, NY, NX), lane(F - WIDE, 2, NX), lane(F - WIDE, NX),
            lane(F - WIDE, NX), lane(F - WIDE, NX - 1),
            buffer(F, HALF_CHUNK), buffer(NZ - 1, F // NZ, HALF_CHUNK), buffer(N_ROW, F // NZ, HALF_CHUNK),
            buffer(CHUNK, F), buffer(CHUNK, F), buffer(CHUNK, F), buffer(NX - 1, quarter, F),
            pltpu.VMEM((quarter, F), jnp.float32), pltpu.VMEM((NY - 1, PIECE, F), jnp.float32),
            buffer(NZ, PIECE, F), buffer(NX * NY, PIECE, F), buffer(NX * NY, PIECE, F),
            pltpu.SemaphoreType.DMA((REDUCE_COPIES,)),
            pltpu.SemaphoreType.DMA((REDUCE_COPIES,)),
        ],
        compiler_params=pltpu.CompilerParams(
            collective_id=1, has_side_effects=True, vmem_limit_bytes=32 * MIB
        ),
    )(dense, feats, *in_hbm(weight, cotangent))


def finish_kernel(out_in, gw_in, gf_in, out, gw_out, gf_out, gw, gf, sems):
    copies = [pltpu.make_async_copy(out_in, out, sems.at[0])]
    copies[0].start()
    for i in range(2):
        part = pl.ds(i * CHUNK, CHUNK)
        gw[part] = f32(gw_in[part])
        copies.append(pltpu.make_async_copy(gw.at[part], gw_out.at[part], sems.at[1 + i]))
        copies[-1].start()
    for h in range(NYH):
        gf[h * HALF_CHUNK : (h + 1) * HALF_CHUNK] = f32(gf_in[h]).T
    copies.append(pltpu.make_async_copy(gf, gf_out, sems.at[3]))
    copies[-1].start()
    for copy in copies:
        copy.wait()


def finish(output, gw, gf):
    vmem = pl.BlockSpec(memory_space=pltpu.VMEM)
    hbm = pl.BlockSpec(memory_space=pltpu.HBM)
    return pl.pallas_call(
        finish_kernel,
        name="finish",
        out_shape=(
            jax.ShapeDtypeStruct(output.shape, jnp.bfloat16),
            jax.ShapeDtypeStruct(gw.shape, jnp.float32),
            jax.ShapeDtypeStruct((CHUNK, F), jnp.float32),
        ),
        in_specs=[vmem] * 3,
        out_specs=(hbm,) * 3,
        scratch_shapes=[
            pltpu.VMEM(gw.shape, jnp.float32),
            pltpu.VMEM((CHUNK, F), jnp.float32),
            pltpu.SemaphoreType.DMA((4,)),
        ],
        compiler_params=pltpu.CompilerParams(vmem_limit_bytes=8 * MIB),
    )(output, gw, gf)


def body(features, block_values, entry_cols, row_lengths, row_owner, weight, cotangent):
    values = block_values.reshape(E_DEV * BLOCK, BLOCK)
    blocks, feats, cols = gather(values, features, entry_cols.reshape(1, E_DEV))
    blocks = blocks.reshape(N_ROW * E_DEV, BLOCK, BLOCK)
    dense = place_blocks(cols, row_lengths, row_owner, blocks)
    return finish(*reduce(dense, feats.reshape(FEAT_NODES, F), weight, cotangent))


def solution(mesh):
    placed = (
        P("col", None),
        P("col", "row", None, None, None),
        P("col", "row", None),
        P("col", None),
        P("col", None),
        P(),
        P(("col", "row"), None),
    )
    return jax.shard_map(
        body,
        mesh=mesh,
        in_specs=placed,
        out_specs=(P(("col", "row"), None), P(), P("col", None)),
        check_vma=False,
    )
```

```python
import functools
import math

import jax
import jax.numpy as jnp
from jax import lax
from jax.experimental import pallas as pl
from jax.experimental.pallas import tpu as pltpu
from jax.sharding import PartitionSpec as P

F = 512
BLOCK = 128
NX, NYL, NC = 4, 2, 2
NZ, NYH = 8, 2
N_COL = NX * NYL * NC
N_ROW = NZ * NYH
E_DEV = 10
ROWS = 48
SLOTS = ROWS // N_ROW
MAX_LEN = 16
CHUNK = 256
PIECE = CHUNK // N_ROW
SLAB_DEV = SLOTS * BLOCK
FEAT_NODES = N_COL * CHUNK
MESH = pl.DeviceIdType.MESH
HALF = E_DEV * BLOCK // 2
OVER = 768
WIDE = 208
NY = NYL * NYH
MIB = 1 << 20


def place():
    col, row = lax.axis_index("col"), lax.axis_index("row")
    core = lax.rem(col, NC)
    yl = lax.rem(col // NC, NYL)
    x = col // (NC * NYL)
    z = row // NYH
    yh = lax.rem(row, NYH)
    return col, row, x, yl, core, z, yh


def col_of(x, yl, core):
    return (lax.rem(x + NX, NX) * NYL + yl) * NC + core


def row_of(z, yh):
    return lax.rem(z + NZ, NZ) * NYH + yh


def greet(peers, meanwhile=None):
    barrier = pltpu.get_barrier_semaphore()
    for peer in peers:
        pl.semaphore_signal(barrier, inc=1, device_id=peer, device_id_type=MESH)
    if meanwhile is not None:
        meanwhile()
    pl.semaphore_wait(barrier, len(peers))


def in_hbm(*arrays):
    return [pltpu.with_memory_space_constraint(array, pltpu.HBM) for array in arrays]


class Copies:
    def __init__(self, send, recv):
        self.send, self.recv, self.count, self.all = send, recv, 0, []

    def start(self, src, dst, peer):
        copy = pltpu.make_async_remote_copy(
            src_ref=src,
            dst_ref=dst,
            send_sem=self.send.at[self.count],
            recv_sem=self.recv.at[self.count],
            device_id=peer,
            device_id_type=MESH,
        )
        copy.start()
        self.count += 1
        self.all.append(copy)
        return copy

    def group(self, received):
        group = Group(self.send.at[self.count], self.recv.at[self.count], received)
        self.count += 1
        self.all.append(group)
        return group

    def start_all(self, copies, received):
        group = self.group(received)
        for copy in copies:
            group.start(*copy)
        return group

    def finish(self):
        for copy in self.all:
            copy.wait_send()


class Group:
    def __init__(self, send, recv, received):
        self.send, self.recv, self.received, self.peer = send, recv, received, None

    def copy(self, src, dst, peer):
        return pltpu.make_async_remote_copy(
            src_ref=src,
            dst_ref=dst,
            send_sem=self.send,
            recv_sem=self.recv,
            device_id=peer,
            device_id_type=MESH,
        )

    def start(self, src, dst, peer):
        self.peer = peer
        self.copy(src, dst, peer).start()

    def wait_recv(self):
        self.copy(self.received, self.received, self.peer).wait_recv()

    def wait_send(self):
        self.copy(self.received, self.received, self.peer).wait_send()


GATHER_COPIES = 64


def gather_kernel(
    a_in, f_in, c_in, g_out, f_out, c_out, c_raw, c_pad, c_all, send, recv, local
):
    col, row, x, yl, core, z, yh = place()
    up, down = (col, row_of(z + 1, yh)), (col, row_of(z - 1, yh))
    across = (col, row_of(z, 1 - yh))
    right, left = (col_of(x + 1, yl, core), row), (col_of(x - 1, yl, core), row)
    beside = [(col_of(x, 1 - yl, core), row_of(z, h)) for h in (yh, 1 - yh)]
    twin = (col_of(x, yl, 1 - core), row)
    others = [(col, lax.rem(row + d, N_ROW)) for d in range(1, N_ROW)]

    own = [
        pltpu.make_async_copy(a_in, g_out.at[row], local.at[0]),
        pltpu.make_async_copy(f_in, f_out.at[col], local.at[1]),
    ]

    def columns():
        load = pltpu.make_async_copy(c_in, c_raw, local.at[2])
        load.start()
        for copy in own:
            copy.start()
        load.wait()
        c_pad[...] = jnp.zeros_like(c_pad)
        c_pad[:, 0:E_DEV] = c_raw[...]

    greet(others + beside + [right, left, twin], columns)
    go = Copies(send, recv)

    low, high = pl.ds(0, OVER), pl.ds(OVER, E_DEV * BLOCK - OVER)
    own_low = (a_in.at[low], g_out.at[row, low])
    own_high = (a_in.at[high], g_out.at[row, high])
    ways = ((1, up), (-1, down))
    got = {("a", 0, way): [go.start(*own_low, peer)] for way, peer in ways}
    cross = go.start(*own_high, across)
    f_beside = []
    for i, peer in enumerate(beside):
        half = pl.ds(i * (CHUNK // 2), CHUNK // 2)
        f_beside.append(go.start(f_in.at[half], f_out.at[col, half], peer))
    f_right = go.start(f_in, f_out.at[col], right)
    f_left = go.start(f_in, f_out.at[col], left)
    got.update({("b", 0, way): [go.start(*own_high, peer)] for way, peer in ways})
    over = [go.start(*own_low, across)]
    twins = [go.start(f_in, f_out.at[col], twin)]
    own.append(pltpu.make_async_copy(c_pad, c_out.at[row], local.at[3]))
    own[-1].start()
    cols = go.start_all([(c_pad, c_out.at[row], peer) for peer in others], c_all)

    def rows_of(stream, t, way):
        if t < 3:
            return [low if stream == "a" else high]
        if stream != "c":
            first, last = (0, OVER) if stream == "a" else (OVER, E_DEV * BLOCK)
            first, last = (first, min(last, HALF)) if way == 1 else (max(first, HALF), last)
            cuts = [first, (first + last) // 2, last] if stream == "a" and way == 1 else [first, last]
            return [pl.ds(i, j - i) for i, j in zip(cuts, cuts[1:]) if i < j]
        size = (E_DEV * BLOCK - OVER) // 2
        return [pl.ds(OVER if way == 1 else OVER + size, size)]

    def arrived(stream, t, way):
        for copy, rows in zip(got[stream, t, way], rows_of(stream, t, way)):
            copy.wait_recv()
            if stream == "a":
                part = g_out.at[row_of(z - way * (t + 1), yh), rows]
                over.append(go.start(part, part, across))

    def pass_on(stream, t):
        y = 1 - yh if stream == "c" else yh
        for way, peer in ways:
            if t and stream == "a":
                got[stream, t - 1, way][0].wait_recv()
            elif t:
                arrived(stream, t - 1, way)
            parts = [g_out.at[row_of(z - way * t, y), rows] for rows in rows_of(stream, t, way)]
            got[stream, t, way] = [go.start(part, part, peer) for part in parts]
            if t and stream == "a":
                arrived_low = g_out.at[row_of(z - way * t, y), low]
                over.append(go.start(arrived_low, arrived_low, across))

    def chunk(dx, y):
        return f_out.at[col_of(x + dx, y, core)]

    for copy in f_beside:
        copy.wait_recv()
    part = chunk(0, 1 - yl)
    f_right2 = go.start(part, part, right)
    f_left2 = go.start(part, part, left)
    twins.append(go.start(part, part, twin))
    cross.wait_recv()
    pass_on("c", 0)
    pass_on("a", 1)
    f_right.wait_recv()
    part = chunk(-1, yl)
    far_right = go.start(part, part, right)
    twins.append(go.start(part, part, twin))
    f_left.wait_recv()
    part = chunk(1, yl)
    twins.append(go.start(part, part, twin))
    pass_on("c", 1)
    pass_on("b", 1)
    f_left2.wait_recv()
    part = chunk(1, 1 - yl)
    far_left = go.start(part, part, left)
    twins.append(go.start(part, part, twin))
    f_right2.wait_recv()
    part = chunk(-1, 1 - yl)
    twins.append(go.start(part, part, twin))
    pass_on("a", 2)
    pass_on("c", 2)
    pass_on("b", 2)
    far_right.wait_recv()
    part = chunk(2, yl)
    twins.append(go.start(part, part, twin))
    far_left.wait_recv()
    part = chunk(2, 1 - yl)
    twins.append(go.start(part, part, twin))
    pass_on("a", 3)
    pass_on("b", 3)
    pass_on("c", 3)
    cols.wait_recv()
    for copy in twins:
        copy.wait_recv()
    for stream in ("a", "b", "c"):
        for way in (1, -1):
            arrived(stream, 3, way)
    for copy in over:
        copy.wait_recv()
    for copy in own:
        copy.wait()
    go.finish()


def gather(values, features, columns):
    any_space = pl.BlockSpec(memory_space=pl.ANY)
    hbm = pl.BlockSpec(memory_space=pltpu.HBM)
    return pl.pallas_call(
        gather_kernel,
        name="gather",
        out_shape=(
            jax.ShapeDtypeStruct((N_ROW, E_DEV * BLOCK, BLOCK), jnp.bfloat16),
            jax.ShapeDtypeStruct((N_COL, CHUNK, F), jnp.bfloat16),
            jax.ShapeDtypeStruct((N_ROW, 1, 128), jnp.int32),
        ),
        in_specs=[hbm, hbm, hbm],
        out_specs=(any_space, any_space, any_space),
        scratch_shapes=[
            pltpu.VMEM((1, E_DEV), jnp.int32),
            pltpu.VMEM((1, 128), jnp.int32),
            pltpu.VMEM((N_ROW - 1, 1, 128), jnp.int32),
            pltpu.SemaphoreType.DMA((GATHER_COPIES,)),
            pltpu.SemaphoreType.DMA((GATHER_COPIES,)),
            pltpu.SemaphoreType.DMA((4,)),
        ],
        compiler_params=pltpu.CompilerParams(
            collective_id=0, has_side_effects=True, vmem_limit_bytes=4 * MIB
        ),
    )(*in_hbm(values, features, columns))


def place_kernel(cols_in, len_in, own_in, blocks, dense, cols, lengths, owners, first, sums, sems):
    row = lax.axis_index("row")
    small = [
        pltpu.make_async_copy(len_in, lengths, sems.at[0]),
        pltpu.make_async_copy(own_in, owners, sems.at[1]),
        pltpu.make_async_copy(cols_in, cols, sems.at[2]),
    ]
    for copy in small:
        copy.start()
    dense[...] = jnp.zeros_like(dense)
    for copy in small:
        copy.wait()

    def find(q, state):
        begin, starts, sizes = state
        length = lengths[0, q]
        which = owners[0, q] - row * SLOTS
        starts = tuple(jnp.where(which == s, begin, v) for s, v in enumerate(starts))
        sizes = tuple(jnp.where(which == s, length, v) for s, v in enumerate(sizes))
        return begin + length, starts, sizes

    nought = jnp.int32(0)
    _, starts, sizes = lax.fori_loop(0, ROWS, find, (nought, (nought,) * SLOTS, (nought,) * SLOTS))
    for s in range(SLOTS):

        @pl.loop(0, FEAT_NODES // BLOCK)
        def _(j):
            first[s, j] = -1

        @pl.loop(0, sizes[s])
        def _(k):
            g = starts[s] + k
            j = cols[g // E_DEV, 0, lax.rem(g, E_DEV)]
            spot = (pl.ds(s * BLOCK, BLOCK), pl.ds(pl.multiple_of(j * BLOCK, BLOCK), BLOCK))
            seen = first[s, j]

            @pl.when(seen < 0)
            def _():
                first[s, j] = k
                sums[k] = f32(blocks[g])
                dense[spot] = blocks[g]

            @pl.when(seen >= 0)
            def _():
                total = sums[seen] + f32(blocks[g])
                sums[seen] = total
                dense[spot] = bf16(total)


def place_blocks(cols, lengths, owners, blocks):
    any_space = pl.BlockSpec(memory_space=pl.ANY)
    vmem = pl.BlockSpec(memory_space=pltpu.VMEM)
    hbm = pl.BlockSpec(memory_space=pltpu.HBM)
    return pl.pallas_call(
        place_kernel,
        name="place",
        out_shape=jax.ShapeDtypeStruct((SLAB_DEV, FEAT_NODES), jnp.bfloat16),
        in_specs=[any_space, hbm, hbm, vmem],
        out_specs=vmem,
        scratch_shapes=[
            pltpu.SMEM((N_ROW, 1, 128), jnp.int32),
            pltpu.SMEM((1, ROWS), jnp.int32),
            pltpu.SMEM((1, ROWS), jnp.int32),
            pltpu.SMEM((SLOTS, FEAT_NODES // BLOCK), jnp.int32),
            pltpu.VMEM((MAX_LEN, BLOCK, BLOCK), jnp.float32),
            pltpu.SemaphoreType.DMA((3,)),
        ],
        compiler_params=pltpu.CompilerParams(vmem_limit_bytes=24 * MIB),
    )(cols, *in_hbm(lengths, owners), blocks)


REDUCE_COPIES = 40
A_SCALE = math.sqrt(2.0 / math.pi)
CUBE = 0.044715


def f32(value):
    return value.astype(jnp.float32)


def bf16(value):
    return value.astype(jnp.bfloat16)


def added(terms):
    total = f32(terms[0])
    for term in terms[1:]:
        total = total + f32(term)
    return total


OVER_ROWS = (((0,), (0,)), ((), ()))
HALF_CHUNK = CHUNK // 2
ORDER = ((2, 1), (2, 0), (1, 1), (3, 1), (0, 1), (1, 0), (3, 0), (0, 0))


def layer(dense, feats, weight, cot, out, acc, hid, gpre, ghid, get_weight, get_cot):
    wide = FEAT_NODES // 4
    acc[...] = jnp.zeros_like(acc)

    @pl.loop(0, 4)
    def _(i):
        part = pl.ds(pl.multiple_of(i * wide, wide), wide)
        acc[...] += jnp.dot(dense[:, part], feats[part], preferred_element_type=jnp.float32)

    hid[...] = acc[...].astype(jnp.bfloat16)
    get_weight.wait()
    acc[...] = jnp.dot(hid[...], weight[...], preferred_element_type=jnp.float32)
    get_cot.wait()

    @pl.loop(0, SLAB_DEV // 32)
    def _(i):
        part = pl.ds(pl.multiple_of(i * 32, 32), 32)
        v = acc[part]
        square = v * v
        t = jnp.tanh(A_SCALE * (v + CUBE * (v * square)))
        cdf = 0.5 * (1.0 + t)
        out[part] = (v * cdf).astype(jnp.bfloat16)
        slope = cdf + 0.5 * v * (1.0 - t * t) * (A_SCALE * (1.0 + 3.0 * CUBE * square))
        gpre[part] = (cot[part].astype(jnp.float32) * slope).astype(jnp.bfloat16)

    ghid[...] = lax.dot_general(
        weight[...], gpre[...], (((1,), (1,)), ((), ())), preferred_element_type=jnp.float32
    ).astype(jnp.bfloat16)


def reduce_kernel(
    dense, feats, w_in, cot_in, out, gw_out, gf_out,
    weight, cot, acc, hid, gpre, ghid, local,
    p0, r0, sx, rx, x_relay, px, qx, sy, ry, y_relay, py, qy, whole, pieces, final,
    w_p0, w_r0, w_s, w_rx, w_t, w_ry, w_z, w_all, w_other, send, recv,
):
    col, row, x, yl, core, z, yh = place()
    y = yh * NYL + yl
    twin = (col_of(x, yl, 1 - core), row)

    def at_y(dx, dy):
        there = lax.rem(y + dy, NY)
        return (col_of(x + dx, lax.rem(there, NYL), core), row_of(z, there // NYL))

    x_peers = [at_y(dx, 0) for dx in range(1, NX)]
    y_peers = [at_y(0, dy) for dy in range(1, NY)]
    z_peers = [(col, row_of(z + dz, yh)) for dz in range(1, NZ)]
    plane_peers = [at_y(dx, dy) for dx in (2, 1, 3, 0) for dy in (2, 1, 3, 0) if dx or dy]
    far_first = (4, 3, 5, 2, 6, 1, 7)
    row_peers = [(col, row_of(z + dz, h)) for dz in far_first for h in (1 - yh, yh)]
    row_peers.append((col, row_of(z, 1 - yh)))
    far_rows = [(col, row_of(z + dz, 1 - yh)) for dz in range(1, NZ)]
    go = Copies(send, recv)

    def lanes(i):
        return pl.ds(pl.multiple_of(i * CHUNK, CHUNK), CHUNK)

    def weight_term(c):
        return lax.dot_general(
            hid[:, lanes(c)], gpre[...], OVER_ROWS, preferred_element_type=jnp.float32
        )

    def side(own):
        return yl if own else 1 - yl

    def feature_term(o, c):
        dx, own = ORDER[o]
        nodes = lanes(col_of(x + dx, side(own), c))
        return jnp.dot(ghid[...], dense[:, nodes], preferred_element_type=jnp.float32)

    get_weight = pltpu.make_async_copy(w_in, weight, local.at[0])
    get_cot = pltpu.make_async_copy(cot_in, cot, local.at[1])
    get_weight.start()
    get_cot.start()

    def first():
        layer(dense, feats, weight, cot, out, acc, hid, gpre, ghid, get_weight, get_cot)
        for o in range(8):
            p0[o] = bf16(feature_term(o, 1 - core))
        w_p0[...] = bf16(weight_term(1 - core))

    greet(plane_peers + z_peers + far_rows + [twin], first)

    twins = [go.start(p0.at[o], r0.at[o], twin) for o in range(2)]
    w_twin = go.start(w_p0, w_r0, twin)
    twins += [go.start(p0.at[o], r0.at[o], twin) for o in range(2, 8)]

    def to_twin(o):
        p0[o] = bf16(feature_term(o, 1 - core))
        twins.append(go.start(p0.at[o], r0.at[o], twin))

    def add_twin(o):
        dx, own = ORDER[o]
        term = feature_term(o, core)
        twins[o].wait_recv()
        term = term + f32(r0[o])
        sx[dx, side(own)] = bf16(term[:WIDE])
        if dx == 2:
            far_x[own] = go.start(sx.at[2, side(own)], x_relay.at[own], x_peers[0 if own else 2])
        elif (dx, own) in ((3, 1), (1, 0)):
            near_x(dx, own)
        there = lax.rem(x + dx, NX)
        part = bf16(term[WIDE:])
        for h in range(NYH):
            half = lax.rem(yh + h, NYH)
            dy = lax.rem(half * NYL + side(own) - y + NY, NY)
            sy[dy, there] = jnp.where(half == 0, part[:, :HALF_CHUNK], part[:, HALF_CHUNK:])
        way = 1 if dx in (1, 2) else 3
        if own:
            far_y[dx] = go.start(sy.at[2, there], y_relay.at[dx], y_peers[way - 1])
        else:
            near_y(4 - way, dx)

    def near_x(dx, own):
        part = rx.at[dx // 2, side(own)]
        by_x.append(go.start(sx.at[dx, side(own)], part, x_peers[dx - 1]))

    def near_y(dy, dx):
        there = lax.rem(x + dx, NX)
        by_y[dy].start(sy.at[dy, there], ry.at[dy // 2, there], y_peers[dy - 1])

    def relay_x(dx, own):
        far_x[own].wait_recv()
        sx[dx, side(own)] = bf16(added([sx[dx, side(own)], x_relay[own]]))
        near_x(dx, own)

    def relay_y(dx):
        dy = 1 if dx in (1, 2) else 3
        there = lax.rem(x + dx, NX)
        far_y[dx].wait_recv()
        sy[dy, there] = bf16(added([sy[dy, there], y_relay[dx]]))
        near_y(dy, dx)

    by_x, far_x, far_y = [], {}, {}
    by_y = {dy: go.group(ry.at[0]) for dy in (1, 3)}
    for o in range(4):
        add_twin(o)
    term = weight_term(core)
    w_twin.wait_recv()
    w_s[...] = bf16(term + f32(w_r0[...]))

    def quarter(i):
        return pl.ds(pl.multiple_of(i * (CHUNK // NX), CHUNK // NX), CHUNK // NX)

    def piece(i):
        return pl.ds(pl.multiple_of(i * PIECE, PIECE), PIECE)

    w_x = go.start_all(
        [
            (w_s.at[quarter(lax.rem(x + dx, NX))], w_rx.at[dx - 1], x_peers[dx - 1])
            for dx in range(1, NX)
        ],
        w_rx,
    )
    add_twin(4)
    add_twin(5)
    add_twin(6)
    add_twin(7)
    relay_x(1, 1)
    relay_x(3, 0)
    for dx in (2, 1, 3, 0):
        relay_y(dx)

    def units(i):
        return pl.ds(pl.multiple_of(i * (F // NZ), F // NZ), F // NZ)

    w_x.wait_recv()
    w_t[...] = added([w_s[quarter(x)]] + [w_rx[i] for i in range(NX - 1)])
    w_y = go.start_all(
        [
            (w_t.at[piece(lax.rem(y + dy, NY))], w_ry.at[dy - 1], y_peers[dy - 1])
            for dy in range(1, NY)
        ],
        w_ry,
    )
    for copy in by_x:
        copy.wait_recv()
    for i in range(NYL):
        for h in range(NYH):
            dy = lax.rem(h * NYL + i - y + NY, NY)
            part = (slice(None), slice(h * HALF_CHUNK, (h + 1) * HALF_CHUNK))
            px[dy] = bf16(added([sx[(0, i) + part]] + [rx[(j, i) + part] for j in range(2)]))
    x_then_y = go.start_all(
        [(px.at[dy], qx.at[dy - 1], y_peers[dy - 1]) for dy in (2, 1, 3)], qx
    )
    for copy in by_y.values():
        copy.wait_recv()
    for i in range(NX):
        dx = lax.rem(i - x + NX, NX)
        py[dx] = bf16(added([sy[0, i]] + [ry[j, i] for j in range(2)]))
    y_then_x = go.start_all(
        [(py.at[dx], qy.at[dx - 1], x_peers[dx - 1]) for dx in (2, 1, 3)], qy
    )
    w_y.wait_recv()
    w_z[z] = bf16(added([w_t[piece(y)]] + [w_ry[i] for i in range(NY - 1)]))
    w_rows = go.start_all([(w_z.at[z], w_z.at[z], z_peers[dz - 1]) for dz in far_first], w_z.at[pl.ds(0, NZ - 1)])

    x_then_y.wait_recv()
    whole[:WIDE] = bf16(added([px[0]] + [qx[i] for i in range(NY - 1)]))
    y_then_x.wait_recv()
    whole[WIDE:] = bf16(added([py[0]] + [qy[i] for i in range(NX - 1)]))
    rows = go.start_all(
        [
            (whole.at[units(lax.rem(z + dz, NZ))], pieces.at[dz - 1], z_peers[dz - 1])
            for dz in far_first
        ],
        pieces,
    )
    w_rows.wait_recv()
    scale = 1.0 / math.sqrt(N_COL * N_ROW * SLOTS * BLOCK)
    w_all[x * NY + y] = bf16(added([w_z[i] for i in range(NZ)]) * scale)
    part = w_all.at[x * NY + y]
    w_plane = go.start_all([(part, part, peer) for peer in plane_peers], w_all.at[pl.ds(0, NX * NY - 1)])
    rows.wait_recv()
    final[yh * NZ + z] = bf16(added([whole[units(z)]] + [pieces[i] for i in range(NZ - 1)]))
    part = final.at[yh * NZ + z]
    everyone = go.start_all([(part, part, peer) for peer in row_peers], final.at[pl.ds(0, N_ROW - 1)])
    w_plane.wait_recv()
    w_back = go.start(w_all, w_other, twin)
    gw_out[lanes(core)] = w_all[...].reshape(CHUNK, F)
    w_back.wait_recv()
    gw_out[lanes(1 - core)] = w_other[...].reshape(CHUNK, F)
    everyone.wait_recv()
    gf_out[...] = final[...].reshape(NYH, F, HALF_CHUNK)
    go.finish()


def reduce(dense, feats, weight, cotangent):
    vmem = pl.BlockSpec(memory_space=pltpu.VMEM)
    hbm = pl.BlockSpec(memory_space=pltpu.HBM)
    rows = (SLAB_DEV, F)

    def buffer(*shape):
        return pltpu.VMEM(shape, jnp.bfloat16)

    def lane(rows, *lead):
        return buffer(*lead, rows, HALF_CHUNK)

    quarter = CHUNK // NX
    return pl.pallas_call(
        reduce_kernel,
        name="reduce",
        out_shape=(
            jax.ShapeDtypeStruct(rows, jnp.bfloat16),
            jax.ShapeDtypeStruct((F, F), jnp.bfloat16),
            jax.ShapeDtypeStruct((NYH, F, HALF_CHUNK), jnp.bfloat16),
        ),
        in_specs=[vmem, vmem, hbm, hbm],
        out_specs=(vmem, vmem, vmem),
        scratch_shapes=[
            buffer(F, F), buffer(*rows), pltpu.VMEM(rows, jnp.float32),
            buffer(*rows), buffer(*rows), buffer(F, SLAB_DEV), pltpu.SemaphoreType.DMA((2,)),
            buffer(8, F, CHUNK), buffer(8, F, CHUNK),
            buffer(NX, NYL, WIDE, CHUNK), buffer(2, NYL, WIDE, CHUNK), buffer(2, WIDE, CHUNK),
            lane(WIDE, NY), lane(WIDE, NY - 1),
            lane(F - WIDE, NY, NX), lane(F - WIDE, 2, NX), lane(F - WIDE, NX),
            lane(F - WIDE, NX), lane(F - WIDE, NX - 1),
            buffer(F, HALF_CHUNK), buffer(NZ - 1, F // NZ, HALF_CHUNK), buffer(N_ROW, F // NZ, HALF_CHUNK),
            buffer(CHUNK, F), buffer(CHUNK, F), buffer(CHUNK, F), buffer(NX - 1, quarter, F),
            pltpu.VMEM((quarter, F), jnp.float32), pltpu.VMEM((NY - 1, PIECE, F), jnp.float32),
            buffer(NZ, PIECE, F), buffer(NX * NY, PIECE, F), buffer(NX * NY, PIECE, F),
            pltpu.SemaphoreType.DMA((REDUCE_COPIES,)),
            pltpu.SemaphoreType.DMA((REDUCE_COPIES,)),
        ],
        compiler_params=pltpu.CompilerParams(
            collective_id=1, has_side_effects=True, vmem_limit_bytes=32 * MIB
        ),
    )(dense, feats, *in_hbm(weight, cotangent))


def finish_kernel(out_in, gw_in, gf_in, out, gw_out, gf_out, gw, gf, sems):
    copies = [pltpu.make_async_copy(out_in, out, sems.at[0])]
    copies[0].start()
    for i in range(2):
        part = pl.ds(i * CHUNK, CHUNK)
        gw[part] = f32(gw_in[part])
        copies.append(pltpu.make_async_copy(gw.at[part], gw_out.at[part], sems.at[1 + i]))
        copies[-1].start()
    for h in range(NYH):
        gf[h * HALF_CHUNK : (h + 1) * HALF_CHUNK] = f32(gf_in[h]).T
    copies.append(pltpu.make_async_copy(gf, gf_out, sems.at[3]))
    copies[-1].start()
    for copy in copies:
        copy.wait()


def finish(output, gw, gf):
    vmem = pl.BlockSpec(memory_space=pltpu.VMEM)
    hbm = pl.BlockSpec(memory_space=pltpu.HBM)
    return pl.pallas_call(
        finish_kernel,
        name="finish",
        out_shape=(
            jax.ShapeDtypeStruct(output.shape, jnp.bfloat16),
            jax.ShapeDtypeStruct(gw.shape, jnp.float32),
            jax.ShapeDtypeStruct((CHUNK, F), jnp.float32),
        ),
        in_specs=[vmem] * 3,
        out_specs=(hbm,) * 3,
        scratch_shapes=[
            pltpu.VMEM(gw.shape, jnp.float32),
            pltpu.VMEM((CHUNK, F), jnp.float32),
            pltpu.SemaphoreType.DMA((4,)),
        ],
        compiler_params=pltpu.CompilerParams(vmem_limit_bytes=8 * MIB),
    )(output, gw, gf)


def body(features, block_values, entry_cols, row_lengths, row_owner, weight, cotangent):
    values = block_values.reshape(E_DEV * BLOCK, BLOCK)
    blocks, feats, cols = gather(values, features, entry_cols.reshape(1, E_DEV))
    blocks = blocks.reshape(N_ROW * E_DEV, BLOCK, BLOCK)
    dense = place_blocks(cols, row_lengths, row_owner, blocks)
    return finish(*reduce(dense, feats.reshape(FEAT_NODES, F), weight, cotangent))


def solution(mesh):
    placed = (
        P("col", None),
        P("col", "row", None, None, None),
        P("col", "row", None),
        P("col", None),
        P("col", None),
        P(),
        P(("col", "row"), None),
    )
    return jax.shard_map(
        body,
        mesh=mesh,
        in_specs=placed,
        out_specs=(P(("col", "row"), None), P(), P("col", None)),
        check_vma=False,
    )
```

```python
import functools
import math

import jax
import jax.numpy as jnp
from jax import lax
from jax.experimental import pallas as pl
from jax.experimental.pallas import tpu as pltpu
from jax.sharding import PartitionSpec as P

F = 512
BLOCK = 128
NX, NYL, NC = 4, 2, 2
NZ, NYH = 8, 2
N_COL = NX * NYL * NC
N_ROW = NZ * NYH
E_DEV = 10
ROWS = 48
SLOTS = ROWS // N_ROW
MAX_LEN = 16
CHUNK = 256
PIECE = CHUNK // N_ROW
SLAB_DEV = SLOTS * BLOCK
FEAT_NODES = N_COL * CHUNK
MESH = pl.DeviceIdType.MESH
HALF = E_DEV * BLOCK // 2
OVER = 768
WIDE = 208
NY = NYL * NYH
MIB = 1 << 20


def place():
    col, row = lax.axis_index("col"), lax.axis_index("row")
    core = lax.rem(col, NC)
    yl = lax.rem(col // NC, NYL)
    x = col // (NC * NYL)
    z = row // NYH
    yh = lax.rem(row, NYH)
    return col, row, x, yl, core, z, yh


def col_of(x, yl, core):
    return (lax.rem(x + NX, NX) * NYL + yl) * NC + core


def row_of(z, yh):
    return lax.rem(z + NZ, NZ) * NYH + yh


def greet(peers, meanwhile=None):
    barrier = pltpu.get_barrier_semaphore()
    for peer in peers:
        pl.semaphore_signal(barrier, inc=1, device_id=peer, device_id_type=MESH)
    if meanwhile is not None:
        meanwhile()
    pl.semaphore_wait(barrier, len(peers))


def in_hbm(*arrays):
    return [pltpu.with_memory_space_constraint(array, pltpu.HBM) for array in arrays]


class Copies:
    def __init__(self, send, recv):
        self.send, self.recv, self.count, self.all = send, recv, 0, []

    def start(self, src, dst, peer):
        copy = pltpu.make_async_remote_copy(
            src_ref=src,
            dst_ref=dst,
            send_sem=self.send.at[self.count],
            recv_sem=self.recv.at[self.count],
            device_id=peer,
            device_id_type=MESH,
        )
        copy.start()
        self.count += 1
        self.all.append(copy)
        return copy

    def group(self, received):
        group = Group(self.send.at[self.count], self.recv.at[self.count], received)
        self.count += 1
        self.all.append(group)
        return group

    def start_all(self, copies, received):
        group = self.group(received)
        for copy in copies:
            group.start(*copy)
        return group

    def finish(self, first=None):
        for copy in self.all[:first]:
            copy.wait_send()
        del self.all[:first]


class Group:
    def __init__(self, send, recv, received):
        self.send, self.recv, self.received, self.peer = send, recv, received, None

    def copy(self, src, dst, peer):
        return pltpu.make_async_remote_copy(
            src_ref=src,
            dst_ref=dst,
            send_sem=self.send,
            recv_sem=self.recv,
            device_id=peer,
            device_id_type=MESH,
        )

    def start(self, src, dst, peer):
        self.peer = peer
        self.copy(src, dst, peer).start()

    def wait_recv(self):
        self.copy(self.received, self.received, self.peer).wait_recv()

    def wait_send(self):
        self.copy(self.received, self.received, self.peer).wait_send()


GATHER_COPIES = 64


def gather_kernel(
    a_in, f_in, c_in, g_out, f_out, c_out, c_raw, c_pad, c_all, send, recv, local
):
    col, row, x, yl, core, z, yh = place()
    up, down = (col, row_of(z + 1, yh)), (col, row_of(z - 1, yh))
    across = (col, row_of(z, 1 - yh))
    right, left = (col_of(x + 1, yl, core), row), (col_of(x - 1, yl, core), row)
    beside = [(col_of(x, 1 - yl, core), row_of(z, h)) for h in (yh, 1 - yh)]
    twin = (col_of(x, yl, 1 - core), row)
    others = [(col, lax.rem(row + d, N_ROW)) for d in range(1, N_ROW)]

    own = [
        pltpu.make_async_copy(a_in, g_out.at[row], local.at[0]),
        pltpu.make_async_copy(f_in, f_out.at[col], local.at[1]),
    ]

    def columns():
        load = pltpu.make_async_copy(c_in, c_raw, local.at[2])
        load.start()
        for copy in own:
            copy.start()
        load.wait()
        c_pad[...] = jnp.zeros_like(c_pad)
        c_pad[:, 0:E_DEV] = c_raw[...]

    greet(others + beside + [right, left, twin], columns)
    go = Copies(send, recv)

    low, high = pl.ds(0, OVER), pl.ds(OVER, E_DEV * BLOCK - OVER)
    own_low = (a_in.at[low], g_out.at[row, low])
    own_high = (a_in.at[high], g_out.at[row, high])
    ways = ((1, up), (-1, down))
    got = {("a", 0, way): [go.start(*own_low, peer)] for way, peer in ways}
    cross = go.start(*own_high, across)
    f_beside = []
    for i, peer in enumerate(beside):
        half = pl.ds(i * (CHUNK // 2), CHUNK // 2)
        f_beside.append(go.start(f_in.at[half], f_out.at[col, half], peer))
    f_right = go.start(f_in, f_out.at[col], right)
    f_left = go.start(f_in, f_out.at[col], left)
    got.update({("b", 0, way): [go.start(*own_high, peer)] for way, peer in ways})
    over = [go.start(*own_low, across)]
    twins = [go.start(f_in, f_out.at[col], twin)]
    own.append(pltpu.make_async_copy(c_pad, c_out.at[row], local.at[3]))
    own[-1].start()
    cols = go.start_all([(c_pad, c_out.at[row], peer) for peer in others], c_all)

    def rows_of(stream, t, way):
        if t < 3:
            return [low if stream == "a" else high]
        if stream != "c":
            first, last = (0, OVER) if stream == "a" else (OVER, E_DEV * BLOCK)
            first, last = (first, min(last, HALF)) if way == 1 else (max(first, HALF), last)
            cuts = [first, (first + last) // 2, last] if stream == "a" and way == 1 else [first, last]
            return [pl.ds(i, j - i) for i, j in zip(cuts, cuts[1:]) if i < j]
        size = (E_DEV * BLOCK - OVER) // 2
        return [pl.ds(OVER if way == 1 else OVER + size, size)]

    def arrived(stream, t, way):
        for copy, rows in zip(got[stream, t, way], rows_of(stream, t, way)):
            copy.wait_recv()
            if stream == "a":
                part = g_out.at[row_of(z - way * (t + 1), yh), rows]
                over.append(go.start(part, part, across))

    def pass_on(stream, t):
        y = 1 - yh if stream == "c" else yh
        for way, peer in ways:
            if t and stream == "a":
                got[stream, t - 1, way][0].wait_recv()
            elif t:
                arrived(stream, t - 1, way)
            parts = [g_out.at[row_of(z - way * t, y), rows] for rows in rows_of(stream, t, way)]
            got[stream, t, way] = [go.start(part, part, peer) for part in parts]
            if t and stream == "a":
                arrived_low = g_out.at[row_of(z - way * t, y), low]
                over.append(go.start(arrived_low, arrived_low, across))

    def chunk(dx, y):
        return f_out.at[col_of(x + dx, y, core)]

    for copy in f_beside:
        copy.wait_recv()
    part = chunk(0, 1 - yl)
    f_right2 = go.start(part, part, right)
    f_left2 = go.start(part, part, left)
    twins.append(go.start(part, part, twin))
    cross.wait_recv()
    pass_on("c", 0)
    pass_on("a", 1)
    f_right.wait_recv()
    part = chunk(-1, yl)
    far_right = go.start(part, part, right)
    twins.append(go.start(part, part, twin))
    f_left.wait_recv()
    part = chunk(1, yl)
    twins.append(go.start(part, part, twin))
    pass_on("c", 1)
    pass_on("b", 1)
    f_left2.wait_recv()
    part = chunk(1, 1 - yl)
    far_left = go.start(part, part, left)
    twins.append(go.start(part, part, twin))
    f_right2.wait_recv()
    part = chunk(-1, 1 - yl)
    twins.append(go.start(part, part, twin))
    early = len(go.all)
    pass_on("a", 2)
    pass_on("c", 2)
    pass_on("b", 2)
    far_right.wait_recv()
    part = chunk(2, yl)
    twins.append(go.start(part, part, twin))
    far_left.wait_recv()
    part = chunk(2, 1 - yl)
    twins.append(go.start(part, part, twin))
    pass_on("a", 3)
    pass_on("b", 3)
    pass_on("c", 3)
    go.finish(early)
    cols.wait_recv()
    for copy in twins:
        copy.wait_recv()
    for stream in ("a", "b", "c"):
        for way in (1, -1):
            arrived(stream, 3, way)
    for copy in over:
        copy.wait_recv()
    for copy in own:
        copy.wait()
    go.finish()


def gather(values, features, columns):
    any_space = pl.BlockSpec(memory_space=pl.ANY)
    hbm = pl.BlockSpec(memory_space=pltpu.HBM)
    return pl.pallas_call(
        gather_kernel,
        name="gather",
        out_shape=(
            jax.ShapeDtypeStruct((N_ROW, E_DEV * BLOCK, BLOCK), jnp.bfloat16),
            jax.ShapeDtypeStruct((N_COL, CHUNK, F), jnp.bfloat16),
            jax.ShapeDtypeStruct((N_ROW, 1, 128), jnp.int32),
        ),
        in_specs=[hbm, hbm, hbm],
        out_specs=(any_space, any_space, any_space),
        scratch_shapes=[
            pltpu.VMEM((1, E_DEV), jnp.int32),
            pltpu.VMEM((1, 128), jnp.int32),
            pltpu.VMEM((N_ROW - 1, 1, 128), jnp.int32),
            pltpu.SemaphoreType.DMA((GATHER_COPIES,)),
            pltpu.SemaphoreType.DMA((GATHER_COPIES,)),
            pltpu.SemaphoreType.DMA((4,)),
        ],
        compiler_params=pltpu.CompilerParams(
            collective_id=0, has_side_effects=True, vmem_limit_bytes=4 * MIB
        ),
    )(*in_hbm(values, features, columns))


def place_kernel(cols_in, len_in, own_in, blocks, dense, cols, lengths, owners, first, sums, sems):
    row = lax.axis_index("row")
    small = [
        pltpu.make_async_copy(len_in, lengths, sems.at[0]),
        pltpu.make_async_copy(own_in, owners, sems.at[1]),
        pltpu.make_async_copy(cols_in, cols, sems.at[2]),
    ]
    for copy in small:
        copy.start()
    dense[...] = jnp.zeros_like(dense)
    for copy in small:
        copy.wait()

    def find(q, state):
        begin, starts, sizes = state
        length = lengths[0, q]
        which = owners[0, q] - row * SLOTS
        starts = tuple(jnp.where(which == s, begin, v) for s, v in enumerate(starts))
        sizes = tuple(jnp.where(which == s, length, v) for s, v in enumerate(sizes))
        return begin + length, starts, sizes

    nought = jnp.int32(0)
    _, starts, sizes = lax.fori_loop(0, ROWS, find, (nought, (nought,) * SLOTS, (nought,) * SLOTS))
    for s in range(SLOTS):

        @pl.loop(0, FEAT_NODES // BLOCK)
        def _(j):
            first[s, j] = -1

        @pl.loop(0, sizes[s])
        def _(k):
            g = starts[s] + k
            j = cols[g // E_DEV, 0, lax.rem(g, E_DEV)]
            spot = (pl.ds(s * BLOCK, BLOCK), pl.ds(pl.multiple_of(j * BLOCK, BLOCK), BLOCK))
            seen = first[s, j]

            @pl.when(seen < 0)
            def _():
                first[s, j] = k
                sums[k] = f32(blocks[g])
                dense[spot] = blocks[g]

            @pl.when(seen >= 0)
            def _():
                total = sums[seen] + f32(blocks[g])
                sums[seen] = total
                dense[spot] = bf16(total)


def place_blocks(cols, lengths, owners, blocks):
    any_space = pl.BlockSpec(memory_space=pl.ANY)
    vmem = pl.BlockSpec(memory_space=pltpu.VMEM)
    hbm = pl.BlockSpec(memory_space=pltpu.HBM)
    return pl.pallas_call(
        place_kernel,
        name="place",
        out_shape=jax.ShapeDtypeStruct((SLAB_DEV, FEAT_NODES), jnp.bfloat16),
        in_specs=[any_space, hbm, hbm, vmem],
        out_specs=vmem,
        scratch_shapes=[
            pltpu.SMEM((N_ROW, 1, 128), jnp.int32),
            pltpu.SMEM((1, ROWS), jnp.int32),
            pltpu.SMEM((1, ROWS), jnp.int32),
            pltpu.SMEM((SLOTS, FEAT_NODES // BLOCK), jnp.int32),
            pltpu.VMEM((MAX_LEN, BLOCK, BLOCK), jnp.float32),
            pltpu.SemaphoreType.DMA((3,)),
        ],
        compiler_params=pltpu.CompilerParams(vmem_limit_bytes=24 * MIB),
    )(cols, *in_hbm(lengths, owners), blocks)


REDUCE_COPIES = 40
A_SCALE = math.sqrt(2.0 / math.pi)
CUBE = 0.044715


def f32(value):
    return value.astype(jnp.float32)


def bf16(value):
    return value.astype(jnp.bfloat16)


def added(terms):
    total = f32(terms[0])
    for term in terms[1:]:
        total = total + f32(term)
    return total


OVER_ROWS = (((0,), (0,)), ((), ()))
HALF_CHUNK = CHUNK // 2
ORDER = ((2, 1), (2, 0), (1, 1), (3, 1), (0, 1), (1, 0), (3, 0), (0, 0))


def layer(dense, feats, weight, cot, out, acc, hid, gpre, ghid, get_weight, get_cot):
    wide = FEAT_NODES // 4
    acc[...] = jnp.zeros_like(acc)

    @pl.loop(0, 4)
    def _(i):
        part = pl.ds(pl.multiple_of(i * wide, wide), wide)
        acc[...] += jnp.dot(dense[:, part], feats[part], preferred_element_type=jnp.float32)

    hid[...] = acc[...].astype(jnp.bfloat16)
    get_weight.wait()
    acc[...] = jnp.dot(hid[...], weight[...], preferred_element_type=jnp.float32)
    get_cot.wait()

    @pl.loop(0, SLAB_DEV // 32)
    def _(i):
        part = pl.ds(pl.multiple_of(i * 32, 32), 32)
        v = acc[part]
        square = v * v
        t = jnp.tanh(A_SCALE * (v + CUBE * (v * square)))
        cdf = 0.5 * (1.0 + t)
        out[part] = (v * cdf).astype(jnp.bfloat16)
        slope = cdf + 0.5 * v * (1.0 - t * t) * (A_SCALE * (1.0 + 3.0 * CUBE * square))
        gpre[part] = (cot[part].astype(jnp.float32) * slope).astype(jnp.bfloat16)

    ghid[...] = lax.dot_general(
        weight[...], gpre[...], (((1,), (1,)), ((), ())), preferred_element_type=jnp.float32
    ).astype(jnp.bfloat16)


def reduce_kernel(
    dense, feats, w_in, cot_in, out, gw_out, gf_out,
    weight, cot, acc, hid, gpre, ghid, local,
    p0, r0, sx, rx, x_relay, px, qx, sy, ry, y_relay, py, qy, whole, pieces, final,
    w_p0, w_r0, w_s, w_rx, w_t, w_ry, w_z, w_all, w_other, send, recv,
):
    col, row, x, yl, core, z, yh = place()
    y = yh * NYL + yl
    twin = (col_of(x, yl, 1 - core), row)

    def at_y(dx, dy):
        there = lax.rem(y + dy, NY)
        return (col_of(x + dx, lax.rem(there, NYL), core), row_of(z, there // NYL))

    x_peers = [at_y(dx, 0) for dx in range(1, NX)]
    y_peers = [at_y(0, dy) for dy in range(1, NY)]
    z_peers = [(col, row_of(z + dz, yh)) for dz in range(1, NZ)]
    plane_peers = [at_y(dx, dy) for dx in (2, 1, 3, 0) for dy in (2, 1, 3, 0) if dx or dy]
    far_first = (4, 3, 5, 2, 6, 1, 7)
    row_peers = [(col, row_of(z + dz, h)) for dz in far_first for h in (1 - yh, yh)]
    row_peers.append((col, row_of(z, 1 - yh)))
    far_rows = [(col, row_of(z + dz, 1 - yh)) for dz in range(1, NZ)]
    go = Copies(send, recv)

    def lanes(i):
        return pl.ds(pl.multiple_of(i * CHUNK, CHUNK), CHUNK)

    def weight_term(c):
        return lax.dot_general(
            hid[:, lanes(c)], gpre[...], OVER_ROWS, preferred_element_type=jnp.float32
        )

    def side(own):
        return yl if own else 1 - yl

    def feature_term(o, c):
        dx, own = ORDER[o]
        nodes = lanes(col_of(x + dx, side(own), c))
        return jnp.dot(ghid[...], dense[:, nodes], preferred_element_type=jnp.float32)

    get_weight = pltpu.make_async_copy(w_in, weight, local.at[0])
    get_cot = pltpu.make_async_copy(cot_in, cot, local.at[1])
    get_weight.start()
    get_cot.start()

    def first():
        layer(dense, feats, weight, cot, out, acc, hid, gpre, ghid, get_weight, get_cot)
        for o in range(8):
            p0[o] = bf16(feature_term(o, 1 - core))
        w_p0[...] = bf16(weight_term(1 - core))

    greet(plane_peers + z_peers + far_rows + [twin], first)

    twins = [go.start(p0.at[o], r0.at[o], twin) for o in range(2)]
    w_twin = go.start(w_p0, w_r0, twin)
    twins += [go.start(p0.at[o], r0.at[o], twin) for o in range(2, 8)]

    def to_twin(o):
        p0[o] = bf16(feature_term(o, 1 - core))
        twins.append(go.start(p0.at[o], r0.at[o], twin))

    def add_twin(o):
        dx, own = ORDER[o]
        term = feature_term(o, core)
        twins[o].wait_recv()
        term = term + f32(r0[o])
        sx[dx, side(own)] = bf16(term[:WIDE])
        if dx == 2:
            far_x[own] = go.start(sx.at[2, side(own)], x_relay.at[own], x_peers[0 if own else 2])
        elif (dx, own) in ((3, 1), (1, 0)):
            near_x(dx, own)
        there = lax.rem(x + dx, NX)
        part = bf16(term[WIDE:])
        for h in range(NYH):
            half = lax.rem(yh + h, NYH)
            dy = lax.rem(half * NYL + side(own) - y + NY, NY)
            sy[dy, there] = jnp.where(half == 0, part[:, :HALF_CHUNK], part[:, HALF_CHUNK:])
        way = 1 if dx in (1, 2) else 3
        if own:
            far_y[dx] = go.start(sy.at[2, there], y_relay.at[dx], y_peers[way - 1])
        else:
            near_y(4 - way, dx)

    def near_x(dx, own):
        part = rx.at[dx // 2, side(own)]
        by_x.append(go.start(sx.at[dx, side(own)], part, x_peers[dx - 1]))

    def near_y(dy, dx):
        there = lax.rem(x + dx, NX)
        by_y[dy].start(sy.at[dy, there], ry.at[dy // 2, there], y_peers[dy - 1])

    def relay_x(dx, own):
        far_x[own].wait_recv()
        sx[dx, side(own)] = bf16(added([sx[dx, side(own)], x_relay[own]]))
        near_x(dx, own)

    def relay_y(dx):
        dy = 1 if dx in (1, 2) else 3
        there = lax.rem(x + dx, NX)
        far_y[dx].wait_recv()
        sy[dy, there] = bf16(added([sy[dy, there], y_relay[dx]]))
        near_y(dy, dx)

    by_x, far_x, far_y = [], {}, {}
    by_y = {dy: go.group(ry.at[0]) for dy in (1, 3)}
    for o in range(4):
        add_twin(o)
    term = weight_term(core)
    w_twin.wait_recv()
    w_s[...] = bf16(term + f32(w_r0[...]))

    def quarter(i):
        return pl.ds(pl.multiple_of(i * (CHUNK // NX), CHUNK // NX), CHUNK // NX)

    def piece(i):
        return pl.ds(pl.multiple_of(i * PIECE, PIECE), PIECE)

    w_x = go.start_all(
        [
            (w_s.at[quarter(lax.rem(x + dx, NX))], w_rx.at[dx - 1], x_peers[dx - 1])
            for dx in range(1, NX)
        ],
        w_rx,
    )
    add_twin(4)
    add_twin(5)
    add_twin(6)
    add_twin(7)
    relay_x(1, 1)
    relay_x(3, 0)
    for dx in (2, 1, 3, 0):
        relay_y(dx)

    def units(i):
        return pl.ds(pl.multiple_of(i * (F // NZ), F // NZ), F // NZ)

    w_x.wait_recv()
    w_t[...] = added([w_s[quarter(x)]] + [w_rx[i] for i in range(NX - 1)])
    w_y = go.start_all(
        [
            (w_t.at[piece(lax.rem(y + dy, NY))], w_ry.at[dy - 1], y_peers[dy - 1])
            for dy in range(1, NY)
        ],
        w_ry,
    )
    for copy in by_x:
        copy.wait_recv()
    for i in range(NYL):
        for h in range(NYH):
            dy = lax.rem(h * NYL + i - y + NY, NY)
            part = (slice(None), slice(h * HALF_CHUNK, (h + 1) * HALF_CHUNK))
            px[dy] = bf16(added([sx[(0, i) + part]] + [rx[(j, i) + part] for j in range(2)]))
    x_then_y = go.start_all(
        [(px.at[dy], qx.at[dy - 1], y_peers[dy - 1]) for dy in (2, 1, 3)], qx
    )
    for copy in by_y.values():
        copy.wait_recv()
    for i in range(NX):
        dx = lax.rem(i - x + NX, NX)
        py[dx] = bf16(added([sy[0, i]] + [ry[j, i] for j in range(2)]))
    y_then_x = go.start_all(
        [(py.at[dx], qy.at[dx - 1], x_peers[dx - 1]) for dx in (2, 1, 3)], qy
    )
    w_y.wait_recv()
    w_z[z] = bf16(added([w_t[piece(y)]] + [w_ry[i] for i in range(NY - 1)]))
    w_rows = go.start_all([(w_z.at[z], w_z.at[z], z_peers[dz - 1]) for dz in far_first], w_z.at[pl.ds(0, NZ - 1)])

    x_then_y.wait_recv()
    whole[:WIDE] = bf16(added([px[0]] + [qx[i] for i in range(NY - 1)]))
    y_then_x.wait_recv()
    whole[WIDE:] = bf16(added([py[0]] + [qy[i] for i in range(NX - 1)]))
    rows = go.start_all(
        [
            (whole.at[units(lax.rem(z + dz, NZ))], pieces.at[dz - 1], z_peers[dz - 1])
            for dz in far_first
        ],
        pieces,
    )
    w_rows.wait_recv()
    scale = 1.0 / math.sqrt(N_COL * N_ROW * SLOTS * BLOCK)
    w_all[x * NY + y] = bf16(added([w_z[i] for i in range(NZ)]) * scale)
    part = w_all.at[x * NY + y]
    early = len(go.all)
    w_plane = go.start_all([(part, part, peer) for peer in plane_peers], w_all.at[pl.ds(0, NX * NY - 1)])
    rows.wait_recv()
    final[yh * NZ + z] = bf16(added([whole[units(z)]] + [pieces[i] for i in range(NZ - 1)]))
    part = final.at[yh * NZ + z]
    everyone = go.start_all([(part, part, peer) for peer in row_peers], final.at[pl.ds(0, N_ROW - 1)])
    go.finish(early)
    w_plane.wait_recv()
    w_back = go.start(w_all, w_other, twin)
    gw_out[lanes(core)] = w_all[...].reshape(CHUNK, F)
    w_back.wait_recv()
    gw_out[lanes(1 - core)] = w_other[...].reshape(CHUNK, F)
    everyone.wait_recv()
    gf_out[...] = final[...].reshape(NYH, F, HALF_CHUNK)
    go.finish()


def reduce(dense, feats, weight, cotangent):
    vmem = pl.BlockSpec(memory_space=pltpu.VMEM)
    hbm = pl.BlockSpec(memory_space=pltpu.HBM)
    rows = (SLAB_DEV, F)

    def buffer(*shape):
        return pltpu.VMEM(shape, jnp.bfloat16)

    def lane(rows, *lead):
        return buffer(*lead, rows, HALF_CHUNK)

    quarter = CHUNK // NX
    return pl.pallas_call(
        reduce_kernel,
        name="reduce",
        out_shape=(
            jax.ShapeDtypeStruct(rows, jnp.bfloat16),
            jax.ShapeDtypeStruct((F, F), jnp.bfloat16),
            jax.ShapeDtypeStruct((NYH, F, HALF_CHUNK), jnp.bfloat16),
        ),
        in_specs=[vmem, vmem, hbm, hbm],
        out_specs=(vmem, vmem, vmem),
        scratch_shapes=[
            buffer(F, F), buffer(*rows), pltpu.VMEM(rows, jnp.float32),
            buffer(*rows), buffer(*rows), buffer(F, SLAB_DEV), pltpu.SemaphoreType.DMA((2,)),
            buffer(8, F, CHUNK), buffer(8, F, CHUNK),
            buffer(NX, NYL, WIDE, CHUNK), buffer(2, NYL, WIDE, CHUNK), buffer(2, WIDE, CHUNK),
            lane(WIDE, NY), lane(WIDE, NY - 1),
            lane(F - WIDE, NY, NX), lane(F - WIDE, 2, NX), lane(F - WIDE, NX),
            lane(F - WIDE, NX), lane(F - WIDE, NX - 1),
            buffer(F, HALF_CHUNK), buffer(NZ - 1, F // NZ, HALF_CHUNK), buffer(N_ROW, F // NZ, HALF_CHUNK),
            buffer(CHUNK, F), buffer(CHUNK, F), buffer(CHUNK, F), buffer(NX - 1, quarter, F),
            pltpu.VMEM((quarter, F), jnp.float32), pltpu.VMEM((NY - 1, PIECE, F), jnp.float32),
            buffer(NZ, PIECE, F), buffer(NX * NY, PIECE, F), buffer(NX * NY, PIECE, F),
            pltpu.SemaphoreType.DMA((REDUCE_COPIES,)),
            pltpu.SemaphoreType.DMA((REDUCE_COPIES,)),
        ],
        compiler_params=pltpu.CompilerParams(
            collective_id=1, has_side_effects=True, vmem_limit_bytes=32 * MIB
        ),
    )(dense, feats, *in_hbm(weight, cotangent))


def finish_kernel(out_in, gw_in, gf_in, out, gw_out, gf_out, gw, gf, sems):
    copies = [pltpu.make_async_copy(out_in, out, sems.at[0])]
    copies[0].start()
    for i in range(2):
        part = pl.ds(i * CHUNK, CHUNK)
        gw[part] = f32(gw_in[part])
        copies.append(pltpu.make_async_copy(gw.at[part], gw_out.at[part], sems.at[1 + i]))
        copies[-1].start()
    for h in range(NYH):
        gf[h * HALF_CHUNK : (h + 1) * HALF_CHUNK] = f32(gf_in[h]).T
    copies.append(pltpu.make_async_copy(gf, gf_out, sems.at[3]))
    copies[-1].start()
    for copy in copies:
        copy.wait()


def finish(output, gw, gf):
    vmem = pl.BlockSpec(memory_space=pltpu.VMEM)
    hbm = pl.BlockSpec(memory_space=pltpu.HBM)
    return pl.pallas_call(
        finish_kernel,
        name="finish",
        out_shape=(
            jax.ShapeDtypeStruct(output.shape, jnp.bfloat16),
            jax.ShapeDtypeStruct(gw.shape, jnp.float32),
            jax.ShapeDtypeStruct((CHUNK, F), jnp.float32),
        ),
        in_specs=[vmem] * 3,
        out_specs=(hbm,) * 3,
        scratch_shapes=[
            pltpu.VMEM(gw.shape, jnp.float32),
            pltpu.VMEM((CHUNK, F), jnp.float32),
            pltpu.SemaphoreType.DMA((4,)),
        ],
        compiler_params=pltpu.CompilerParams(vmem_limit_bytes=8 * MIB),
    )(output, gw, gf)


def body(features, block_values, entry_cols, row_lengths, row_owner, weight, cotangent):
    values = block_values.reshape(E_DEV * BLOCK, BLOCK)
    blocks, feats, cols = gather(values, features, entry_cols.reshape(1, E_DEV))
    blocks = blocks.reshape(N_ROW * E_DEV, BLOCK, BLOCK)
    dense = place_blocks(cols, row_lengths, row_owner, blocks)
    return finish(*reduce(dense, feats.reshape(FEAT_NODES, F), weight, cotangent))


def solution(mesh):
    placed = (
        P("col", None),
        P("col", "row", None, None, None),
        P("col", "row", None),
        P("col", None),
        P("col", None),
        P(),
        P(("col", "row"), None),
    )
    return jax.shard_map(
        body,
        mesh=mesh,
        in_specs=placed,
        out_specs=(P(("col", "row"), None), P(), P("col", None)),
        check_vma=False,
    )
```
